32 devices in a mesh: fsdp: 8 (over y, x, core), dp: 4 (over z).
Axes of the slice: x: 2, y: 2, z: 4, core: 2. Of those that a mesh axis runs over, the one named last changes fastest.
Arguments:
- hidden_in: bfloat16 [16384, 768], P(('fsdp', 'dp')), may hold values from -6 to 6
- norm_gain_attn: bfloat16 [768], P('fsdp'), may hold values from 0.5 to 1.5
- w_query: bfloat16 [768, 768], P('fsdp'), may hold values from -0.02734375 to 0.02734375
- w_key: bfloat16 [768, 768], P('fsdp'), may hold values from -0.21875 to 0.21875
- w_value: bfloat16 [768, 768], P('fsdp'), may hold values from -0.21875 to 0.21875
- w_out: bfloat16 [768, 768], P('fsdp'), may hold values from -1.75 to 1.75
- rel_bias: bfloat16 [32, 12], P('fsdp'), may hold values from -6 to 6
- norm_gain_ffn: bfloat16 [768], P('fsdp'), may hold values from 0.5 to 1.5
- w_in: bfloat16 [768, 3072], P('fsdp'), may hold values from -0.21875 to 0.21875
- w_ffout: bfloat16 [3072, 768], P('fsdp'), may hold values from -0.109375 to 0.109375
- bucket_index: int32 [1023], replicated, may hold values from 0 to 31
- row_lengths: int32 [32], P(('fsdp', 'dp')), may hold values from 80 to 512, as said below
- prefix_lengths: int32 [32], P(('fsdp', 'dp')), may hold values from 5 to 40
- out_cotangent: bfloat16 [16384, 768], P(('fsdp', 'dp')), may hold values from -12 to 12
- pool_cotangent: float32 [32, 768], P(('fsdp', 'dp')), may hold values from -768 to 768
Outputs:
- hidden_out: bfloat16 [16384, 768], P(('fsdp', 'dp'))
- pooled: float32 [32, 768], P(('fsdp', 'dp'))
- grad_hidden: float32 [16384, 768], P(('fsdp', 'dp'))
- grad_gain_attn: float32 [768], P('fsdp')
- grad_query: float32 [768, 768], P('fsdp')
- grad_key: float32 [768, 768], P('fsdp')
- grad_value: float32 [768, 768], P('fsdp')
- grad_out: float32 [768, 768], P('fsdp')
- grad_rel: float32 [32, 12], P('fsdp')
- grad_gain_ffn: float32 [768], P('fsdp')
- grad_in: float32 [768, 3072], P('fsdp')
- grad_ffout: float32 [3072, 768], P('fsdp')
- token_root_mean_square: float32 [32, 3], P(('fsdp', 'dp'))
The draws below stay inside these ranges and needn't reach their ends.
Inputs may be any that keep to these rules, and one draw needn't show every extreme that they name: `row_lengths`: some sequence has exactly 512 live tokens.
All inputs are finite; a program needn't handle non-finite values.
Results may differ from the reference program's by a relative error of at most 0.019.
Values may be sent and summed in bfloat16 or wider, within the bound.
No kernel may reach another device: no remote copies, remote signals or barrier semaphores. Data moves between devices by JAX's collectives and lax.ppermute only.
A program may use at most 128 MiB of HBM per device.

```python
import jax
import jax.numpy as jnp
from jax import lax

D = 768
H = 12
DH = 64
FF = 3072
BUCKETS = 32
SEQ_LEN = 512
PREFIX_MIN = 5
PREFIX_MAX = 40
ROWS = 32
TOKENS = 16384


def draw_row_lengths(key, part):
    key = jax.random.fold_in(key, 11)
    first_key, second_key = jax.random.split(key)
    lengths = jax.random.randint(first_key, (ROWS,), 2 * PREFIX_MAX, SEQ_LEN + 1)
    picked = jax.random.randint(second_key, (), 0, ROWS)
    places = jnp.arange(ROWS, dtype=jnp.int32)
    return jnp.where(places == picked, SEQ_LEN, lengths).astype(jnp.int32)


def set_ends(values, rng, least, high):
    longest = values.shape.index(max(values.shape))
    spots = []
    for shift in (0, 1):
        where = [jax.random.randint(jax.random.fold_in(rng, axis), (), 0, length) for axis, length in enumerate(values.shape)]
        where[longest] = (where[longest] + shift) % values.shape[longest]
        spots.append(tuple(where))
    return values.at[spots[0]].set(least).at[spots[1]].set(high)


def strengthened(values, stream_key, source, target, blocks, factor):
    def block_of(dim):
        return (jnp.arange(values.shape[dim]) // (values.shape[dim] // blocks)).reshape((-1,) + (1,) * (values.ndim - 1 - dim))

    one_side = jax.random.permutation(stream_key, blocks)[block_of(target)]
    other_side = (block_of(target) + blocks // 2) % blocks
    return jnp.where((block_of(source) == one_side) | (block_of(source) == other_side), factor * values, values)


def levels(own_key, shape, cuts, smallest, top_value):
    gain, own = 1.0, jax.random.fold_in(own_key, 6)
    for position, blocks in cuts:
        draws = jnp.exp(jax.random.uniform(jax.random.fold_in(own, position), (blocks,), jnp.float32, smallest / len(cuts), top_value / len(cuts)))
        gain = gain * jnp.repeat(draws, shape[position] // blocks).reshape([-1 if axis == position else 1 for axis in range(len(shape))])
    return gain


def scatter_about(own_key, extent, deviation, reach, shards=(), kind=jnp.bfloat16):
    result = jax.random.normal(own_key, extent, jnp.float32) * deviation
    if len(shards) > 0:
        result = levels(own_key, extent, shards, -0.22, 0.18) * result
    return jnp.clip(result, min=-reach, max=reach).astype(kind)


def gaussian_with(own_key, dims, width, reach, shards, heavy, kind=jnp.bfloat16):
    values = width * jax.random.normal(own_key, dims, jnp.float32)
    if shards:
        values = values * levels(own_key, dims, shards, -0.22, 0.18)
    return jnp.clip(strengthened(values, jax.random.fold_in(own_key, 3), *heavy), -reach, reach).astype(kind)


def setup_inputs(seed: int = 0) -> dict:
    seeds = jax.random.split(jax.random.key(seed), 16)
    return {
        "hidden_in": scatter_about(seeds[0], (TOKENS, D), 1.0, 6.0, ((0, 32),)),
        "norm_gain_attn": jnp.clip(1.0 + 0.1 * jax.random.normal(seeds[1], (D,), jnp.float32), 0.5, 1.5).astype(jnp.bfloat16),
        "w_query": scatter_about(seeds[2], (D, H * DH), (D * DH) ** -0.5, 0.02734375, ((0, 8),)),
        "w_key": scatter_about(seeds[3], (D, H * DH), D ** -0.5, 0.21875, ((0, 8),)),
        "w_value": scatter_about(seeds[4], (D, H * DH), D ** -0.5, 0.21875, ((0, 8),)),
        "w_out": scatter_about(seeds[5], (H * DH, D), (H * DH // 64) ** -0.5, 1.75, ((0, 8),)),
        "rel_bias": scatter_about(seeds[6], (BUCKETS, H), 1.0, 6.0, ((0, 8),)),
        "norm_gain_ffn": jnp.clip(1.0 + 0.1 * jax.random.normal(seeds[7], (D,), jnp.float32), 0.5, 1.5).astype(jnp.bfloat16),
        "w_in": scatter_about(seeds[8], (D, FF), D ** -0.5, 0.21875, ((0, 8),)),
        "w_ffout": scatter_about(seeds[9], (FF, D), FF ** -0.5, 0.109375, ((0, 8),)),
        "bucket_index": set_ends(jax.random.randint(seeds[10], (2 * SEQ_LEN - 1,), 0, BUCKETS), jax.random.fold_in(seeds[10], 1), 0, BUCKETS - 1).astype(jnp.int32),
        "row_lengths": draw_row_lengths(jax.random.fold_in(seeds[15], 71), 0),
        "prefix_lengths": set_ends(jax.random.randint(seeds[12], (ROWS,), PREFIX_MIN, PREFIX_MAX + 1), jax.random.fold_in(seeds[12], 1), PREFIX_MIN, PREFIX_MAX).astype(jnp.int32),
        "out_cotangent": gaussian_with(seeds[13], (TOKENS, D), 1.0, 12.0, ((0, 32),), (0, 1, 32, 2.75)),
        "pool_cotangent": scatter_about(seeds[14], (ROWS, D), (SEQ_LEN // 4), 768.0, ((0, 32),), jnp.float32),
    }


@jax.custom_vjp
def low(v):
    return lax.optimization_barrier(v.astype(jnp.bfloat16)).astype(jnp.float32)

@jax.custom_vjp
def low_back(v):
    return v

def low_keep(v):
    return (low(v), None)

def low_pass(kept, grad):
    return (grad,)

def back_keep(v):
    return (v, None)

def back_low(kept, grad):
    return (low(grad),)
low.defvjp(low_keep, low_pass)
low_back.defvjp(back_keep, back_low)
epsilon = 1e-06
masked_score = -1e+30
highest = lax.Precision.HIGHEST

def rms_norm(values, gain_vec):
    inv_rms = lax.rsqrt(lax.optimization_barrier(jnp.mean(values * values, axis=-1, keepdims=True)) + epsilon)
    return values * inv_rms * gain_vec

def both_ways(values):
    return low(low_back(values))

def project(tensor, weight):
    return jnp.einsum('gld,de->gle', tensor, weight, precision=highest)

def group_layer(weights, bucket_index, group_in, lengths, prefixes):
    gain_attn, w_query, w_key, w_value, w_out, rel_bias, gain_ffn, w_in, w_ffout = weights
    sequence_count, sequence_length, embedding_width = group_in.shape
    head_count = rel_bias.shape[1]
    head_dim = w_query.shape[1] // head_count
    rows_at = lax.broadcasted_iota(jnp.int32, (sequence_length, sequence_length), 0)
    cols_at = lax.broadcasted_iota(jnp.int32, (sequence_length, sequence_length), 1)
    chosen = jnp.take(bucket_index, (cols_at - rows_at + sequence_length - 1).astype(jnp.int32))
    pos_bias = jnp.transpose(jnp.take(rel_bias, chosen, axis=0), (2, 0, 1))
    normed_attn = low(rms_norm(group_in, gain_attn))
    queries = both_ways(project(normed_attn, w_query)).reshape(sequence_count, sequence_length, head_count, head_dim)
    key_rows = both_ways(project(normed_attn, w_key)).reshape(sequence_count, sequence_length, head_count, head_dim)
    value_rows = both_ways(project(normed_attn, w_value)).reshape(sequence_count, sequence_length, head_count, head_dim)
    scores = jnp.einsum('gihd,gjhd->ghij', queries, key_rows, precision=highest) + pos_bias[None]
    scores = low_back(scores)
    allowed = lax.broadcasted_iota(jnp.int32, scores.shape, 3) < lengths[:, None, None, None]
    scores = jnp.where(allowed, scores, masked_score)
    attn_probs = jax.nn.softmax(scores, axis=-1)
    attended = jnp.einsum('ghij,gjhd->gihd', low(attn_probs), value_rows, precision=highest)
    attended = both_ways(attended.reshape(sequence_count, sequence_length, head_count * head_dim))
    branch_attn = low_back(project(attended, w_out))
    residual = group_in + branch_attn
    normed_ffn = low(rms_norm(residual, gain_ffn))
    pre_act = low_back(project(normed_ffn, w_in))
    activated = low(jax.nn.gelu(pre_act))
    branch_ffn = low_back(project(activated, w_ffout))
    layer_output = residual + branch_ffn
    positions = lax.broadcasted_iota(jnp.int32, (sequence_count, sequence_length), 1)
    pool_mask = ((positions >= prefixes[:, None]) & (positions < lengths[:, None])).astype(jnp.float32)
    pooled = lax.optimization_barrier(jnp.sum(pool_mask[:, :, None] * layer_output, axis=1)) / lax.optimization_barrier(jnp.sum(pool_mask, axis=1))[:, None]
    valid_mask = (positions < lengths[:, None]).astype(jnp.float32)

    def row_measure(tensor):
        return jnp.sqrt(lax.optimization_barrier(jnp.sum(valid_mask[:, :, None] * tensor * tensor, axis=(1, 2))) / (lengths.astype(jnp.float32) * embedding_width))
    row_stats = jnp.stack([row_measure(group_in), row_measure(branch_attn), row_measure(branch_ffn)], axis=-1)
    return (layer_output, pooled, row_stats)

def reference(hidden_in, norm_gain_attn, w_query, w_key, w_value, w_out, rel_bias, norm_gain_ffn, w_in, w_ffout, bucket_index, row_lengths, prefix_lengths, out_cotangent, pool_cotangent):
    group_size = 8
    group_total = ROWS // group_size
    weights = tuple((tensor.astype(jnp.float32) for tensor in (norm_gain_attn, w_query, w_key, w_value, w_out, rel_bias, norm_gain_ffn, w_in, w_ffout)))
    inputs = hidden_in.astype(jnp.float32).reshape(group_total, group_size, SEQ_LEN, D)
    len_groups = row_lengths.reshape(group_total, group_size)
    pre_groups = prefix_lengths.reshape(group_total, group_size)

    def forward(weight_set, input_set):

        def one_group(group_items):
            return group_layer(weight_set, bucket_index, group_items[0], group_items[1], group_items[2])
        layer_output, pooled, row_stats = lax.map(jax.checkpoint(one_group), (input_set, len_groups, pre_groups))
        return ((layer_output, pooled), row_stats)
    primal, pullback, row_stats = jax.vjp(forward, weights, inputs, has_aux=True)
    layer_output, pooled = primal
    cotangents = (out_cotangent.astype(jnp.float32).reshape(group_total, group_size, SEQ_LEN, D), pool_cotangent.reshape(group_total, group_size, D))
    grad_weights, grad_inputs = pullback(cotangents)
    return (layer_output.reshape(TOKENS, D).astype(jnp.bfloat16), pooled.reshape(ROWS, D), grad_inputs.reshape(TOKENS, D), grad_weights[0], grad_weights[1], grad_weights[2], grad_weights[3], grad_weights[4], grad_weights[5], grad_weights[6], grad_weights[7], grad_weights[8], row_stats.reshape(ROWS, 3))
```

```python
import functools

import jax
import jax.numpy as jnp
from jax import lax
from jax.experimental import pallas as pl
from jax.experimental.pallas import tpu as pltpu
from jax.sharding import PartitionSpec as P

EPS = 1e-06
F32 = jnp.float32
BF16 = jnp.bfloat16
VMEM_LIMIT = 44 * 2**20
GELU_A = 0.7978845608028654
GELU_B = 0.044715


def dot(a, b):
    return lax.dot_general(a, b, (((1,), (0,)), ((), ())), preferred_element_type=F32)


def dot_right(a, b):
    return lax.dot_general(a, b, (((1,), (1,)), ((), ())), preferred_element_type=F32)


def dot_left(a, b):
    return lax.dot_general(a, b, (((0,), (0,)), ((), ())), preferred_element_type=F32)


def iota(shape, dim):
    return lax.broadcasted_iota(jnp.int32, shape, dim)


def call(kernel, name, ins, outs, scratch=(), flops=0, nbytes=0, trans=0):
    spaces = {"v": pltpu.VMEM, "s": pltpu.SMEM, "h": pl.ANY}
    return pl.pallas_call(
        kernel,
        name=name,
        out_shape=[jax.ShapeDtypeStruct(s, d) for s, d, _ in outs],
        in_specs=[pl.BlockSpec(memory_space=spaces[m]) for _, m in ins],
        out_specs=[pl.BlockSpec(memory_space=spaces[m]) for _, _, m in outs],
        scratch_shapes=list(scratch),
        compiler_params=pltpu.CompilerParams(vmem_limit_bytes=VMEM_LIMIT),
        cost_estimate=pl.CostEstimate(flops=flops, bytes_accessed=nbytes, transcendentals=trans),
    )(*[a for a, _ in ins])


def place(meta, pieces, targets, copies, sems):
    handles = []
    for number, (src, row, rows, dst, base, column, unit, far, level) in enumerate(copies):
        start = base
        if unit:
            start = pl.multiple_of(base + unit * jnp.bitwise_xor(meta[level], far), 16)
        width = pieces[src].shape[1]
        handle = pltpu.make_async_copy(
            pieces[src].at[pl.ds(row, rows), :],
            targets[dst].at[pl.ds(start, rows), pl.ds(column, width)],
            sems.at[number],
        )
        handle.start()
        handles.append(handle)
    return handles


def wait_all(handles):
    for handle in handles:
        handle.wait()


def rows_loop(count, step, fn):
    def one(i, carry):
        fn(pl.ds(pl.multiple_of(i * step, step), step))
        return carry

    lax.fori_loop(0, count // step, one, 0)


def prepare_kernel(
    meta, hidden, gain, table, buckets, out_cot, pool_cot, normed, bias, low, table_rows
):
    size = hidden.shape[0]
    length, prefix = meta[4], meta[5]
    count = (length - prefix).astype(F32)

    def rows(ds):
        x = hidden[ds, :].astype(F32)
        inv = lax.rsqrt(jnp.mean(x * x, axis=-1, keepdims=True) + EPS)
        normed[ds, :] = (x * inv * gain[...]).astype(BF16)
        t = iota((128, 1), 0) + ds.start
        pool = jnp.where((t >= prefix) & (t < length), 1.0, 0.0) / count
        low[ds, :] = (out_cot[ds, :].astype(F32) + pool * pool_cot[...]).astype(BF16)

    rows_loop(size, 128, rows)
    span = 2 * size
    hot = (buckets[...] == iota((table.shape[1], span), 0)).astype(BF16)
    table_rows[...] = dot(table[...], hot)
    width = bias.shape[2]

    def head(h, carry):
        row = table_rows[pl.ds(h, 1), :]
        first = jnp.broadcast_to(pltpu.roll(row, span - 127, 1), (8, span))
        sub = iota((8, span), 0)
        block = first
        for k in range(1, 8):
            block = jnp.where(sub == k, pltpu.roll(first, k, 1), block)
        bias[h, 0:8, :] = block[:, :width]
        full = block
        have = 8
        while have < 128:
            more = pltpu.roll(full, have, 1)
            bias[h, have : 2 * have, :] = more[:, :width]
            full = jnp.concatenate([full, more], axis=0)
            have *= 2
        return carry

    lax.fori_loop(0, bias.shape[0], head, 0)


def attend_kernel(copies, n_pieces, *refs):
    meta, normed, bias = refs[:3]
    pieces = refs[3 : 3 + n_pieces]
    q, k, v, attended, powers, inv_sums, wq, wk, wv, scores, sems = refs[3 + n_pieces :]
    handles = place(meta, pieces, (wq, wk, wv), copies, sems)
    wait_all(handles)
    size = normed.shape[0]
    length = meta[4]

    def project(ds):
        x = normed[ds, :]
        q[ds, :] = dot(x, wq[...]).astype(BF16)
        k[ds, :] = dot(x, wk[...]).astype(BF16)
        v[ds, :] = dot(x, wv[...]).astype(BF16)

    rows_loop(size, 256, project)
    lane = iota((1, 128), 1)
    half = lane < 64
    masked = jnp.where(iota((size, 1), 0) < length, 0.0, -1e30).astype(F32)
    strips = size // 128
    inv_sums[...] = jnp.zeros_like(inv_sums)

    def pair(p, carry):
        cols = pl.ds(pl.multiple_of(p * 128, 128), 128)
        qp, kp, vp = q[:, cols].astype(F32), k[:, cols].astype(F32), v[:, cols].astype(F32)
        joined = None
        for side in range(2):
            head = 2 * p + side
            own = half if side == 0 else jnp.logical_not(half)
            spare = lane == (64 if side == 0 else 0)
            qa = jnp.where(own, qp, jnp.where(spare, 1.0, 0.0)).astype(BF16)
            ka = jnp.where(own, kp, jnp.where(spare, masked, 0.0)).astype(BF16)
            va = jnp.where(own, vp, jnp.where(spare, 1.0, 0.0)).astype(BF16)
            top = None
            for a in range(strips):
                rows = slice(128 * a, 128 * a + 128)
                off = 128 * (strips - 1 - a)
                s = dot_right(ka[rows], qa) + bias[head, :, off : off + size]
                scores[rows, :] = s
                peak = jnp.max(s, axis=0, keepdims=True)
                top = peak if top is None else jnp.maximum(top, peak)
            for a in range(strips):
                rows = slice(128 * a, 128 * a + 128)
                powers[head, rows, :] = jnp.exp(scores[rows, :] - top).astype(BF16)
            mixed = dot_left(va, powers[head]).T
            total = jnp.sum(jnp.where(spare, mixed, 0.0), axis=1, keepdims=True)
            inv = 1.0 / total
            inv_sums[...] = jnp.where(lane == head, inv, inv_sums[...])
            mixed = mixed * inv
            joined = mixed if side == 0 else jnp.where(half, joined, mixed)
        attended[:, cols] = joined.astype(BF16)
        return carry

    lax.fori_loop(0, q.shape[1] // 128, pair, 0)


def residual_kernel(copies, n_pieces, *refs):
    meta, hidden, attended, gain = refs[:4]
    pieces = refs[4 : 4 + n_pieces]
    residual, normed, sums, w_out, sems = refs[4 + n_pieces :]
    wait_all(place(meta, pieces, (w_out,), copies, sems))
    size = hidden.shape[0]
    length = meta[4]
    sums[...] = jnp.zeros_like(sums)

    def rows(ds):
        x = hidden[ds, :].astype(F32)
        branch = dot(attended[ds, :], w_out[...])
        live = (iota((256, 1), 0) + ds.start) < length
        sums[0:1, :] += jnp.sum(jnp.where(live, x * x, 0.0), axis=0, keepdims=True)
        sums[1:2, :] += jnp.sum(jnp.where(live, branch * branch, 0.0), axis=0, keepdims=True)
        r = x + branch
        residual[ds, :] = r
        inv = lax.rsqrt(jnp.mean(r * r, axis=-1, keepdims=True) + EPS)
        normed[ds, :] = (r * inv * gain[...]).astype(BF16)

    rows_loop(size, 256, rows)


def scatter_out(meta, scratch, outs, plan, sems):
    handles = []
    for number, (dst, row, rows, unit, far, offset) in enumerate(plan):
        start = offset
        if unit:
            start = pl.multiple_of(offset + unit * jnp.bitwise_xor(meta[1], far), 16)
        handle = pltpu.make_async_copy(
            scratch.at[pl.ds(start, rows), :], outs[dst].at[pl.ds(row, rows), :], sems.at[number]
        )
        handle.start()
        handles.append(handle)
    return handles


def expand_kernel(copies, n_pieces, plan, n_out, *refs):
    meta, x_own, x_peer, low_own, low_peer = refs[:5]
    pieces = refs[5 : 5 + n_pieces]
    activated, slope = refs[5 + n_pieces : 7 + n_pieces]
    outs = refs[7 + n_pieces : 7 + n_pieces + n_out]
    w_in, grads, sems, out_sems = refs[7 + n_pieces + n_out :]
    wait_all(place(meta, pieces, (w_in,), copies, sems))
    size = x_own.shape[0]
    chunk = 512 if w_in.shape[1] % 512 == 0 else 256

    for which, x_ref in enumerate((x_own, x_peer)):

        def rows(ds, which=which, x_ref=x_ref):
            x = x_ref[ds, :]
            for c in range(0, w_in.shape[1], chunk):
                t = dot(x, w_in[:, c : c + chunk])
                square = t * t
                th = jnp.tanh(GELU_A * t * (1.0 + GELU_B * square))
                phi = 0.5 + 0.5 * th
                activated[which, ds, c : c + chunk] = (t * phi).astype(BF16)
                inner = GELU_A + (3.0 * GELU_A * GELU_B) * square
                slope[which, ds, c : c + chunk] = (
                    phi + 0.5 * t * (1.0 - th * th) * inner
                ).astype(BF16)

        rows_loop(size, 256, rows)

    for c in range(0, w_in.shape[1], 256):
        part = dot_left(activated[0, :, c : c + 256], low_own[...])
        part += dot_left(activated[1, :, c : c + 256], low_peer[...])
        grads[c : c + 256, :] = part.astype(BF16)
    wait_all(scatter_out(meta, grads, outs, plan, out_sems))


def contract_kernel(copies, n_pieces, *refs):
    meta, slope, low_own, low_peer = refs[:4]
    pieces = refs[4 : 4 + n_pieces]
    grad_pre, part_own, part_peer, w_in, w_ffout, sems = refs[4 + n_pieces :]
    wait_all(place(meta, pieces, (w_in, w_ffout), copies, sems))
    size = low_own.shape[0]
    chunk = 512 if w_in.shape[1] % 512 == 0 else 256
    for which, (low, part) in ((1, (low_peer, part_peer)), (0, (low_own, part_own))):

        def rows(ds, which=which, low=low, part=part):
            y = low[ds, :]
            total = None
            for c in range(0, w_in.shape[1], chunk):
                g = dot_right(y, w_ffout[c : c + chunk, :])
                g = (slope[which, ds, c : c + chunk].astype(F32) * g).astype(BF16)
                grad_pre[which, ds, c : c + chunk] = g
                t = dot_right(g, w_in[:, c : c + chunk])
                total = t if total is None else total + t
            part[ds, :] = total.astype(part.dtype)

        rows_loop(size, 256, rows)


def outer_kernel(plan, n_out, *refs):
    meta, x_own, x_peer, grad_pre = refs[:4]
    outs = refs[4 : 4 + n_out]
    grads, out_sems = refs[4 + n_out :]
    for c in range(0, grads.shape[0], 256):
        part = dot_left(x_own[:, c : c + 256], grad_pre[0])
        part += dot_left(x_peer[:, c : c + 256], grad_pre[1])
        grads[c : c + 256, :] = part.astype(BF16)
    wait_all(scatter_out(meta, grads, outs, plan, out_sems))


def through_kernel(copies, n_pieces, *refs):
    meta, residual, part, other, out_cot, pool_cot, gain = refs[:7]
    pieces = refs[7 : 7 + n_pieces]
    grad_residual, low_residual, grad_attended, grad_gain, w_out, sems = refs[7 + n_pieces :]
    handles = place(meta, pieces, (w_out,), copies, sems)
    size = residual.shape[0]
    length, prefix = meta[4], meta[5]
    count = (length - prefix).astype(F32)
    grad_gain[...] = jnp.zeros_like(grad_gain)
    wait_all(handles)

    def rows(ds):
        x = residual[ds, :]
        gn = part[ds, :] + other[ds, :].astype(F32)
        inv = lax.rsqrt(jnp.mean(x * x, axis=-1, keepdims=True) + EPS)
        u = gain[...] * gn
        xr = x * inv
        t = iota((128, 1), 0) + ds.start
        pool = jnp.where((t >= prefix) & (t < length), 1.0, 0.0) / count
        go = out_cot[ds, :].astype(F32) + pool * pool_cot[...]
        g = go + inv * (u - xr * jnp.mean(xr * u, axis=-1, keepdims=True))
        grad_gain[...] += jnp.sum(xr * gn, axis=0, keepdims=True)
        grad_residual[ds, :] = g
        lr = g.astype(BF16)
        low_residual[ds, :] = lr
        grad_attended[ds, :] = dot_right(lr, w_out[...]).astype(BF16)

    rows_loop(size, 128, rows)


def attend_back_kernel(*refs):
    meta, q, k, v, powers, grad_att, attended, inv_sums, buckets = refs[:9]
    send, keep, grad_table, grads, slant, diag = refs[9:]
    size, width = q.shape
    pairs = width // 128
    group = pairs // 2
    strips = size // 128
    span = 2 * size
    lane = iota((1, 128), 1)
    half = lane < 64
    diag[...] = jnp.zeros_like(diag)

    def pair(p, slot, out):
        cols = pl.ds(pl.multiple_of(p * 128, 128), 128)
        qp, kp = q[:, cols], k[:, cols]
        vp = v[:, cols].astype(F32)
        do = grad_att[:, cols].astype(F32)
        prod = do * attended[:, cols].astype(F32)
        dq_all = None
        base = pl.multiple_of(slot * 128, 128)
        for side in range(2):
            head = 2 * p + side
            own = half if side == 0 else jnp.logical_not(half)
            one = 64 if side == 0 else 0
            inv = jnp.sum(jnp.where(lane == head, inv_sums[...], 0.0), axis=1, keepdims=True)
            inner = jnp.sum(jnp.where(own, prod, 0.0), axis=1, keepdims=True) * inv
            upper = inner.astype(BF16).astype(F32)
            dos = jnp.where(
                own,
                do * inv,
                jnp.where(lane == one, -upper, jnp.where(lane == one + 1, upper - inner, 0.0)),
            ).astype(BF16)
            ones = (lane == one) | (lane == one + 1)
            va = jnp.where(own, vp, jnp.where(ones, 1.0, 0.0)).astype(BF16)
            slant[...] = jnp.zeros_like(slant)
            for a in range(strips):
                rows = slice(128 * a, 128 * a + 128)
                off = 128 * (strips - 1 - a)
                e = powers[head, rows, :]
                ds = (e.astype(F32) * dot_right(va[rows], dos)).astype(BF16)
                grads[rows, :] = ds
                slant[:, off : off + size] += ds.astype(F32)
                dk = dot(ds, qp).astype(BF16)
                dv = dot(e, dos).astype(BF16)
                kcols = pl.ds(base + width // 2, 128)
                vcols = pl.ds(base + width, 128)
                if side == 1:
                    dk = jnp.where(half, out[rows, kcols].astype(F32), dk.astype(F32)).astype(BF16)
                    dv = jnp.where(half, out[rows, vcols].astype(F32), dv.astype(F32)).astype(BF16)
                out[rows, kcols] = dk
                out[rows, vcols] = dv
            dq = dot_left(kp, grads[...]).T
            dq_all = dq if side == 0 else jnp.where(half, dq_all, dq)
            y = slant[...]
            rest = 64
            while rest >= 1:
                y = y[:rest] + pltpu.roll(y[rest:], span - rest, 1)
                rest //= 2
            diag[pl.ds(head, 1), :] = pltpu.roll(y, 127, 1)
        out[:, pl.ds(base, 128)] = dq_all.astype(BF16)

    mine = meta[2]

    def first(t, carry):
        pair((1 - mine) * group + t, t, send)
        return carry

    def second(t, carry):
        pair(mine * group + t, t, keep)
        return carry

    lax.fori_loop(0, group, first, 0)
    lax.fori_loop(0, group, second, 0)
    hot = (buckets[...] == iota((grad_table.shape[1], span), 0)).astype(F32)
    grad_table[...] = lax.dot_general(
        diag[...],
        hot,
        (((1,), (1,)), ((), ())),
        preferred_element_type=F32,
        precision=lax.Precision.HIGHEST,
    )


def input_kernel(copies, n_pieces, *refs):
    meta, hidden, grad_residual, send, keep, gain = refs[:6]
    pieces = refs[6 : 6 + n_pieces]
    grad_hidden, grad_gain, wq, wk, wv, sems = refs[6 + n_pieces :]
    wait_all(place(meta, pieces, (wq, wk, wv), copies, sems))
    size, width = hidden.shape
    part = width // 2
    mine = meta[2]
    grad_gain[...] = jnp.zeros_like(grad_gain)

    def rows(ds):
        total = None
        for ref, which in ((send, 1 - mine), (keep, mine)):
            cols = pl.ds(pl.multiple_of(which * part, 128), part)
            for n, w in enumerate((wq, wk, wv)):
                t = dot_right(ref[ds, n * part : (n + 1) * part], w[:, cols])
                total = t if total is None else total + t
        x = hidden[ds, :].astype(F32)
        inv = lax.rsqrt(jnp.mean(x * x, axis=-1, keepdims=True) + EPS)
        u = gain[...] * total
        xr = x * inv
        grad_gain[...] += jnp.sum(xr * total, axis=0, keepdims=True)
        grad_hidden[ds, :] = grad_residual[ds, :] + inv * (
            u - xr * jnp.mean(xr * u, axis=-1, keepdims=True)
        )

    rows_loop(size, 256, rows)


def weights_kernel(plan, n_out, *refs):
    meta, x_own, x_peer, keep, got, att_own, att_peer, low_own, low_peer, extra = refs[:10]
    outs = refs[10 : 10 + n_out]
    grads, out_sems = refs[10 + n_out :]
    part = keep.shape[1]
    depth = x_own.shape[1]
    for c in range(0, depth, 256):
        cols = slice(c, c + 256)
        g = dot_left(x_own[:, cols], keep[...]) + dot_left(x_peer[:, cols], got[...])
        grads[cols, 0:part] = g.astype(BF16)
        g = dot_left(att_own[:, cols], low_own[...]) + dot_left(att_peer[:, cols], low_peer[...])
        grads[cols, part:] = g.astype(BF16)
    grads[depth:, :] = extra[...]
    wait_all(scatter_out(meta, grads, outs, plan, out_sems))


def output_kernel(copies, n_pieces, *refs):
    meta, activated = refs[:2]
    pieces = refs[2 : 2 + n_pieces]
    part_own, part_peer, w_ffout, sems = refs[2 + n_pieces :]
    wait_all(place(meta, pieces, (w_ffout,), copies, sems))
    size = part_own.shape[0]
    for which, part in ((1, part_peer), (0, part_own)):

        def rows(ds, which=which, part=part):
            part[ds, :] = dot(activated[which, ds, :], w_ffout[...]).astype(part.dtype)

        rows_loop(size, 256, rows)


def finish_kernel(meta, residual, part, other, sums, hidden_out, pooled, stats):
    size, width = residual.shape
    length, prefix = meta[4], meta[5]
    count = (length - prefix).astype(F32)
    pooled[...] = jnp.zeros_like(pooled)
    stats[...] = jnp.zeros_like(stats)

    def rows(ds):
        branch = part[ds, :] + other[ds, :].astype(F32)
        out = residual[ds, :] + branch
        hidden_out[ds, :] = out.astype(BF16)
        t = iota((128, 1), 0) + ds.start
        live = t < length
        stats[0:1, :] += jnp.sum(jnp.where(live, branch * branch, 0.0), axis=0, keepdims=True)
        pooled[...] += jnp.sum(jnp.where((t >= prefix) & live, out, 0.0), axis=0, keepdims=True)

    rows_loop(size, 128, rows)
    pooled[...] = pooled[...] / count
    total = jnp.sum(stats[0:1, :])
    first = jnp.sum(sums[0:1, :])
    second = jnp.sum(sums[1:2, :])
    denominator = length.astype(F32) * width
    column = iota(stats.shape, 1)
    values = jnp.where(column == 0, first, jnp.where(column == 1, second, total))
    stats[...] = jnp.sqrt(values / denominator)


def swap(v, axis, count, far):
    return lax.ppermute(v, axis, [(i, i ^ far) for i in range(count)])


def add(a, b):
    return (a.astype(F32) + b.astype(F32)).astype(BF16)


def chip_gather(v):
    h = v.shape[0] // 2
    by_x = swap(v, "fsdp", 8, 2)
    by_y = swap(v, "fsdp", 8, 4)
    upper = swap(by_x[:h], "fsdp", 8, 4)
    lower = swap(by_y[h:], "fsdp", 8, 2)
    return [(v, 0, 0), (by_x, 0, 1), (by_y, 0, 2), (upper, 0, 3), (lower, h, 3)]


def chip_scatter(to_x, to_y, keep_a, keep_b, extra=0):
    h = keep_a.shape[0] // 2
    if extra:
        h = (keep_a.shape[0] - extra) // 2
    got_x = swap(to_x, "fsdp", 8, 2)
    got_y = swap(to_y, "fsdp", 8, 4)
    on_y = add(keep_a[h:], got_x[h:])
    on_x = add(keep_b[h:], got_y[h:])
    last_y = swap(on_y, "fsdp", 8, 4)
    last_x = swap(on_x, "fsdp", 8, 2)
    own_a = add(keep_a[:h], got_x[:h])
    own_b = add(keep_b[:h], got_y[:h])
    upper = add(own_a, last_y[:h])
    lower = add(own_b, last_x)
    parts = [upper, lower]
    if extra:
        parts.append(add(on_y[h:], last_y[h:]))
    return jnp.concatenate(parts, axis=0)


def chain_sum(v, count, where):
    if count != 4:
        for bit in range(count.bit_length() - 1):
            v = add(v, swap(v, "dp", count, 1 << bit))
        return v
    v = add(v, lax.ppermute(v, "dp", [(0, 1), (3, 2)]))
    v = add(v, lax.ppermute(v, "dp", [(1, 2), (2, 1)]))
    back = lax.ppermute(v, "dp", [(1, 0), (2, 3)])
    return jnp.where((where == 1) | (where == 2), v, back)


def message_plan(unit):
    h = unit // 2
    plan = []
    for dst, (near, far) in enumerate(((1, 3), (2, 3), (0, 2), (0, 1))):
        offset = 0 if dst in (0, 2) else h
        plan.append((dst, 0, h, unit, near, offset))
        plan.append((dst, h, h, unit, far, offset))
    return plan


def body(
    nf,
    nz,
    hidden_in,
    norm_gain_attn,
    w_query,
    w_key,
    w_value,
    w_out,
    rel_bias,
    norm_gain_ffn,
    w_in,
    w_ffout,
    bucket_index,
    row_lengths,
    prefix_lengths,
    out_cotangent,
    pool_cotangent,
):
    fast = nf == 8 and nz & (nz - 1) == 0
    size, width = hidden_in.shape
    shard = w_query.shape[0]
    heads = rel_bias.shape[1]
    levels = rel_bias.shape[0] * nf
    full_ff = w_in.shape[1]
    part_ff = full_ff // 2
    block = w_ffout.shape[0]
    half = width // 2
    me = lax.axis_index("fsdp").astype(jnp.int32)
    where = lax.axis_index("dp").astype(jnp.int32)
    core = me & 1
    zero = jnp.zeros((), jnp.int32)
    meta = jnp.stack([me, me >> 1, core, where, row_lengths[0], prefix_lengths[0], zero, zero])

    def by_core(first, second):
        return jnp.where(core == 0, first, second)

    def peer(v):
        return swap(v, "fsdp", nf, 1)

    cols = w_in.reshape(shard, nf // 2, 2, block)
    kept = by_core(cols[:, :, 0], cols[:, :, 1]).reshape(shard, part_ff)
    given = by_core(cols[:, :, 1], cols[:, :, 0]).reshape(shard, part_ff)
    if fast:
        stage = chip_gather(jnp.concatenate([w_query, w_key, w_value], axis=0))
        qkv_pieces, qkv_copies = [], []

        def put(piece, first, far):
            number = len(qkv_pieces)
            qkv_pieces.append(piece)
            for n in range(3):
                low, high = max(first, n * shard), min(first + piece.shape[0], (n + 1) * shard)
                if low < high:
                    qkv_copies.append(
                        (number, low - first, high - low, n, low - n * shard, 0, shard, far, 0)
                    )

        for piece, first, far in stage:
            put(piece, first, 2 * far)
            put(peer(piece), first, 2 * far + 1)

        taken = peer(given)
        both = by_core(
            jnp.concatenate([kept, taken], axis=0), jnp.concatenate([taken, kept], axis=0)
        )
        second = jnp.concatenate([w_out, both[:, :width], both[:, width:]], axis=0)
        in_pieces, in_copies, out_pieces, out_copies = [], [], [], []
        for piece, first, far in chip_gather(second):
            number = len(in_pieces)
            in_pieces.append(piece)
            for n in range(2):
                start = shard + n * 2 * shard
                low, high = max(first, start), min(first + piece.shape[0], start + 2 * shard)
                if low < high:
                    in_copies.append(
                        (number, low - first, high - low, 0, low - start, n * width, 2 * shard, far, 1)
                    )
            if first == 0:
                rows = piece[:shard]
                for extra, arr in ((0, rows), (1, peer(rows))):
                    out_copies.append(
                        (len(out_pieces), 0, shard, 0, 0, 0, shard, 2 * far + extra, 0)
                    )
                    out_pieces.append(arr)
        ff_pieces, ff_copies = [], []
        for piece, first, far in chip_gather(w_ffout):
            ff_copies.append(
                (len(ff_pieces), 0, piece.shape[0], 0, first, 0, block, far, 1)
            )
            ff_pieces.append(piece)
    else:

        def whole(v):
            return lax.all_gather(v, "fsdp", axis=0, tiled=True)

        qkv_pieces = [whole(w) for w in (w_query, w_key, w_value)]
        qkv_copies = [(n, 0, width, n, 0, 0, 0, 0, 0) for n in range(3)]
        out_pieces, out_copies = [whole(w_out)], [(0, 0, width, 0, 0, 0, 0, 0, 0)]
        all_in = whole(w_in).reshape(width, nf // 2, 2, block)
        in_pieces = [by_core(all_in[:, :, 0], all_in[:, :, 1]).reshape(width, part_ff)]
        in_copies = [(0, 0, width, 0, 0, 0, 0, 0, 0)]
        all_ff = whole(w_ffout).reshape(nf // 2, 2, block, width)
        ff_pieces = [by_core(all_ff[:, 0], all_ff[:, 1]).reshape(part_ff, width)]
        ff_copies = [(0, 0, part_ff, 0, 0, 0, 0, 0, 0)]

    small = jnp.concatenate([norm_gain_attn, norm_gain_ffn, rel_bias.reshape(-1)])
    small = lax.all_gather(small, "fsdp").astype(F32)
    gain_one = small[:, :shard].reshape(1, width)
    gain_two = small[:, shard : 2 * shard].reshape(1, width)
    table = small[:, 2 * shard :].reshape(levels, heads).T
    head_rows = -(-heads // 16) * 16
    table = jnp.pad(table, ((0, head_rows - heads), (0, 0))).astype(BF16)
    buckets = jnp.concatenate([bucket_index[::-1], jnp.full((1,), -1, jnp.int32)])[None, :]

    def dma(n):
        return pltpu.SemaphoreType.DMA((n,))

    def ins(arrays):
        return [(a, "h") for a in arrays]

    meta_in = (meta, "s")
    dense = size * width * width
    normed, bias, low = call(
        prepare_kernel,
        "prepare",
        [meta_in] + [(a, "v") for a in (hidden_in, gain_one, table, buckets, out_cotangent, pool_cotangent)],
        [
            ((size, width), BF16, "v"),
            ((heads, 128, 2 * size - 128), F32, "v"),
            ((size, width), BF16, "v"),
        ],
        [pltpu.VMEM((head_rows, 2 * size), F32)],
        nbytes=12 * 2**20,
    )
    low_peer = peer(low)
    normed_peer = peer(normed)
    square = pltpu.VMEM((width, width), BF16)
    q, k, v, attended, powers, inv_sums = call(
        functools.partial(attend_kernel, qkv_copies, len(qkv_pieces)),
        "attend",
        [meta_in, (normed, "v"), (bias, "v")] + ins(qkv_pieces),
        [((size, width), BF16, "v")] * 4
        + [((heads, size, size), BF16, "v"), ((size, 128), F32, "v")],
        [square] * 3 + [pltpu.VMEM((size, size), F32), dma(len(qkv_copies))],
        flops=8 * dense,
        nbytes=20 * 2**20,
        trans=heads * size * size,
    )
    attended_peer = peer(attended)
    residual, normed_two, sums = call(
        functools.partial(residual_kernel, out_copies, len(out_pieces)),
        "residual",
        [meta_in, (hidden_in, "v"), (attended, "v"), (gain_two, "v")] + ins(out_pieces),
        [((size, width), F32, "v"), ((size, width), BF16, "v"), ((8, width), F32, "v")],
        [square, dma(len(out_copies))],
        flops=2 * dense,
        nbytes=6 * 2**20,
    )
    normed_two_peer = peer(normed_two)
    shape_in = pltpu.VMEM((width, part_ff), BF16)
    shape_ff = pltpu.VMEM((part_ff, width), BF16)
    if fast:
        ff_plan, in_plan = message_plan(block), message_plan(2 * shard)
        ff_outs = [((block, width), BF16, "h")] * 4
        in_outs = [((2 * shard, part_ff), BF16, "h")] * 4
    else:
        ff_plan = [(0, 0, part_ff, 0, 0, 0)]
        in_plan = [(0, 0, width, 0, 0, 0)]
        ff_outs = [((part_ff, width), BF16, "h")]
        in_outs = [((width, part_ff), BF16, "h")]
    activated, slope, *ff_parts = call(
        functools.partial(expand_kernel, in_copies, len(in_pieces), ff_plan, len(ff_outs)),
        "expand",
        [meta_in]
        + [(a, "v") for a in (normed_two, normed_two_peer, low, low_peer)]
        + ins(in_pieces),
        [((2, size, part_ff), BF16, "v")] * 2 + ff_outs,
        [shape_in, shape_ff, dma(len(in_copies)), dma(len(ff_plan))],
        flops=16 * dense,
        nbytes=16 * 2**20,
        trans=size * full_ff,
    )
    grad_pre, part_gn, send_gn = call(
        functools.partial(
            contract_kernel,
            in_copies + [(n + len(in_pieces), r, c, 1, b, o, u, f, l) for n, r, c, d, b, o, u, f, l in ff_copies],
            len(in_pieces) + len(ff_pieces),
        ),
        "contract",
        [meta_in] + [(a, "v") for a in (slope, low, low_peer)] + ins(in_pieces + ff_pieces),
        [
            ((2, size, part_ff), BF16, "v"),
            ((size, width), F32, "v"),
            ((size, width), BF16, "v"),
        ],
        [shape_in, shape_ff, dma(len(in_copies) + len(ff_copies))],
        flops=16 * dense,
        nbytes=16 * 2**20,
    )
    other_gn = peer(send_gn)
    in_parts = call(
        functools.partial(outer_kernel, in_plan, len(in_outs)),
        "outer",
        [meta_in] + [(a, "v") for a in (normed_two, normed_two_peer, grad_pre)],
        in_outs,
        [shape_in, dma(len(in_plan))],
        flops=8 * dense,
        nbytes=8 * 2**20,
    )
    grad_residual, low_residual, grad_attended, grad_gain_two = call(
        functools.partial(through_kernel, out_copies, len(out_pieces)),
        "through",
        [meta_in]
        + [(a, "v") for a in (residual, part_gn, other_gn, out_cotangent, pool_cotangent, gain_two)]
        + ins(out_pieces),
        [
            ((size, width), F32, "v"),
            ((size, width), BF16, "v"),
            ((size, width), BF16, "v"),
            ((1, width), F32, "v"),
        ],
        [square, dma(len(out_copies))],
        flops=2 * dense,
        nbytes=10 * 2**20,
    )
    low_mine = by_core(low_residual[:, :half], low_residual[:, half:])
    low_other = peer(by_core(low_residual[:, half:], low_residual[:, :half]))
    send, keep, grad_table = call(
        attend_back_kernel,
        "attend_back",
        [meta_in]
        + [(a, "v") for a in (q, k, v, powers, grad_attended, attended, inv_sums, buckets)],
        [
            ((size, 3 * half), BF16, "v"),
            ((size, 3 * half), BF16, "v"),
            ((head_rows, levels), F32, "v"),
        ],
        [
            pltpu.VMEM((size, size), BF16),
            pltpu.VMEM((128, 2 * size), F32),
            pltpu.VMEM((head_rows, 2 * size), F32),
        ],
        flops=10 * dense,
        nbytes=14 * 2**20,
    )
    got = peer(send)
    grad_hidden, grad_gain_one = call(
        functools.partial(input_kernel, qkv_copies, len(qkv_pieces)),
        "inputs",
        [meta_in]
        + [(a, "v") for a in (hidden_in, grad_residual, send, keep, gain_one)]
        + ins(qkv_pieces),
        [((size, width), F32, "v"), ((1, width), F32, "v")],
        [square] * 3 + [dma(len(qkv_copies))],
        flops=6 * dense,
        nbytes=12 * 2**20,
    )
    tail = jnp.concatenate([grad_gain_one, grad_gain_two, grad_table[:heads].T.reshape(1, -1)], axis=1)
    tail_size = tail.shape[1]
    tail = jnp.pad(tail, ((0, 0), (0, 4 * half * 2 - tail_size))).reshape(2, 4 * half)
    extra = jnp.pad(tail, ((0, 14), (0, 0))).astype(BF16)
    if fast:
        at_plan = message_plan(2 * shard)
        at_plan = at_plan + [
            (0, 2 * shard, 16, 0, 0, width),
            (2, 2 * shard, 16, 0, 0, width),
        ]
        at_outs = [((2 * shard + (16 if n in (0, 2) else 0), 4 * half), BF16, "h") for n in range(4)]
    else:
        at_plan = [(0, 0, width + 16, 0, 0, 0)]
        at_outs = [((width + 16, 4 * half), BF16, "h")]
    at_parts = call(
        functools.partial(weights_kernel, at_plan, len(at_outs)),
        "weights",
        [meta_in]
        + [
            (a, "v")
            for a in (normed, normed_peer, keep, got, attended, attended_peer, low_mine, low_other, extra)
        ],
        at_outs,
        [pltpu.VMEM((width + 16, 4 * half), BF16), dma(len(at_plan))],
        flops=8 * dense,
        nbytes=10 * 2**20,
    )
    part_branch, send_branch = call(
        functools.partial(output_kernel, ff_copies, len(ff_pieces)),
        "output",
        [meta_in, (activated, "v")] + ins(ff_pieces),
        [((size, width), F32, "v"), ((size, width), BF16, "v")],
        [shape_ff, dma(len(ff_copies))],
        flops=8 * dense,
        nbytes=8 * 2**20,
    )
    other_branch = peer(send_branch)
    hidden_out, pooled, stats = call(
        finish_kernel,
        "finish",
        [meta_in] + [(a, "v") for a in (residual, part_branch, other_branch, sums)],
        [((size, width), BF16, "v"), ((1, width), F32, "v"), ((1, width), F32, "v")],
        nbytes=6 * 2**20,
    )

    if fast:
        sum_ff = chip_scatter(*ff_parts)
        grad_ffout = chain_sum(sum_ff, nz, where).astype(F32)

        def trade(v):
            mine_rows = by_core(v[:shard], v[shard : 2 * shard])
            other_rows = by_core(v[shard : 2 * shard], v[:shard])
            return mine_rows, other_rows

        sum_in = chip_scatter(*in_parts)
        mine_in, other_in = trade(sum_in)
        sum_in = jnp.concatenate([mine_in, peer(other_in)], axis=0)
        sum_in = chain_sum(sum_in, nz, where)
        mine_in = sum_in[:shard].reshape(shard, nf // 2, 1, block)
        other_in = sum_in[shard:].reshape(shard, nf // 2, 1, block)
        grad_in = by_core(
            jnp.concatenate([mine_in, other_in], axis=2),
            jnp.concatenate([other_in, mine_in], axis=2),
        ).reshape(shard, full_ff).astype(F32)
        sum_at = chip_scatter(*at_parts, extra=16)
        mine_at, other_at = trade(sum_at)
        rest = sum_at[2 * shard :]
        got_at = peer(jnp.concatenate([other_at, rest], axis=0))
        sum_at = jnp.concatenate([mine_at, got_at[:shard], add(rest, got_at[shard:])], axis=0)
        sum_at = chain_sum(sum_at, nz, where)
        mine_at, other_at = sum_at[:shard], sum_at[shard : 2 * shard]
        rest = sum_at[2 * shard :].astype(F32)

        def joined(n):
            a, b = mine_at[:, n * half : (n + 1) * half], other_at[:, n * half : (n + 1) * half]
            return by_core(jnp.concatenate([a, b], axis=1), jnp.concatenate([b, a], axis=1)).astype(F32)

    else:

        def reduced(v):
            v = lax.psum_scatter(v, "fsdp", scatter_dimension=0, tiled=True)
            return lax.psum(v, "dp").astype(F32)

        def spread(v, axis):
            none = jnp.zeros_like(v)
            return by_core(jnp.stack([v, none], axis), jnp.stack([none, v], axis))

        grad_ffout = reduced(
            spread(ff_parts[0].reshape(nf // 2, block, width), 1).reshape(full_ff, width)
        )
        grad_in = reduced(
            spread(in_parts[0].reshape(width, nf // 2, block), 2).reshape(width, full_ff)
        )
        grads = spread(at_parts[0][:width].reshape(width, 4, half), 2).reshape(width, 4 * width)
        grads = reduced(grads)
        rest = lax.psum(at_parts[0][width:], ("fsdp", "dp")).astype(F32)

        def joined(n):
            return grads[:, n * width : (n + 1) * width]

    rest = rest[:2].reshape(-1)
    all_one, all_two = rest[:width], rest[width : 2 * width]
    all_table = rest[2 * width : 2 * width + levels * heads].reshape(levels, heads)

    def mine(v):
        count = v.shape[0] // nf
        return lax.dynamic_slice_in_dim(v, me * count, count, 0)

    return (
        hidden_out,
        pooled,
        grad_hidden,
        mine(all_one),
        joined(0),
        joined(1),
        joined(2),
        joined(3),
        mine(all_table),
        mine(all_two),
        grad_in,
        grad_ffout,
        stats[:, :3],
    )


def solution(mesh):
    token = P(("fsdp", "dp"), None)
    weight = P("fsdp", None)
    return jax.shard_map(
        functools.partial(body, mesh.shape["fsdp"], mesh.shape["dp"]),
        mesh=mesh,
        in_specs=(
            token,
            P("fsdp"),
            weight,
            weight,
            weight,
            weight,
            weight,
            P("fsdp"),
            weight,
            weight,
            P(),
            P(("fsdp", "dp")),
            P(("fsdp", "dp")),
            token,
            token,
        ),
        out_specs=(
            token,
            token,
            token,
            P("fsdp"),
            weight,
            weight,
            weight,
            weight,
            weight,
            P("fsdp"),
            weight,
            weight,
            token,
        ),
        check_vma=False,
    )
```

```python
import functools
import math

import jax
import jax.numpy as jnp
from jax import lax
from jax.experimental import pallas as pl
from jax.experimental.pallas import tpu as pltpu
from jax.sharding import PartitionSpec as P

EPS = 1e-06
F32 = jnp.float32
BF16 = jnp.bfloat16
VMEM_SPARE = 6 * 2**20
WEIGHTS = {"turn": 30.0, "expand_own": 30.0}
GELU_A = 0.7978845608028654
GELU_B = 0.044715


def dot(a, b):
    return lax.dot_general(a, b, (((1,), (0,)), ((), ())), preferred_element_type=F32)


def dot_right(a, b):
    return lax.dot_general(a, b, (((1,), (1,)), ((), ())), preferred_element_type=F32)


def dot_left(a, b):
    return lax.dot_general(a, b, (((0,), (0,)), ((), ())), preferred_element_type=F32)


def iota(shape, dim):
    return lax.broadcasted_iota(jnp.int32, shape, dim)


def call(kernel, name, meta, ins, outs, scratch=(), deps=(), limit=0):
    spaces = {"v": pltpu.VMEM, "s": pltpu.SMEM, "h": pl.ANY}
    held = [(a.shape, a.dtype) for a, m in ins if m == "v"]
    held += [(s, d) for s, d, m in outs if m == "v"]
    held += [(x.shape, x.dtype) for x in scratch if x.memory_space == pltpu.VMEM]
    need = sum(math.prod(s) * jnp.dtype(d).itemsize for s, d in held)
    ins = [(after(meta, *deps), "s")] + list(ins)
    return pl.pallas_call(
        kernel,
        name=name,
        out_shape=[jax.ShapeDtypeStruct(s, d) for s, d, _ in outs],
        in_specs=[pl.BlockSpec(memory_space=spaces[m]) for _, m in ins],
        out_specs=[pl.BlockSpec(memory_space=spaces[m]) for _, _, m in outs],
        scratch_shapes=list(scratch),
        compiler_params=pltpu.CompilerParams(vmem_limit_bytes=max(limit, need + VMEM_SPARE)),
        cost_estimate=pl.CostEstimate(
            flops=1000, bytes_accessed=int(3.7e6 * WEIGHTS.get(name, 0.0)) + 1000, transcendentals=0
        ),
    )(*[a for a, _ in ins])


def after(v, *deps):
    return lax.optimization_barrier((v,) + deps)[0] if deps else v


def place(meta, pieces, targets, copies):
    for src, row, rows, from_column, dst, base, column, width, unit, far, side in copies:
        start = base
        if unit:
            start = base + unit * jnp.bitwise_xor(meta[1], far)
            if side == 1:
                start = start + (unit // 2) * meta[2]
            if side == 2:
                start = start + (unit // 2) * (1 - meta[2])
            start = pl.multiple_of(start, 16)
        targets[dst][pl.ds(start, rows), column : column + width] = pieces[src][
            row : row + rows, from_column : from_column + width
        ]


def rows_loop(count, step, fn):
    def one(i, carry):
        fn(pl.ds(pl.multiple_of(i * step, step), step))
        return carry

    lax.fori_loop(0, count // step, one, 0)


def scatter_out(meta, scratch, outs, plan):
    for dst, row, rows, unit, far, offset in plan:
        start = offset
        if unit:
            start = pl.multiple_of(offset + unit * jnp.bitwise_xor(meta[1], far), 16)
        outs[dst][row : row + rows, :] = scratch[pl.ds(start, rows), :]


def pack_kernel(n_chips, meta, *refs):
    sources = refs[:5]
    gain_one, gain_two, rel = refs[5:8]
    kept_a, given_a, kept_b, given_b, small = refs[8:13]
    held, sems = refs[13:18], refs[18]
    handles = [pltpu.make_async_copy(a, b, sems.at[n]) for n, (a, b) in enumerate(zip(sources, held))]
    for handle in handles:
        handle.start()
    small[...] = jnp.zeros_like(small)
    small[0:1, 0 : gain_one.shape[1]] = gain_one[...].astype(F32)
    small[1:2, 0 : gain_two.shape[1]] = gain_two[...].astype(F32)
    small[2:3, :] = jnp.broadcast_to(meta[4].astype(F32), (1, 128))
    small[4 : 4 + rel.shape[0], 0 : rel.shape[1]] = rel[...].astype(F32)
    for handle in handles:
        handle.wait()
    wq, wk, wv, wo, w_in = held
    core = meta[2]
    half = wq.shape[1] // 2
    block = w_in.shape[1] // (2 * n_chips)
    for which, a_ref, b_ref in ((core, kept_a, kept_b), (1 - core, given_a, given_b)):
        for n, w in enumerate((wq, wk, wv, wo)):
            cols = pl.ds(pl.multiple_of(which * half, 128), half)
            a_ref[:, n * half : (n + 1) * half] = w[:, cols]
        for n in range(b_ref.shape[1] // block):
            cols = pl.ds(pl.multiple_of((2 * n + which) * block, 128), block)
            b_ref[:, n * block : (n + 1) * block] = w_in[:, cols]


def stack_kernel(meta, kept_a, taken_a, kept_b, taken_b, both_a, both_b):
    shard = kept_a.shape[0]
    mine = pl.ds(pl.multiple_of(shard * meta[2], 16), shard)
    theirs = pl.ds(pl.multiple_of(shard * (1 - meta[2]), 16), shard)
    for kept, taken, both in ((kept_a, taken_a, both_a), (kept_b, taken_b, both_b)):
        both[mine, :] = kept[...]
        both[theirs, :] = taken[...]


def rows_kernel(meta, *refs):
    for n, ref in enumerate(refs[:-1]):
        refs[-1][8 * n : 8 * n + 8, :] = ref[...]


def prepare_kernel(n_small, relative, levels, meta, hidden, hidden_peer, *refs):
    smalls = refs[:n_small]
    buckets, out_cot, pool_cot = refs[n_small : n_small + 3]
    normed, normed_peer, bias, low, gain_one, gain_two, length_peer, table, table_rows = refs[n_small + 3 :]
    size, width = hidden.shape
    length, prefix = meta[4], meta[5]
    count = (length - prefix).astype(F32)
    pieces = [ref[8 * n : 8 * n + 8, :] for ref in smalls for n in range(ref.shape[0] // 8)]
    shard = width // len(pieces)
    some = levels // len(pieces)
    table[...] = jnp.zeros_like(table)
    first = jnp.zeros((1, width), F32)
    second = jnp.zeros((1, width), F32)
    rest = jnp.zeros((1, width - 128), F32)
    peers = jnp.zeros((1, 128), F32)
    for p, piece in enumerate(pieces):
        where = jnp.bitwise_xor(meta[0], 2 * (p % 4) + p // 4) if relative else jnp.int32(p)
        first += pltpu.roll(jnp.concatenate([piece[0:1], rest], axis=1), shard * where, 1)
        second += pltpu.roll(jnp.concatenate([piece[1:2], rest], axis=1), shard * where, 1)
        peers += jnp.where(where == jnp.bitwise_xor(meta[0], 1), piece[2:3], 0.0)
        for b in range(some):
            table[pl.ds(some * where + b, 1), :] = piece[4 + b : 5 + b]
    length_peer[...] = peers
    gain_one[...] = first
    gain_two[...] = second

    for x_ref, n_ref in ((hidden, normed), (hidden_peer, normed_peer)):

        def rows(ds, x_ref=x_ref, n_ref=n_ref):
            x = x_ref[ds, :].astype(F32)
            inv = lax.rsqrt(jnp.mean(x * x, axis=-1, keepdims=True) + EPS)
            n_ref[ds, :] = (x * inv * gain_one[...]).astype(BF16)

        rows_loop(size, 256, rows)

    def lows(ds):
        t = iota((256, 1), 0) + ds.start
        pool = jnp.where((t >= prefix) & (t < length), 1.0, 0.0) / count
        low[ds, :] = (out_cot[ds, :].astype(F32) + pool * pool_cot[...]).astype(BF16)

    rows_loop(size, 256, lows)
    span = 2 * size
    hot = (buckets[...] == iota((levels, span), 0)).astype(BF16)
    table_rows[...] = dot_left(table[...].astype(BF16), hot)
    heads, _, wide = bias.shape
    base = heads * meta[2]

    def head(h, carry):
        row = table_rows[pl.ds(base + h, 1), :]
        first = jnp.broadcast_to(pltpu.roll(row, span - 127, 1), (8, span))
        sub = iota((8, span), 0)
        full = first
        for k in range(1, 8):
            full = jnp.where(sub == k, pltpu.roll(first, k, 1), full)
        bias[h, 0:8, :] = full[:, :wide]
        have = 8
        while have < 128:
            more = pltpu.roll(full, have, 1)
            bias[h, have : 2 * have, :] = more[:, :wide]
            full = jnp.concatenate([full, more], axis=0)
            have *= 2
        return carry

    lax.fori_loop(0, heads, head, 0)


def collect_kernel(copies, n_pieces, *refs):
    meta = refs[0]
    pieces = refs[1 : 1 + n_pieces]
    qkv, w_half = refs[1 + n_pieces :]
    place(meta, pieces, (qkv, w_half), copies)


def attend_kernel(meta, x_ref, bias, w, length, qkv, out, upper, lower, powers, inv_sums, scores):
    size = x_ref.shape[0]
    part = w.shape[1] // 3
    pairs = part // 128
    lane = iota((1, 128), 1)
    half = lane < 64
    strips = size // 128
    inv_sums[...] = jnp.zeros_like(inv_sums)

    def project(ds):
        for n in range(3):
            cols = slice(n * part, (n + 1) * part)
            qkv[ds, cols] = dot(x_ref[ds, :], w[:, cols]).astype(BF16)

    rows_loop(size, 256, project)
    masked = jnp.where(iota((size, 1), 0).astype(F32) < length[0:1, 0:1], 0.0, -1e30).astype(F32)

    def pair(p, carry):
        base = pl.multiple_of(p * 128, 128)
        qp = qkv[:, pl.ds(base, 128)].astype(F32)
        kp = qkv[:, pl.ds(base + part, 128)].astype(F32)
        vp = qkv[:, pl.ds(base + 2 * part, 128)].astype(F32)
        joined = None
        for side in range(2):
            head = 2 * p + side
            own = half if side == 0 else jnp.logical_not(half)
            spare = lane == (64 if side == 0 else 0)
            qa = jnp.where(own, qp, jnp.where(spare, 1.0, 0.0)).astype(BF16)
            ka = jnp.where(own, kp, jnp.where(spare, masked, 0.0)).astype(BF16)
            va = jnp.where(own, vp, jnp.where(spare, 1.0, 0.0)).astype(BF16)
            top = None
            for a in range(strips):
                rows = slice(128 * a, 128 * a + 128)
                off = 128 * (strips - 1 - a)
                s = dot_right(ka[rows], qa) + bias[head, :, off : off + size]
                scores[rows, :] = s
                peak = jnp.max(s, axis=0, keepdims=True)
                top = peak if top is None else jnp.maximum(top, peak)
            for a in range(strips):
                rows = slice(128 * a, 128 * a + 128)
                powers[head, rows, :] = jnp.exp(scores[rows, :] - top).astype(BF16)
            mixed = dot_left(va, powers[head]).T
            sums = jnp.sum(jnp.where(spare, mixed, 0.0), axis=1, keepdims=True)
            inv = 1.0 / sums
            inv_sums[...] = jnp.where(lane == head, inv, inv_sums[...])
            mixed = mixed * inv
            joined = mixed if side == 0 else jnp.where(half, joined, mixed)
        joined = joined.astype(BF16)
        cols = pl.ds(base, 128)
        out[:, cols] = joined
        upper[:, cols] = joined[: size // 2]
        lower[:, cols] = joined[size // 2 :]
        return carry

    lax.fori_loop(0, pairs, pair, 0)


def residual_kernel(meta, hidden, attended, upper, lower, gain, w_half, w_other, residual, normed, left, middle, right, sums, w_out):
    size, width = hidden.shape
    half = width // 2
    length = meta[4]
    core = meta[2]
    w_out[:, pl.ds(pl.multiple_of(core * half, 128), half)] = w_half[...]
    w_out[:, pl.ds(pl.multiple_of((1 - core) * half, 128), half)] = w_other[...]
    mine = pl.ds(pl.multiple_of(core * half, 128), half)
    other = pl.ds(pl.multiple_of((1 - core) * half, 128), half)
    sums[...] = jnp.zeros_like(sums)

    for first, got in ((0, upper), (size // 2, lower)):
        ds = slice(first, first + size // 2)
        x = hidden[ds, :].astype(F32)
        branch = dot(attended[ds, :], w_out[mine, :]) + dot(got[...], w_out[other, :])
        live = (iota((size // 2, 1), 0) + first) < length
        sums[0:1, :] += jnp.sum(jnp.where(live, x * x, 0.0), axis=0, keepdims=True)
        sums[1:2, :] += jnp.sum(jnp.where(live, branch * branch, 0.0), axis=0, keepdims=True)
        r = x + branch
        residual[ds, :] = r
        inv = lax.rsqrt(jnp.mean(r * r, axis=-1, keepdims=True) + EPS)
        value = (r * inv * gain[...]).astype(BF16)
        normed[ds, :] = value
        third = left.shape[1]
        for n, ref in enumerate((left, middle, right)):
            ref[ds, :] = value[:, n * third : (n + 1) * third]


def expand_kernel(copies, n_pieces, *refs):
    meta, x_ref = refs[:2]
    pieces = refs[2 : 2 + n_pieces]
    if copies:
        activated, slope, w_in = refs[2 + n_pieces :]
        place(meta, pieces, (w_in,), copies)
    else:
        w_in = pieces[0]
        activated, slope, whole = refs[2 + n_pieces :]
        third = x_ref.shape[1]
        for n, ref in enumerate((x_ref, *pieces[1:])):
            whole[:, n * third : (n + 1) * third] = ref[...]
        x_ref = whole
    chunk = 512 if w_in.shape[1] % 512 == 0 else 256

    def rows(ds):
        x = x_ref[ds, :]
        for c in range(0, w_in.shape[1], chunk):
            t = dot(x, w_in[:, c : c + chunk])
            square = t * t
            th = jnp.tanh(t * (GELU_A + (GELU_A * GELU_B) * square))
            phi = 0.5 + 0.5 * th
            activated[ds, c : c + chunk] = (t * phi).astype(BF16)
            inner = GELU_A + (3.0 * GELU_A * GELU_B) * square
            slope[ds, c : c + chunk] = (phi + 0.5 * t * (1.0 - th * th) * inner).astype(BF16)

    rows_loop(x_ref.shape[0], 256, rows)


def product_kernel(plan, n_out, *refs):
    meta, left_own, left_peer, right_own, right_peer = refs[:5]
    outs = refs[5 : 5 + n_out]
    grads = refs[5 + n_out]
    for c in range(0, grads.shape[0], 256):
        part = dot_left(left_own[:, c : c + 256], right_own[...])
        part += dot_left(left_peer[:, c : c + 256], right_peer[...])
        grads[c : c + 256, :] = part.astype(BF16)
    scatter_out(meta, grads, outs, plan)


def contract_kernel(copies, n_pieces, *refs):
    meta, slope_own, slope_peer, low_own, low_peer, w_in = refs[:6]
    pieces = refs[6 : 6 + n_pieces]
    pre_own, pre_peer, part_own, send_left, send_right, w_ffout = refs[6 + n_pieces :]
    half = send_left.shape[1]
    place(meta, pieces, (w_ffout,), copies)
    size = low_own.shape[0]
    chunk = 512 if w_in.shape[1] % 512 == 0 else 256
    for slope, low, grad_pre, part in (
        (slope_peer, low_peer, pre_peer, (send_left, send_right)),
        (slope_own, low_own, pre_own, (part_own,)),
    ):

        def rows(ds, slope=slope, low=low, grad_pre=grad_pre, part=part):
            y = low[ds, :]
            total = None
            for c in range(0, w_in.shape[1], chunk):
                g = dot_right(y, w_ffout[c : c + chunk, :])
                g = (slope[ds, c : c + chunk].astype(F32) * g).astype(BF16)
                grad_pre[ds, c : c + chunk] = g
                t = dot_right(g, w_in[:, c : c + chunk])
                total = t if total is None else total + t
            if len(part) == 2:
                part[0][ds, :] = total[:, :half].astype(BF16)
                part[1][ds, :] = total[:, half:].astype(BF16)
            else:
                part[0][ds, :] = total

        rows_loop(size, 256, rows)


def through_kernel(meta, residual, part, other, other_right, out_cot, pool_cot, gain, w_half, w_other,
                   grad_residual, low_mine, upper, lower, grad_keep, grad_send, grad_gain):
    size, width = residual.shape
    half = width // 2
    core = meta[2]
    mine = pl.ds(pl.multiple_of(core * half, 128), half)
    theirs = pl.ds(pl.multiple_of((1 - core) * half, 128), half)
    length, prefix = meta[4], meta[5]
    count = (length - prefix).astype(F32)
    grad_gain[...] = jnp.zeros_like(grad_gain)

    def rows(ds, low_given, start):
        x = residual[ds, :]
        gn = part[ds, :] + jnp.concatenate([other[ds, :], other_right[ds, :]], axis=1).astype(F32)
        inv = lax.rsqrt(jnp.mean(x * x, axis=-1, keepdims=True) + EPS)
        u = gain[...] * gn
        xr = x * inv
        t = iota((128, 1), 0) + ds.start
        pool = jnp.where((t >= prefix) & (t < length), 1.0, 0.0) / count
        go = out_cot[ds, :].astype(F32) + pool * pool_cot[...]
        g = go + inv * (u - xr * jnp.mean(xr * u, axis=-1, keepdims=True))
        grad_gain[...] += jnp.sum(xr * gn, axis=0, keepdims=True)
        grad_residual[ds, :] = g
        first, second = g[:, :half].astype(BF16), g[:, half:].astype(BF16)
        on_first = jnp.broadcast_to(core == 0, first.shape)
        a = jnp.where(on_first, g[:, :half], g[:, half:]).astype(BF16)
        b = jnp.where(on_first, g[:, half:], g[:, :half]).astype(BF16)
        low_mine[ds, :] = a
        low_given[pl.ds(ds.start - start, 128), :] = b
        grad_keep[ds, :] = (dot_right(a, w_half[mine, :]) + dot_right(b, w_other[mine, :])).astype(BF16)
        grad_send[ds, :] = (dot_right(a, w_half[theirs, :]) + dot_right(b, w_other[theirs, :])).astype(BF16)

    middle = size // 2
    for first, low_given in ((0, upper), (middle, lower)):

        def some(i, carry, first=first, low_given=low_given):
            rows(pl.ds(pl.multiple_of(first + 128 * i, 128), 128), low_given, first)
            return carry

        lax.fori_loop(0, middle // 128, some, 0)


def attend_back_kernel(meta, qkv, powers, g_ref, a_ref, inv_sums, diag_in, out, diag, grads, slant):
    size = g_ref.shape[0]
    part = qkv.shape[1] // 3
    pairs = part // 128
    strips = size // 128
    span = 2 * size
    lane = iota((1, 128), 1)
    half = lane < 64
    diag[...] = diag_in[...]

    def pair(p, carry):
        base = pl.multiple_of(p * 128, 128)
        cols = pl.ds(base, 128)
        kcols = pl.ds(base + part, 128)
        vcols = pl.ds(base + 2 * part, 128)
        qp, kp = qkv[:, cols], qkv[:, kcols]
        vp = qkv[:, vcols].astype(F32)
        do = g_ref[:, cols].astype(F32)
        prod = do * a_ref[:, cols].astype(F32)
        dq_all = None
        for side in range(2):
            head = 2 * p + side
            own = half if side == 0 else jnp.logical_not(half)
            one = 64 if side == 0 else 0
            inv = jnp.sum(jnp.where(lane == head, inv_sums[...], 0.0), axis=1, keepdims=True)
            inner = jnp.sum(jnp.where(own, prod, 0.0), axis=1, keepdims=True) * inv
            upper = inner.astype(BF16).astype(F32)
            dos = jnp.where(
                own,
                do * inv,
                jnp.where(lane == one, -upper, jnp.where(lane == one + 1, upper - inner, 0.0)),
            ).astype(BF16)
            ones = (lane == one) | (lane == one + 1)
            va = jnp.where(own, vp, jnp.where(ones, 1.0, 0.0)).astype(BF16)
            slant[...] = jnp.zeros_like(slant)
            for a in range(strips):
                rows = slice(128 * a, 128 * a + 128)
                off = 128 * (strips - 1 - a)
                e = powers[head, rows, :]
                ds = (e.astype(F32) * dot_right(va[rows], dos)).astype(BF16)
                grads[rows, :] = ds
                slant[:, off : off + size] += ds.astype(F32)
                dk = dot(ds, qp).astype(BF16)
                dv = dot(e, dos).astype(BF16)
                if side == 1:
                    dk = jnp.where(half, out[rows, kcols].astype(F32), dk.astype(F32)).astype(BF16)
                    dv = jnp.where(half, out[rows, vcols].astype(F32), dv.astype(F32)).astype(BF16)
                out[rows, kcols] = dk
                out[rows, vcols] = dv
            dq = dot_left(kp, grads[...]).T
            dq_all = dq if side == 0 else jnp.where(half, dq_all, dq)
            y = slant[...]
            rest = 64
            while rest >= 1:
                y = y[:rest] + pltpu.roll(y[rest:], span - rest, 1)
                rest //= 2
            diag[pl.ds(head, 1), :] += pltpu.roll(y, 127, 1)
        out[:, cols] = dq_all.astype(BF16)
        return carry

    lax.fori_loop(0, pairs, pair, 0)


def weights_kernel(plan, n_out, *refs):
    meta, x_own, x_peer, dqkv_own, dqkv_peer, att_own, upper, lower, att_peer, got_peer, low_own, low_upper, low_lower, small = refs[:14]
    outs = refs[14 : 14 + n_out]
    (grads,) = refs[14 + n_out :]
    middle = upper.shape[0]
    part = dqkv_own.shape[1]
    depth = x_own.shape[1]
    half = depth // 2
    for c in range(0, depth, 256):
        cols = slice(c, c + 256)
        g = dot_left(x_own[:, cols], dqkv_own[...]) + dot_left(x_peer[:, cols], dqkv_peer[...])
        grads[cols, 0:part] = g.astype(BF16)
    core = meta[2]
    mine = pl.multiple_of(core * half, 16)
    theirs = pl.multiple_of((1 - core) * half, 16)
    for c in range(0, half, 128):
        cols = slice(c, c + 128)
        g = dot_left(att_own[:, cols], low_own[...]) + dot_left(att_peer[:middle, cols], low_upper[...])
        g += dot_left(att_peer[middle:, cols], low_lower[...])
        grads[pl.ds(mine + c, 128), part:] = g.astype(BF16)
        g = dot_left(upper[:, cols], low_own[:middle]) + dot_left(lower[:, cols], low_own[middle:])
        g += dot_left(got_peer[:middle, cols], low_upper[...])
        g += dot_left(got_peer[middle:, cols], low_lower[...])
        grads[pl.ds(theirs + c, 128), part:] = g.astype(BF16)
    grads[depth:, :] = jnp.zeros((16, grads.shape[1]), BF16)
    grads[depth:, 0:128] = small[...].astype(BF16)
    scatter_out(meta, grads, outs, plan)


def inputs_kernel(meta, dqkv_own, dqkv_peer, w, hidden, hidden_peer, gain_two, diag, buckets,
                  part_own, left, right, small, gain_one):
    size, width = part_own.shape
    half = width // 2
    small[...] = jnp.zeros_like(small)
    gain_one[...] = jnp.zeros_like(gain_one)

    def share(x_ref, ds, value):
        x = x_ref[ds, :].astype(F32)
        inv = lax.rsqrt(jnp.mean(x * x, axis=-1, keepdims=True) + EPS)
        gain_one[...] += jnp.sum(x * inv * value, axis=0, keepdims=True)

    def peers(ds):
        value = dot_right(dqkv_peer[ds, :], w[...])
        share(hidden_peer, ds, value)
        value = value.astype(BF16)
        left[ds, :] = value[:, :half]
        right[ds, :] = value[:, half:]

    def own(ds):
        value = dot_right(dqkv_own[ds, :], w[...])
        share(hidden, ds, value)
        part_own[ds, :] = value

    rows_loop(size, 256, peers)
    rows_loop(size, 256, own)
    count = width // 128
    for n in range(count):
        small[n : n + 1, :] = gain_one[:, 128 * n : 128 * n + 128]
        small[count + n : count + n + 1, :] = gain_two[:, 128 * n : 128 * n + 128]
    hot = (buckets[...] == iota((128, diag.shape[1]), 0)).astype(F32)
    table = lax.dot_general(
        diag[...],
        hot,
        (((1,), (1,)), ((), ())),
        preferred_element_type=F32,
        precision=lax.Precision.HIGHEST,
    )
    lane = iota((1, 128), 1)
    few = (16 - 2 * count) * 2 - 2
    for n in range(few):
        head = few * meta[2] + n
        row = jnp.where(lane < 32, table[n : n + 1, :], 0.0)
        small[pl.ds(2 * count + head // 4, 1), :] += pltpu.roll(row, 32 * (head % 4), 1)


def hidden_kernel(meta, hidden, grad_residual, part, left, right, gain, grad_hidden):
    def rows(ds):
        total = part[ds, :] + jnp.concatenate([left[ds, :], right[ds, :]], axis=1).astype(F32)
        x = hidden[ds, :].astype(F32)
        inv = lax.rsqrt(jnp.mean(x * x, axis=-1, keepdims=True) + EPS)
        u = gain[...] * total
        xr = x * inv
        grad_hidden[ds, :] = grad_residual[ds, :] + inv * (
            u - xr * jnp.mean(xr * u, axis=-1, keepdims=True)
        )

    rows_loop(hidden.shape[0], 256, rows)


def output_kernel(meta, act_own, act_peer, w_ffout, part_own, left, right):
    size, width = part_own.shape
    half = width // 2

    def peers(ds):
        value = dot(act_peer[ds, :], w_ffout[...]).astype(BF16)
        left[ds, :] = value[:, :half]
        right[ds, :] = value[:, half:]

    def own(ds):
        part_own[ds, :] = dot(act_own[ds, :], w_ffout[...])

    rows_loop(size, 256, peers)
    rows_loop(size, 256, own)


def finish_kernel(meta, residual, part, left, right, sums, hidden_out, pooled, stats):
    size, width = residual.shape
    length, prefix = meta[4], meta[5]
    count = (length - prefix).astype(F32)
    pooled[...] = jnp.zeros_like(pooled)
    stats[...] = jnp.zeros_like(stats)

    def rows(ds):
        branch = part[ds, :] + jnp.concatenate([left[ds, :], right[ds, :]], axis=1).astype(F32)
        out = residual[ds, :] + branch
        hidden_out[ds, :] = out.astype(BF16)
        t = iota((128, 1), 0) + ds.start
        live = t < length
        stats[0:1, :] += jnp.sum(jnp.where(live, branch * branch, 0.0), axis=0, keepdims=True)
        pooled[...] += jnp.sum(jnp.where((t >= prefix) & live, out, 0.0), axis=0, keepdims=True)

    rows_loop(size, 128, rows)
    pooled[...] = pooled[...] / count
    total = jnp.sum(stats[0:1, :])
    first = jnp.sum(sums[0:1, :])
    second = jnp.sum(sums[1:2, :])
    denominator = length.astype(F32) * width
    column = iota(stats.shape, 1)
    values = jnp.where(column == 0, first, jnp.where(column == 1, second, total))
    stats[...] = jnp.sqrt(values / denominator)


def total(*parts):
    value = parts[0].astype(F32)
    for part in parts[1:]:
        value = value + part.astype(F32)
    return value.astype(BF16)


def turn_kernel(meta, keep_a, got_x, keep_b, got_y, on_y, on_x):
    h = on_x.shape[0]
    on_y[...] = total(keep_a[h:], got_x[h:])
    on_x[...] = total(keep_b[h:], got_y[h:])


def add_kernel(meta, a, b, out):
    out[...] = total(a[...], b[...])


def land_half_kernel(meta, keep_a, got_x, last_y, keep_b, got_y, last_x, keep, send):
    h, width = last_x.shape
    upper = total(keep_a[:h], got_x[:h], last_y[:h])
    lower = total(keep_b[:h], got_y[:h], last_x[...])
    first = jnp.broadcast_to(meta[3] % 2 == 0, upper.shape)
    keep[:, :width] = jnp.where(first, upper.astype(F32), lower.astype(F32)).astype(BF16)
    send[:, :width] = jnp.where(first, lower.astype(F32), upper.astype(F32)).astype(BF16)
    if keep.shape[1] > width:
        rows = slice(2 * h, 2 * h + 16)
        small = total(keep_a[rows, 0:128], got_x[rows, 0:128], last_y[h:, 0:128])
        for out in (keep, send):
            out[:, width:] = jnp.zeros((h, 128), BF16)
            out[:16, width:] = small


def halve_kernel(width, meta, a, b, keep, send):
    h = keep.shape[0]
    place_at = pl.multiple_of(h * (meta[3] // 2), 16)
    other_at = pl.multiple_of(h * (1 - meta[3] // 2), 16)
    keep[:, :width] = total(a[pl.ds(place_at, h), :width], b[pl.ds(place_at, h), :width])
    send[:, :width] = total(a[pl.ds(other_at, h), :width], b[pl.ds(other_at, h), :width])
    if width < keep.shape[1]:
        extra = total(a[:h, width:], b[:h, width:])
        keep[:, width:] = extra
        send[:, width:] = extra


def last_kernel(meta, a, b, out, small):
    width = out.shape[1]
    out[...] = total(a[:, :width], b[:, :width])
    small[...] = a[:16, width:].astype(F32) + b[:16, width:].astype(F32)


def join_rows_kernel(meta, own, by_low, by_high, by_both, out):
    h = own.shape[0]
    low, high = meta[3] % 2, meta[3] // 2
    for value, at_low, at_high in (
        (own, low, high),
        (by_low, 1 - low, high),
        (by_high, low, 1 - high),
        (by_both, 1 - low, 1 - high),
    ):
        out[pl.ds(pl.multiple_of(h * (2 * at_low + at_high), 16), h), :] = value[...].astype(F32)


def join_kernel(meta, own, by_low, by_high, by_both, mine, other):
    h = own.shape[0]
    low, high = meta[3] % 2, meta[3] // 2
    for value, at_low, at_high in (
        (own, low, high),
        (by_low, 1 - low, high),
        (by_high, low, 1 - high),
        (by_both, 1 - low, 1 - high),
    ):
        rows = pl.ds(pl.multiple_of(h * at_high, 16), h)

        @pl.when(at_low == meta[2])
        def _(value=value, rows=rows):
            mine[rows, :] = value[...]

        @pl.when(at_low != meta[2])
        def _(value=value, rows=rows):
            other[rows, :] = value[...]


def weave_in_kernel(block, meta, mine, other, out):
    for which, ref in ((meta[2], mine), (1 - meta[2], other)):
        for n in range(ref.shape[1] // block):
            cols = pl.ds(pl.multiple_of((2 * n + which) * block, 128), block)
            out[:, cols] = ref[:, n * block : (n + 1) * block].astype(F32)


def weave_at_kernel(meta, mine, other, *outs):
    half = outs[0].shape[1] // 2
    for which, ref in ((meta[2], mine), (1 - meta[2], other)):
        cols = pl.ds(pl.multiple_of(which * half, 128), half)
        for n, out in enumerate(outs):
            out[:, cols] = ref[:, n * half : (n + 1) * half].astype(F32)


def swap(v, axis, count, far):
    return lax.ppermute(v, axis, [(i, i ^ far) for i in range(count)])


def message_plan(unit):
    h = unit // 2
    plan = []
    for dst, (near, far) in enumerate(((1, 3), (2, 3), (0, 2), (0, 1))):
        offset = 0 if dst in (0, 2) else h
        plan.append((dst, 0, h, unit, near, offset))
        plan.append((dst, h, h, unit, far, offset))
    return plan


class Link:
    def __init__(self, far):
        self.far = far
        self.sent = []

    def send(self, v):
        if len(self.sent) >= 2:
            v = after(v, self.sent[-2])
        got = swap(v, "fsdp", 8, self.far)
        self.sent.append(got)
        return got


def body(
    nf,
    nz,
    hidden_in,
    norm_gain_attn,
    w_query,
    w_key,
    w_value,
    w_out,
    rel_bias,
    norm_gain_ffn,
    w_in,
    w_ffout,
    bucket_index,
    row_lengths,
    prefix_lengths,
    out_cotangent,
    pool_cotangent,
):
    fast = nf == 8 and nz == 4
    size, width = hidden_in.shape
    shard = w_query.shape[0]
    heads = rel_bias.shape[1]
    levels = rel_bias.shape[0] * nf
    full_ff = w_in.shape[1]
    part_ff = full_ff // 2
    block = w_ffout.shape[0]
    half = width // 2
    few = heads // 2
    me = lax.axis_index("fsdp").astype(jnp.int32)
    where = lax.axis_index("dp").astype(jnp.int32)
    core = me & 1
    zero = jnp.zeros((), jnp.int32)

    def by_core(first, second):
        return jnp.where(core == 0, first, second)

    def peer(v):
        return swap(v, "fsdp", nf, 1)

    def dma(n):
        return pltpu.SemaphoreType.DMA((n,))

    def vm(*arrays):
        return [(a, "v") for a in arrays]

    meta = jnp.stack([me, me >> 1, core, where, row_lengths[0], prefix_lengths[0], zero, zero])
    hidden_peer = peer(hidden_in)
    wide = 3 * half
    buckets = jnp.concatenate([bucket_index[::-1], jnp.full((1,), -1, jnp.int32)])[None, :]

    if fast:
        kept_a, given_a, kept_b, given_b, small = call(
            functools.partial(pack_kernel, nf // 2),
            "pack",
            meta,
            [(a, "h") for a in (w_query, w_key, w_value, w_out, w_in)]
            + vm(norm_gain_attn[None], norm_gain_ffn[None], rel_bias),
            [((shard, 4 * half), BF16, "v")] * 2
            + [((shard, part_ff), BF16, "v")] * 2
            + [((8, 128), F32, "v")],
            [pltpu.VMEM(w.shape, BF16) for w in (w_query, w_key, w_value, w_out, w_in)] + [dma(5)],
            limit=56 * 2**20,
        )
        on_x, on_y = Link(2), Link(4)
        taken_a, taken_b = peer(given_a), peer(given_b)
        both_a, both_b = call(
            stack_kernel,
            "stack",
            meta,
            vm(kept_a, taken_a, kept_b, taken_b),
            [((2 * shard, 4 * half), BF16, "v"), ((2 * shard, part_ff), BF16, "v")],
            deps=(hidden_peer,),
            limit=56 * 2**20,
        )

        def near(v):
            return [v, on_x.send(v), on_y.send(v)]

        def distant(three, *deps):
            v, by_x, by_y = three
            h = v.shape[0] // 2
            far_y = on_y.send(after(by_x, *deps)[:h])
            far_x = on_x.send(after(by_y, *deps)[h:])
            return three + [far_y, far_x]

        def rows_of(five):
            h = five[3].shape[0]
            return zip(five, (0, 0, 0, 0, h), (0, 1, 2, 3, 3))

        a_pieces = near(both_a)
        smalls = [small] + [swap(after(small, both_a), "fsdp", nf, far) for far in (2, 4, 6)]
        a_pieces = distant(a_pieces, *smalls)
        (small,) = call(rows_kernel, "rows", meta, vm(*smalls), [((32, 128), F32, "v")])
        smalls = [small, peer(small)]
        a_copies = []
        for number, (piece, row, far) in enumerate(rows_of(a_pieces)):
            rows = piece.shape[0]
            a_copies.append((number, 0, rows, 0, 0, row, 0, wide, 2 * shard, far, 0))
            a_copies.append((number, 0, rows, wide, 1, row, 0, half, 2 * shard, far, 0))
        b_pieces = near(both_b)
    else:

        def whole(v):
            return lax.all_gather(v, "fsdp", axis=0, tiled=True)

        a_full = [whole(w) for w in (w_query, w_key, w_value, w_out)]
        a_full = [by_core(w[:, :half], w[:, half:]) for w in a_full]
        qkv_w, out_half = jnp.concatenate(a_full[:3], axis=1), a_full[3]
        b_full = whole(w_in).reshape(width, nf // 2, 2, block)
        b_pieces = [by_core(b_full[:, :, 0], b_full[:, :, 1]).reshape(width, part_ff)]
        b_copies = [(0, 0, width, 0, 0, 0, 0, part_ff, 0, 0, 0)]
        c_full = whole(w_ffout).reshape(nf // 2, 2, block, width)
        c_pieces = [by_core(c_full[:, 0], c_full[:, 1]).reshape(part_ff, width)]
        c_copies = [(0, 0, part_ff, 0, 0, 0, 0, width, 0, 0, 0)]
        pad = jnp.zeros((1, 128 - shard), BF16)
        rows = [norm_gain_attn[None], norm_gain_ffn[None]]
        rows = [jnp.concatenate([r, pad], axis=1) for r in rows]
        rel = jnp.pad(rel_bias, ((0, 4 - rel_bias.shape[0]), (0, 128 - heads)))
        small = jnp.concatenate(rows + [jnp.zeros((2, 128), BF16), rel], axis=0).astype(F32)
        small = small.at[2].set(row_lengths[0].astype(F32))
        smalls = [whole(small)]

    normed, normed_peer, bias, low, gain_one, gain_two, length_peer = call(
        functools.partial(prepare_kernel, len(smalls), fast, levels),
        "prepare",
        meta,
        vm(hidden_in, hidden_peer, *smalls, buckets, out_cotangent, pool_cotangent),
        [
            ((size, width), BF16, "v"),
            ((size, width), BF16, "v"),
            ((few, 128, 2 * size - 128), F32, "v"),
            ((size, width), BF16, "v"),
            ((1, width), F32, "v"),
            ((1, width), F32, "v"),
            ((1, 128), F32, "v"),
        ],
        [pltpu.VMEM((levels, 128), F32), pltpu.VMEM((128, 2 * size), F32)],
    )
    if fast:
        qkv_w, out_half = call(
            functools.partial(collect_kernel, a_copies, len(a_pieces)),
            "collect",
            meta,
            vm(*a_pieces),
            [((width, wide), BF16, "v"), ((width, half), BF16, "v")],
            deps=(gain_one,),
        )
    out_other = peer(out_half)

    def attend(x, length, name, *deps):
        return call(
            attend_kernel,
            name,
            meta,
            vm(x, bias, qkv_w, length),
            [
                ((size, wide), BF16, "v"),
                ((size, half), BF16, "v"),
                ((size // 2, half), BF16, "v"),
                ((size // 2, half), BF16, "v"),
                ((few, size, size), BF16, "v"),
                ((size, 128), F32, "v"),
            ],
            [pltpu.VMEM((size, size), F32)],
            deps=deps,
        )

    qkv_peer, given_att, *given_halves, powers_peer, sums_peer = attend(
        normed_peer, length_peer, "attend_peer"
    )
    low_peer = peer(after(low, given_att))
    if fast:
        b_pieces = distant(b_pieces, given_att)
        b_copies = [
            (number, 0, piece.shape[0], 0, 0, row, 0, part_ff, 2 * shard, far, 0)
            for number, (piece, row, far) in enumerate(rows_of(b_pieces))
        ]
        c_pieces = near(w_ffout)
    served = tuple(b_pieces[n] for n in (1, 2)) if fast else ()
    length_own = jnp.broadcast_to(row_lengths.astype(F32)[None], (1, 128))
    qkv_own, attended, _, _, powers_own, sums_own = attend(
        normed, length_own, "attend_own", given_att, out_other, *served
    )
    served = tuple(b_pieces[n] for n in (3, 4)) if fast else ()
    got_att = [peer(after(v, attended, *served)) for v in given_halves]
    residual, normed_two, *thirds, sums = call(
        residual_kernel,
        "residual",
        meta,
        vm(hidden_in, attended, *got_att, gain_two, out_half, out_other),
        [((size, width), F32, "v"), ((size, width), BF16, "v")]
        + [((size, width // 3), BF16, "v")] * 3
        + [((8, width), F32, "v")],
        [pltpu.VMEM((width, width), BF16)],
        deps=(low_peer,),
    )
    thirds = [peer(v) for v in thirds]
    shape_in = pltpu.VMEM((width, part_ff), BF16)
    shape_ff = pltpu.VMEM((part_ff, width), BF16)
    if fast:
        ff_plan, in_plan = message_plan(block), message_plan(2 * shard)
        ff_outs = [((block, width), BF16, "v")] * 4
        in_outs = [((2 * shard, part_ff), BF16, "v")] * 4
    else:
        ff_plan = [(0, 0, part_ff, 0, 0, 0)]
        in_plan = [(0, 0, width, 0, 0, 0)]
        ff_outs = [((part_ff, width), BF16, "v")]
        in_outs = [((width, part_ff), BF16, "v")]
    act_own, slope_own, in_w = call(
        functools.partial(expand_kernel, b_copies, len(b_pieces)),
        "expand_own",
        meta,
        vm(normed_two, *b_pieces),
        [((size, part_ff), BF16, "v")] * 2 + [((width, part_ff), BF16, "v")],
        deps=tuple(thirds),
    )
    act_peer, slope_peer, normed_two_peer = call(
        functools.partial(expand_kernel, (), 3),
        "expand_peer",
        meta,
        vm(thirds[0], in_w, *thirds[1:]),
        [((size, part_ff), BF16, "v")] * 2 + [((size, width), BF16, "v")],
    )
    served = tuple(c_pieces[n] for n in (1, 2)) if fast else ()
    if fast:
        c_pieces = distant(c_pieces, act_peer)
        c_copies = [
            (number, 0, piece.shape[0], 0, 0, row, 0, width, block, far, 0)
            for number, (piece, row, far) in enumerate(rows_of(c_pieces))
        ]
    got_att_peer = peer(after(attended, act_peer, *served))
    ff_parts = call(
        functools.partial(product_kernel, ff_plan, len(ff_outs)),
        "product",
        meta,
        vm(act_own, act_peer, low, low_peer),
        ff_outs,
        [shape_ff],
        deps=(got_att_peer,),
    )
    ff_parts = list(ff_parts)
    if fast:
        ff_x = on_x.send(after(ff_parts[0], c_pieces[3], c_pieces[4]))
        ff_y = on_y.send(after(ff_parts[1], c_pieces[3], c_pieces[4]))
    pre_own, pre_peer, part_gn, *send_gn, ff_w = call(
        functools.partial(contract_kernel, c_copies, len(c_pieces)),
        "contract",
        meta,
        vm(slope_own, slope_peer, low, low_peer, in_w, *c_pieces),
        [((size, part_ff), BF16, "v")] * 2
        + [((size, width), F32, "v")]
        + [((size, half), BF16, "v")] * 2
        + [((part_ff, width), BF16, "v")],
        deps=(ff_parts[0],),
    )
    in_parts = call(
        functools.partial(product_kernel, in_plan, len(in_outs)),
        "outer",
        meta,
        vm(normed_two, normed_two_peer, pre_own, pre_peer),
        in_outs,
        [shape_in],
    )
    in_parts = list(in_parts)
    last = in_parts[0]

    def turn(parts, by_x, by_y, *deps):
        h = parts[3].shape[0] // 2
        columns = parts[3].shape[1]
        to_y, to_x = call(
            turn_kernel,
            "turn",
            meta,
            vm(parts[2], by_x, parts[3], by_y),
            [((parts[2].shape[0] - h, columns), BF16, "v"), ((h, columns), BF16, "v")],
            deps=deps,
        )
        return on_y.send(to_y), on_x.send(to_x), to_y

    def add(a, b, *deps):
        (out,) = call(add_kernel, "add", meta, vm(a, b), [(a.shape, BF16, "v")], deps=deps)
        return out

    if fast:
        other_gn = [peer(v) for v in send_gn]
        in_x = on_x.send(after(in_parts[0], ff_x))
        in_y = on_y.send(after(in_parts[1], ff_y))
        last_y, last_x, last = turn(ff_parts, ff_x, ff_y, last)
        ff_last = (last_y, last_x)
    else:
        other_gn = [peer(v) for v in send_gn]
    grad_residual, low_mine, *low_given, grad_keep, grad_send, grad_gain_two = call(
        through_kernel,
        "through",
        meta,
        vm(residual, part_gn, *other_gn, out_cotangent, pool_cotangent, gain_two, out_half, out_other),
        [
            ((size, width), F32, "v"),
            ((size, half), BF16, "v"),
            ((size // 2, half), BF16, "v"),
            ((size // 2, half), BF16, "v"),
            ((size, half), BF16, "v"),
            ((size, half), BF16, "v"),
            ((1, width), F32, "v"),
        ],
        deps=(last,),
    )
    grad_got = peer(grad_send)
    last = grad_gain_two
    head_rows = 8

    def halve_first(parts, by_x, by_y, last_y, last_x, *deps, extra=0):
        rows, columns = parts[3].shape
        keep, send = call(
            land_half_kernel,
            "land",
            meta,
            vm(parts[2], by_x, last_y, parts[3], by_y, last_x),
            [((rows // 2, columns + extra), BF16, "v")] * 2,
            deps=deps,
        )
        return keep, swap(send, "dp", nz, 1)

    def halve_next(keep, got, *deps, extra=0):
        rows, columns = keep.shape
        keep, send = call(
            functools.partial(halve_kernel, columns - extra),
            "halve",
            meta,
            vm(keep, got),
            [((rows // 2, columns), BF16, "v")] * 2,
            deps=deps,
        )
        return keep, swap(send, "dp", nz, 2)

    def quarter(keep, got, *deps):
        own = add(keep, got, *deps)
        return own, swap(own, "dp", nz, 1), swap(own, "dp", nz, 2)

    def quarters(own, by_low, by_high, *deps):
        return own, by_low, by_high, swap(after(by_high, *deps), "dp", nz, 1)

    def shards(four, *deps):
        columns = four[0].shape[1]
        return call(join_kernel, "join", meta, vm(*four), [((shard, columns), BF16, "v")] * 2, deps=deps)

    def attend_back(qkv, powers, g, att, sums, diag, name, *deps):
        return call(
            attend_back_kernel,
            name,
            meta,
            vm(qkv, powers, g, att, sums, diag),
            [((size, wide), BF16, "v"), ((head_rows, 2 * size), F32, "v")],
            [pltpu.VMEM((size, size), BF16), pltpu.VMEM((128, 2 * size), F32)],
            deps=deps,
        )

    diag = jnp.zeros((head_rows, 2 * size), F32)
    dqkv_own, diag = attend_back(
        qkv_own, powers_own, grad_keep, attended, sums_own, diag, "attend_back_own", last
    )
    last = dqkv_own
    if fast:
        last_y, last_x, last = turn(in_parts, in_x, in_y, last)
        in_last = (last_y, last_x)
    dqkv_peer, diag = attend_back(
        qkv_peer, powers_peer, grad_got, given_att, sums_peer, diag, "attend_back_peer", last
    )
    last = diag
    if fast:
        ff_keep, ff_one = halve_first(ff_parts, ff_x, ff_y, *ff_last, last)
        in_keep, in_one = halve_first(in_parts, in_x, in_y, *in_last, ff_keep)
        last = in_keep
        at_plan = message_plan(2 * shard)
        at_plan = at_plan + [(n, 2 * shard, 16, 0, 0, width) for n in (0, 2)]
        at_outs = [((2 * shard + (16 if n in (0, 2) else 0), 4 * half), BF16, "v") for n in range(4)]
    else:
        at_plan = [(0, 0, width + 16, 0, 0, 0)]
        at_outs = [((width + 16, 4 * half), BF16, "v")]
    part_gh, *send_gh, small_grads = call(
        inputs_kernel,
        "inputs",
        meta,
        vm(dqkv_own, dqkv_peer, qkv_w, hidden_in, hidden_peer, grad_gain_two, diag, buckets),
        [((size, width), F32, "v")] + [((size, half), BF16, "v")] * 2 + [((16, 128), F32, "v")],
        [pltpu.VMEM((1, width), F32)],
        deps=(last,),
    )
    low_other = [peer(after(v, part_gh)) for v in low_given]
    other_gh = [peer(v) for v in send_gh]
    at_parts = call(
        functools.partial(weights_kernel, at_plan, len(at_outs)),
        "weights",
        meta,
        vm(
            normed,
            normed_peer,
            dqkv_own,
            dqkv_peer,
            attended,
            *got_att,
            given_att,
            got_att_peer,
            low_mine,
            *low_other,
            small_grads,
        ),
        at_outs,
        [pltpu.VMEM((width + 16, 4 * half), BF16)],
        deps=(part_gh,),
    )
    at_parts = list(at_parts)
    last = at_parts[0]
    if fast:
        at_x = on_x.send(at_parts[0])
        at_y = on_y.send(at_parts[1])
    (grad_hidden,) = call(
        hidden_kernel,
        "hidden",
        meta,
        vm(hidden_in, grad_residual, part_gh, *other_gh, gain_one),
        [((size, width), F32, "v")],
        deps=(last,),
    )
    last = grad_hidden
    if fast:
        ff_keep, ff_two = halve_next(ff_keep, ff_one, last)
        in_keep, in_two = halve_next(in_keep, in_one, ff_keep)
        last = in_keep
    part_branch, *send_branch = call(
        output_kernel,
        "output",
        meta,
        vm(act_own, act_peer, ff_w),
        [((size, width), F32, "v")] + [((size, half), BF16, "v")] * 2,
        deps=(last,),
    )
    last = part_branch

    if fast:
        last_y, last_x, last = turn(at_parts, at_x, at_y, last)
        at_last = (last_y, last_x)
        ff_four = quarter(ff_keep, ff_two, last)
        in_four = quarter(in_keep, in_two, ff_four[0])
        at_keep, at_one = halve_first(at_parts, at_x, at_y, *at_last, in_four[0], extra=128)
        ff_four = quarters(*ff_four, at_keep)
        last = at_keep
        other_branch = [peer(after(v, last)) for v in send_branch]
    else:
        other_branch = [peer(v) for v in send_branch]
    hidden_out, pooled, stats = call(
        finish_kernel,
        "finish",
        meta,
        vm(residual, part_branch, *other_branch, sums),
        [((size, width), BF16, "v"), ((1, width), F32, "v"), ((1, width), F32, "v")],
        deps=(last,),
    )
    last = stats
    if fast:
        at_keep, at_two = halve_next(at_keep, at_one, last, extra=128)
        in_four = quarters(*in_four, at_keep)
        (grad_ffout,) = call(
            join_rows_kernel,
            "join_rows",
            meta,
            vm(*ff_four),
            [((block, width), F32, "v")],
            deps=(at_keep,),
        )
        own_at, small_grads = call(
            last_kernel,
            "last",
            meta,
            vm(at_keep, at_two),
            [((shard // 2, 4 * half), BF16, "v"), ((16, 128), F32, "v")],
            deps=(grad_ffout,),
        )
        at_four = own_at, swap(own_at, "dp", nz, 1), swap(own_at, "dp", nz, 2)
        small_grads = small_grads + peer(small_grads)
        mine_in, other_in = shards(in_four, own_at)
        got_in = peer(other_in)
        at_four = quarters(*at_four, mine_in)
        (grad_in,) = call(
            functools.partial(weave_in_kernel, block),
            "weave_in",
            meta,
            vm(mine_in, got_in),
            [((shard, full_ff), F32, "v")],
        )
        mine_at, other_at = shards(at_four, grad_in)
        got_at = peer(other_at)
        grad_at = call(
            weave_at_kernel, "weave_at", meta, vm(mine_at, got_at), [((shard, width), F32, "v")] * 4
        )
    else:

        def reduced(v):
            v = lax.psum_scatter(v, "fsdp", scatter_dimension=0, tiled=True)
            return lax.psum(v, "dp").astype(F32)

        def spread(v, axis):
            none = jnp.zeros_like(v)
            return by_core(jnp.stack([v, none], axis), jnp.stack([none, v], axis))

        grad_ffout = reduced(
            spread(ff_parts[0].reshape(nf // 2, block, width), 1).reshape(full_ff, width)
        )
        grad_in = reduced(
            spread(in_parts[0].reshape(width, nf // 2, block), 2).reshape(width, full_ff)
        )
        grads = spread(at_parts[0][:width].reshape(width, 4, half), 2).reshape(width, 4 * width)
        grads = reduced(grads)
        grad_at = [grads[:, n * width : (n + 1) * width] for n in range(4)]
        small_grads = lax.psum(small_grads, ("fsdp", "dp"))

    count = width // 128
    rows = levels // nf
    table = small_grads[2 * count :].reshape(-1)[: heads * levels].reshape(heads, levels)
    grad_table = lax.dynamic_slice_in_dim(table, me * rows, rows, 1).T
    gains = small_grads[: 2 * count].reshape(2, width)
    gains = lax.dynamic_slice_in_dim(gains, me * shard, shard, 1)
    return (
        hidden_out,
        pooled,
        grad_hidden,
        gains[0],
        grad_at[0],
        grad_at[1],
        grad_at[2],
        grad_at[3],
        grad_table,
        gains[1],
        grad_in,
        grad_ffout,
        stats[:, :3],
    )


def solution(mesh):
    token = P(("fsdp", "dp"), None)
    weight = P("fsdp", None)
    return jax.shard_map(
        functools.partial(body, mesh.shape["fsdp"], mesh.shape["dp"]),
        mesh=mesh,
        in_specs=(
            token,
            P("fsdp"),
            weight,
            weight,
            weight,
            weight,
            weight,
            P("fsdp"),
            weight,
            weight,
            P(),
            P(("fsdp", "dp")),
            P(("fsdp", "dp")),
            token,
            token,
        ),
        out_specs=(
            token,
            token,
            token,
            P("fsdp"),
            weight,
            weight,
            weight,
            weight,
            weight,
            P("fsdp"),
            weight,
            weight,
            token,
        ),
        check_vma=False,
    )
```

```python
import functools
import math

import jax
import jax.numpy as jnp
from jax import lax
from jax.experimental import pallas as pl
from jax.experimental.pallas import tpu as pltpu
from jax.sharding import PartitionSpec as P

EPS = 1e-06
F32 = jnp.float32
BF16 = jnp.bfloat16
VMEM_SPARE = 6 * 2**20
WEIGHTS = {"turn": 30.0, "expand_own": 30.0}
GELU_A = 0.7978845608028654
GELU_B = 0.044715


def dot(a, b):
    return lax.dot_general(a, b, (((1,), (0,)), ((), ())), preferred_element_type=F32)


def dot_right(a, b):
    return lax.dot_general(a, b, (((1,), (1,)), ((), ())), preferred_element_type=F32)


def dot_left(a, b):
    return lax.dot_general(a, b, (((0,), (0,)), ((), ())), preferred_element_type=F32)


def iota(shape, dim):
    return lax.broadcasted_iota(jnp.int32, shape, dim)


def call(kernel, name, meta, ins, outs, scratch=(), deps=(), limit=0):
    spaces = {"v": pltpu.VMEM, "s": pltpu.SMEM, "h": pl.ANY}
    held = [(a.shape, a.dtype) for a, m in ins if m == "v"]
    held += [(s, d) for s, d, m in outs if m == "v"]
    held += [(x.shape, x.dtype) for x in scratch if x.memory_space == pltpu.VMEM]
    need = sum(math.prod(s) * jnp.dtype(d).itemsize for s, d in held)
    ins = [(after(meta, *deps), "s")] + list(ins)
    return pl.pallas_call(
        kernel,
        name=name,
        out_shape=[jax.ShapeDtypeStruct(s, d) for s, d, _ in outs],
        in_specs=[pl.BlockSpec(memory_space=spaces[m]) for _, m in ins],
        out_specs=[pl.BlockSpec(memory_space=spaces[m]) for _, _, m in outs],
        scratch_shapes=list(scratch),
        compiler_params=pltpu.CompilerParams(vmem_limit_bytes=max(limit, need + VMEM_SPARE)),
        cost_estimate=pl.CostEstimate(
            flops=1000, bytes_accessed=int(3.7e6 * WEIGHTS.get(name, 0.0)) + 1000, transcendentals=0
        ),
    )(*[a for a, _ in ins])


def after(v, *deps):
    return lax.optimization_barrier((v,) + deps)[0] if deps else v


def place(meta, pieces, targets, copies):
    for src, row, rows, from_column, dst, base, column, width, unit, far, side in copies:
        start = base
        if unit:
            start = base + unit * jnp.bitwise_xor(meta[1], far)
            if side == 1:
                start = start + (unit // 2) * meta[2]
            if side == 2:
                start = start + (unit // 2) * (1 - meta[2])
            start = pl.multiple_of(start, 16)
        targets[dst][pl.ds(start, rows), column : column + width] = pieces[src][
            row : row + rows, from_column : from_column + width
        ]


def rows_loop(count, step, fn):
    def one(i, carry):
        fn(pl.ds(pl.multiple_of(i * step, step), step))
        return carry

    lax.fori_loop(0, count // step, one, 0)


def scatter_out(meta, scratch, outs, plan):
    for dst, row, rows, unit, far, offset in plan:
        start = offset
        if unit:
            start = pl.multiple_of(offset + unit * jnp.bitwise_xor(meta[1], far), 16)
        outs[dst][row : row + rows, :] = scratch[pl.ds(start, rows), :]


def small_block(meta, gain_one, gain_two, rel):
    row, lane = iota((16, 128), 0), iota((16, 128), 1)
    block = jnp.where((row == 2) & (lane == 0), (meta[4] // 256).astype(F32), 0.0)
    block = jnp.where((row == 2) & (lane == 1), (meta[4] % 256).astype(F32), block)
    parts = [(0, gain_one), (1, gain_two)] + [(4 + n, rel[n : n + 1, :]) for n in range(rel.shape[0])]
    for at, value in parts:
        value = value[...].astype(F32)
        wide = jnp.concatenate([value, jnp.zeros((1, 128 - value.shape[1]), F32)], axis=1)
        block = jnp.where(row == at, wide, block)
    return block.astype(BF16)


def pack_kernel(n_chips, meta, *refs):
    sources = refs[:5]
    gain_one, gain_two, rel = refs[5:8]
    kept_a, given_a, kept_b, given_b = refs[8:12]
    held, sems = refs[12:17], refs[17]
    handles = [pltpu.make_async_copy(a, b, sems.at[n]) for n, (a, b) in enumerate(zip(sources, held))]
    for handle in handles:
        handle.start()
    width = 4 * (held[0].shape[1] // 2)
    block = small_block(meta, gain_one, gain_two, rel)
    for out in (kept_a, given_a):
        out[:, width:] = jnp.zeros((out.shape[0], 128), BF16)
        out[0:16, width:] = block
    for handle in handles:
        handle.wait()
    wq, wk, wv, wo, w_in = held
    core = meta[2]
    half = wq.shape[1] // 2
    block = w_in.shape[1] // (2 * n_chips)
    for which, a_ref, b_ref in ((core, kept_a, kept_b), (1 - core, given_a, given_b)):
        for n, w in enumerate((wq, wk, wv, wo)):
            cols = pl.ds(pl.multiple_of(which * half, 128), half)
            a_ref[:, n * half : (n + 1) * half] = w[:, cols]
        for n in range(b_ref.shape[1] // block):
            cols = pl.ds(pl.multiple_of((2 * n + which) * block, 128), block)
            b_ref[:, n * block : (n + 1) * block] = w_in[:, cols]


def stack_kernel(meta, kept, taken, both):
    shard = kept.shape[0]
    both[pl.ds(pl.multiple_of(shard * meta[2], 16), shard), :] = kept[...]
    both[pl.ds(pl.multiple_of(shard * (1 - meta[2]), 16), shard), :] = taken[...]


def cut_kernel(meta, by_x, by_y, upper, lower):
    h = upper.shape[0]
    upper[...] = by_x[:h, :]
    lower[...] = by_y[h:, :]


def low_kernel(meta, out_cot, pool_cot, low):
    size = low.shape[0]
    length, prefix = meta[4], meta[5]
    count = (length - prefix).astype(F32)

    def lows(ds):
        t = iota((256, 1), 0) + ds.start
        pool = jnp.where((t >= prefix) & (t < length), 1.0, 0.0) / count
        low[ds, :] = (out_cot[ds, :].astype(F32) + pool * pool_cot[...]).astype(BF16)

    rows_loop(size, 256, lows)


def prepare_kernel(copies, n_pieces, levels, meta, hidden, hidden_peer, buckets, *refs):
    pieces = refs[:n_pieces]
    normed, normed_peer, bias, gain_one, gain_two, length_peer = refs[n_pieces : n_pieces + 6]
    rest = refs[n_pieces + 6 :]
    if copies:
        qkv, w_half, table, table_rows = rest
        place(meta, pieces, (qkv, w_half), copies)
        count = n_pieces
        column = pieces[0].shape[1] - 128
        blocks = [ref[0:16, column:].astype(F32) for ref in pieces]
        places = [jnp.bitwise_xor(meta[0], 2 * (p % 4) + p // 4) for p in range(count)]
    else:
        table, table_rows = rest
        count = pieces[0].shape[0] // 16
        blocks = [pieces[0][16 * p : 16 * p + 16, :].astype(F32) for p in range(count)]
        places = [jnp.int32(p) for p in range(count)]
    size, width = hidden.shape
    shard = width // count
    some = levels // count
    table[...] = jnp.zeros_like(table)
    first = jnp.zeros((1, width), F32)
    second = jnp.zeros((1, width), F32)
    rest = jnp.zeros((1, width - 128), F32)
    peers = jnp.zeros((1, 1), F32)
    for where, piece in zip(places, blocks):
        first += pltpu.roll(jnp.concatenate([piece[0:1], rest], axis=1), shard * where, 1)
        second += pltpu.roll(jnp.concatenate([piece[1:2], rest], axis=1), shard * where, 1)
        length = 256.0 * piece[2:3, 0:1] + piece[2:3, 1:2]
        peers += jnp.where(where == jnp.bitwise_xor(meta[0], 1), length, 0.0)
        for b in range(some):
            table[pl.ds(some * where + b, 1), :] = piece[4 + b : 5 + b]
    length_peer[...] = jnp.broadcast_to(peers, (1, 128))
    gain_one[...] = first
    gain_two[...] = second

    for x_ref, n_ref in ((hidden, normed), (hidden_peer, normed_peer)):

        def rows(ds, x_ref=x_ref, n_ref=n_ref):
            x = x_ref[ds, :].astype(F32)
            inv = lax.rsqrt(jnp.mean(x * x, axis=-1, keepdims=True) + EPS)
            n_ref[ds, :] = (x * inv * gain_one[...]).astype(BF16)

        rows_loop(size, 256, rows)

    span = 2 * size
    hot = (buckets[...] == iota((levels, span), 0)).astype(BF16)
    table_rows[...] = dot_left(table[...].astype(BF16), hot)
    heads, _, wide = bias.shape
    base = heads * meta[2]

    def head(h, carry):
        row = table_rows[pl.ds(base + h, 1), :]
        first = jnp.broadcast_to(pltpu.roll(row, span - 127, 1), (8, span))
        sub = iota((8, span), 0)
        full = first
        for k in range(1, 8):
            full = jnp.where(sub == k, pltpu.roll(first, k, 1), full)
        bias[h, 0:8, :] = full[:, :wide]
        have = 8
        while have < 128:
            more = pltpu.roll(full, have, 1)
            bias[h, have : 2 * have, :] = more[:, :wide]
            full = jnp.concatenate([full, more], axis=0)
            have *= 2
        return carry

    lax.fori_loop(0, heads, head, 0)


def attend_kernel(meta, x_ref, bias, w, length, qkv, out, upper, lower, powers, inv_sums, scores):
    size = x_ref.shape[0]
    part = w.shape[1] // 3
    pairs = part // 128
    lane = iota((1, 128), 1)
    half = lane < 64
    strips = size // 128
    inv_sums[...] = jnp.zeros_like(inv_sums)

    def project(ds):
        for n in range(3):
            cols = slice(n * part, (n + 1) * part)
            qkv[ds, cols] = dot(x_ref[ds, :], w[:, cols]).astype(BF16)

    rows_loop(size, 256, project)
    masked = jnp.where(iota((size, 1), 0).astype(F32) < length[0:1, 0:1], 0.0, -1e30).astype(F32)

    def pair(p, carry):
        base = pl.multiple_of(p * 128, 128)
        qp = qkv[:, pl.ds(base, 128)].astype(F32)
        kp = qkv[:, pl.ds(base + part, 128)].astype(F32)
        vp = qkv[:, pl.ds(base + 2 * part, 128)].astype(F32)
        joined = None
        for side in range(2):
            head = 2 * p + side
            own = half if side == 0 else jnp.logical_not(half)
            spare = lane == (64 if side == 0 else 0)
            qa = jnp.where(own, qp, jnp.where(spare, 1.0, 0.0)).astype(BF16)
            ka = jnp.where(own, kp, jnp.where(spare, masked, 0.0)).astype(BF16)
            va = jnp.where(own, vp, jnp.where(spare, 1.0, 0.0)).astype(BF16)
            top = None
            for a in range(strips):
                rows = slice(128 * a, 128 * a + 128)
                off = 128 * (strips - 1 - a)
                s = dot_right(ka[rows], qa) + bias[head, :, off : off + size]
                scores[rows, :] = s
                peak = jnp.max(s, axis=0, keepdims=True)
                top = peak if top is None else jnp.maximum(top, peak)
            for a in range(strips):
                rows = slice(128 * a, 128 * a + 128)
                powers[head, rows, :] = jnp.exp(scores[rows, :] - top).astype(BF16)
            mixed = dot_left(va, powers[head]).T
            sums = jnp.sum(jnp.where(spare, mixed, 0.0), axis=1, keepdims=True)
            inv = 1.0 / sums
            inv_sums[...] = jnp.where(lane == head, inv, inv_sums[...])
            mixed = mixed * inv
            joined = mixed if side == 0 else jnp.where(half, joined, mixed)
        joined = joined.astype(BF16)
        cols = pl.ds(base, 128)
        out[:, cols] = joined
        upper[:, cols] = joined[: size // 2]
        lower[:, cols] = joined[size // 2 :]
        return carry

    lax.fori_loop(0, pairs, pair, 0)


def residual_kernel(meta, hidden, attended, upper, lower, gain, w_half, w_other, residual, normed, left, middle, right, sums, w_out):
    size, width = hidden.shape
    half = width // 2
    length = meta[4]
    core = meta[2]
    w_out[:, pl.ds(pl.multiple_of(core * half, 128), half)] = w_half[...]
    w_out[:, pl.ds(pl.multiple_of((1 - core) * half, 128), half)] = w_other[...]
    mine = pl.ds(pl.multiple_of(core * half, 128), half)
    other = pl.ds(pl.multiple_of((1 - core) * half, 128), half)
    sums[...] = jnp.zeros_like(sums)

    for first, got in ((0, upper), (size // 2, lower)):
        ds = slice(first, first + size // 2)
        x = hidden[ds, :].astype(F32)
        branch = dot(attended[ds, :], w_out[mine, :]) + dot(got[...], w_out[other, :])
        live = (iota((size // 2, 1), 0) + first) < length
        sums[0:1, :] += jnp.sum(jnp.where(live, x * x, 0.0), axis=0, keepdims=True)
        sums[1:2, :] += jnp.sum(jnp.where(live, branch * branch, 0.0), axis=0, keepdims=True)
        r = x + branch
        residual[ds, :] = r
        inv = lax.rsqrt(jnp.mean(r * r, axis=-1, keepdims=True) + EPS)
        value = (r * inv * gain[...]).astype(BF16)
        normed[ds, :] = value
        third = left.shape[1]
        for n, ref in enumerate((left, middle, right)):
            ref[ds, :] = value[:, n * third : (n + 1) * third]


def expand_kernel(copies, n_pieces, *refs):
    meta, x_ref = refs[:2]
    pieces = refs[2 : 2 + n_pieces]
    if copies:
        activated, slope, w_in = refs[2 + n_pieces :]
        place(meta, pieces, (w_in,), copies)
    else:
        w_in = pieces[0]
        activated, slope, whole = refs[2 + n_pieces :]
        third = x_ref.shape[1]
        for n, ref in enumerate((x_ref, *pieces[1:])):
            whole[:, n * third : (n + 1) * third] = ref[...]
        x_ref = whole
    chunk = 512 if w_in.shape[1] % 512 == 0 else 256

    def rows(ds):
        x = x_ref[ds, :]
        for c in range(0, w_in.shape[1], chunk):
            t = dot(x, w_in[:, c : c + chunk])
            square = t * t
            th = jnp.tanh(t * (GELU_A + (GELU_A * GELU_B) * square))
            phi = 0.5 + 0.5 * th
            activated[ds, c : c + chunk] = (t * phi).astype(BF16)
            inner = GELU_A + (3.0 * GELU_A * GELU_B) * square
            slope[ds, c : c + chunk] = (phi + 0.5 * t * (1.0 - th * th) * inner).astype(BF16)

    rows_loop(x_ref.shape[0], 256, rows)


def product_kernel(plan, n_out, *refs):
    meta, left_own, left_peer, right_own, right_peer = refs[:5]
    outs = refs[5 : 5 + n_out]
    grads = refs[5 + n_out]
    for c in range(0, grads.shape[0], 256):
        part = dot_left(left_own[:, c : c + 256], right_own[...])
        part += dot_left(left_peer[:, c : c + 256], right_peer[...])
        grads[c : c + 256, :] = part.astype(BF16)
    scatter_out(meta, grads, outs, plan)


def contract_kernel(copies, n_pieces, *refs):
    meta, slope_own, slope_peer, low_own, low_peer, w_in = refs[:6]
    pieces = refs[6 : 6 + n_pieces]
    pre_own, pre_peer, part_own, *sends, w_ffout = refs[6 + n_pieces :]
    third = sends[0].shape[1]
    place(meta, pieces, (w_ffout,), copies)
    size = low_own.shape[0]
    chunk = 512 if w_in.shape[1] % 512 == 0 else 256
    for slope, low, grad_pre, part in (
        (slope_peer, low_peer, pre_peer, sends),
        (slope_own, low_own, pre_own, (part_own,)),
    ):

        def rows(ds, slope=slope, low=low, grad_pre=grad_pre, part=part):
            y = low[ds, :]
            total = None
            for c in range(0, w_in.shape[1], chunk):
                g = dot_right(y, w_ffout[c : c + chunk, :])
                g = (slope[ds, c : c + chunk].astype(F32) * g).astype(BF16)
                grad_pre[ds, c : c + chunk] = g
                t = dot_right(g, w_in[:, c : c + chunk])
                total = t if total is None else total + t
            if len(part) > 1:
                for n, ref in enumerate(part):
                    ref[ds, :] = total[:, n * third : (n + 1) * third].astype(BF16)
            else:
                part[0][ds, :] = total

        rows_loop(size, 256, rows)


def through_kernel(meta, residual, part, left, center, right, out_cot, pool_cot, gain, w_half, w_other,
                   grad_residual, low_mine, upper, lower, grad_keep, grad_send, grad_gain):
    size, width = residual.shape
    half = width // 2
    core = meta[2]
    mine = pl.ds(pl.multiple_of(core * half, 128), half)
    theirs = pl.ds(pl.multiple_of((1 - core) * half, 128), half)
    length, prefix = meta[4], meta[5]
    count = (length - prefix).astype(F32)
    grad_gain[...] = jnp.zeros_like(grad_gain)

    def rows(ds, low_given, start):
        x = residual[ds, :]
        gn = part[ds, :] + jnp.concatenate([left[ds, :], center[ds, :], right[ds, :]], axis=1).astype(F32)
        inv = lax.rsqrt(jnp.mean(x * x, axis=-1, keepdims=True) + EPS)
        u = gain[...] * gn
        xr = x * inv
        t = iota((128, 1), 0) + ds.start
        pool = jnp.where((t >= prefix) & (t < length), 1.0, 0.0) / count
        go = out_cot[ds, :].astype(F32) + pool * pool_cot[...]
        g = go + inv * (u - xr * jnp.mean(xr * u, axis=-1, keepdims=True))
        grad_gain[...] += jnp.sum(xr * gn, axis=0, keepdims=True)
        grad_residual[ds, :] = g
        first, second = g[:, :half].astype(BF16), g[:, half:].astype(BF16)
        on_first = jnp.broadcast_to(core == 0, first.shape)
        a = jnp.where(on_first, g[:, :half], g[:, half:]).astype(BF16)
        b = jnp.where(on_first, g[:, half:], g[:, :half]).astype(BF16)
        low_mine[ds, :] = a
        low_given[pl.ds(ds.start - start, 128), :] = b
        grad_keep[ds, :] = (dot_right(a, w_half[mine, :]) + dot_right(b, w_other[mine, :])).astype(BF16)
        grad_send[ds, :] = (dot_right(a, w_half[theirs, :]) + dot_right(b, w_other[theirs, :])).astype(BF16)

    middle = size // 2
    for first, low_given in ((0, upper), (middle, lower)):

        def some(i, carry, first=first, low_given=low_given):
            rows(pl.ds(pl.multiple_of(first + 128 * i, 128), 128), low_given, first)
            return carry

        lax.fori_loop(0, middle // 128, some, 0)


def attend_back_kernel(meta, qkv, powers, g_ref, a_ref, inv_sums, diag_in, out, diag, grads, slant):
    size = g_ref.shape[0]
    part = qkv.shape[1] // 3
    pairs = part // 128
    strips = size // 128
    span = 2 * size
    lane = iota((1, 128), 1)
    half = lane < 64
    diag[...] = diag_in[...]

    def pair(p, carry):
        base = pl.multiple_of(p * 128, 128)
        cols = pl.ds(base, 128)
        kcols = pl.ds(base + part, 128)
        vcols = pl.ds(base + 2 * part, 128)
        qp, kp = qkv[:, cols], qkv[:, kcols]
        vp = qkv[:, vcols].astype(F32)
        do = g_ref[:, cols].astype(F32)
        prod = do * a_ref[:, cols].astype(F32)
        dq_all = None
        for side in range(2):
            head = 2 * p + side
            own = half if side == 0 else jnp.logical_not(half)
            one = 64 if side == 0 else 0
            inv = jnp.sum(jnp.where(lane == head, inv_sums[...], 0.0), axis=1, keepdims=True)
            inner = jnp.sum(jnp.where(own, prod, 0.0), axis=1, keepdims=True) * inv
            upper = inner.astype(BF16).astype(F32)
            dos = jnp.where(
                own,
                do * inv,
                jnp.where(lane == one, -upper, jnp.where(lane == one + 1, upper - inner, 0.0)),
            ).astype(BF16)
            ones = (lane == one) | (lane == one + 1)
            va = jnp.where(own, vp, jnp.where(ones, 1.0, 0.0)).astype(BF16)
            slant[...] = jnp.zeros_like(slant)
            for a in range(strips):
                rows = slice(128 * a, 128 * a + 128)
                off = 128 * (strips - 1 - a)
                e = powers[head, rows, :]
                ds = (e.astype(F32) * dot_right(va[rows], dos)).astype(BF16)
                grads[rows, :] = ds
                slant[:, off : off + size] += ds.astype(F32)
                dk = dot(ds, qp).astype(BF16)
                dv = dot(e, dos).astype(BF16)
                if side == 1:
                    dk = jnp.where(half, out[rows, kcols].astype(F32), dk.astype(F32)).astype(BF16)
                    dv = jnp.where(half, out[rows, vcols].astype(F32), dv.astype(F32)).astype(BF16)
                out[rows, kcols] = dk
                out[rows, vcols] = dv
            dq = dot_left(kp, grads[...]).T
            dq_all = dq if side == 0 else jnp.where(half, dq_all, dq)
            y = slant[...]
            rest = 64
            while rest >= 1:
                y = y[:rest] + pltpu.roll(y[rest:], span - rest, 1)
                rest //= 2
            diag[pl.ds(head, 1), :] += pltpu.roll(y, 127, 1)
        out[:, cols] = dq_all.astype(BF16)
        return carry

    lax.fori_loop(0, pairs, pair, 0)


def weights_kernel(plan, n_out, *refs):
    meta, x_own, x_peer, dqkv_own, dqkv_peer, att_own, upper, lower, att_peer, got_upper, got_lower, low_own, low_upper, low_lower, small = refs[:15]
    outs = refs[15 : 15 + n_out]
    (grads,) = refs[15 + n_out :]
    middle = upper.shape[0]
    part = dqkv_own.shape[1]
    depth = x_own.shape[1]
    half = depth // 2
    for c in range(0, depth, 256):
        cols = slice(c, c + 256)
        g = dot_left(x_own[:, cols], dqkv_own[...]) + dot_left(x_peer[:, cols], dqkv_peer[...])
        grads[cols, 0:part] = g.astype(BF16)
    core = meta[2]
    mine = pl.multiple_of(core * half, 16)
    theirs = pl.multiple_of((1 - core) * half, 16)
    for c in range(0, half, 128):
        cols = slice(c, c + 128)
        g = dot_left(att_own[:, cols], low_own[...]) + dot_left(att_peer[:middle, cols], low_upper[...])
        g += dot_left(att_peer[middle:, cols], low_lower[...])
        grads[pl.ds(mine + c, 128), part:] = g.astype(BF16)
        g = dot_left(upper[:, cols], low_own[:middle]) + dot_left(lower[:, cols], low_own[middle:])
        g += dot_left(got_upper[:, cols], low_upper[...])
        g += dot_left(got_lower[:, cols], low_lower[...])
        grads[pl.ds(theirs + c, 128), part:] = g.astype(BF16)
    grads[depth:, :] = jnp.zeros((16, grads.shape[1]), BF16)
    grads[depth:, 0:128] = small[...].astype(BF16)
    scatter_out(meta, grads, outs, plan)


def inputs_kernel(meta, dqkv_own, dqkv_peer, w, hidden, hidden_peer, gain_two, diag, buckets,
                  part_own, left, right, small, gain_one):
    size, width = part_own.shape
    half = width // 2
    small[...] = jnp.zeros_like(small)
    gain_one[...] = jnp.zeros_like(gain_one)

    def share(x_ref, ds, value):
        x = x_ref[ds, :].astype(F32)
        inv = lax.rsqrt(jnp.mean(x * x, axis=-1, keepdims=True) + EPS)
        gain_one[...] += jnp.sum(x * inv * value, axis=0, keepdims=True)

    def peers(ds):
        value = dot_right(dqkv_peer[ds, :], w[...])
        share(hidden_peer, ds, value)
        value = value.astype(BF16)
        left[ds, :] = value[:, :half]
        right[ds, :] = value[:, half:]

    def own(ds):
        value = dot_right(dqkv_own[ds, :], w[...])
        share(hidden, ds, value)
        part_own[ds, :] = value

    rows_loop(size, 256, peers)
    rows_loop(size, 256, own)
    count = width // 128
    for n in range(count):
        small[n : n + 1, :] = gain_one[:, 128 * n : 128 * n + 128]
        small[count + n : count + n + 1, :] = gain_two[:, 128 * n : 128 * n + 128]
    hot = (buckets[...] == iota((128, diag.shape[1]), 0)).astype(F32)
    table = lax.dot_general(
        diag[...],
        hot,
        (((1,), (1,)), ((), ())),
        preferred_element_type=F32,
        precision=lax.Precision.HIGHEST,
    )
    lane = iota((1, 128), 1)
    few = (16 - 2 * count) * 2 - 2
    for n in range(few):
        head = few * meta[2] + n
        row = jnp.where(lane < 32, table[n : n + 1, :], 0.0)
        small[pl.ds(2 * count + head // 4, 1), :] += pltpu.roll(row, 32 * (head % 4), 1)


def hidden_kernel(meta, hidden, grad_residual, part, left, right, gain, grad_hidden):
    def rows(ds):
        total = part[ds, :] + jnp.concatenate([left[ds, :], right[ds, :]], axis=1).astype(F32)
        x = hidden[ds, :].astype(F32)
        inv = lax.rsqrt(jnp.mean(x * x, axis=-1, keepdims=True) + EPS)
        u = gain[...] * total
        xr = x * inv
        grad_hidden[ds, :] = grad_residual[ds, :] + inv * (
            u - xr * jnp.mean(xr * u, axis=-1, keepdims=True)
        )

    rows_loop(hidden.shape[0], 256, rows)


def output_kernel(meta, act_own, act_peer, w_ffout, part_own, left, right):
    size, width = part_own.shape
    half = width // 2

    def peers(ds):
        value = dot(act_peer[ds, :], w_ffout[...]).astype(BF16)
        left[ds, :] = value[:, :half]
        right[ds, :] = value[:, half:]

    def own(ds):
        part_own[ds, :] = dot(act_own[ds, :], w_ffout[...])

    rows_loop(size, 256, peers)
    rows_loop(size, 256, own)


def finish_kernel(meta, residual, part, left, right, sums, hidden_out, pooled, stats):
    size, width = residual.shape
    length, prefix = meta[4], meta[5]
    count = (length - prefix).astype(F32)
    pooled[...] = jnp.zeros_like(pooled)
    stats[...] = jnp.zeros_like(stats)

    def rows(ds):
        branch = part[ds, :] + jnp.concatenate([left[ds, :], right[ds, :]], axis=1).astype(F32)
        out = residual[ds, :] + branch
        hidden_out[ds, :] = out.astype(BF16)
        t = iota((128, 1), 0) + ds.start
        live = t < length
        stats[0:1, :] += jnp.sum(jnp.where(live, branch * branch, 0.0), axis=0, keepdims=True)
        pooled[...] += jnp.sum(jnp.where((t >= prefix) & live, out, 0.0), axis=0, keepdims=True)

    rows_loop(size, 128, rows)
    pooled[...] = pooled[...] / count
    total = jnp.sum(stats[0:1, :])
    first = jnp.sum(sums[0:1, :])
    second = jnp.sum(sums[1:2, :])
    denominator = length.astype(F32) * width
    column = iota(stats.shape, 1)
    values = jnp.where(column == 0, first, jnp.where(column == 1, second, total))
    stats[...] = jnp.sqrt(values / denominator)


def total(*parts):
    value = parts[0].astype(F32)
    for part in parts[1:]:
        value = value + part.astype(F32)
    return value.astype(BF16)


def turn_kernel(meta, keep_a, got_x, keep_b, got_y, on_y, on_x):
    h = on_x.shape[0]
    on_y[...] = total(keep_a[h:], got_x[h:])
    on_x[...] = total(keep_b[h:], got_y[h:])


def add_kernel(meta, a, b, out):
    out[...] = total(a[...], b[...])


def land_half_kernel(meta, keep_a, got_x, last_y, keep_b, got_y, last_x, keep, send):
    h, width = last_x.shape
    upper = total(keep_a[:h], got_x[:h], last_y[:h])
    lower = total(keep_b[:h], got_y[:h], last_x[...])
    first = jnp.broadcast_to(meta[3] % 2 == 0, upper.shape)
    keep[:, :width] = jnp.where(first, upper.astype(F32), lower.astype(F32)).astype(BF16)
    send[:, :width] = jnp.where(first, lower.astype(F32), upper.astype(F32)).astype(BF16)
    if keep.shape[1] > width:
        rows = slice(2 * h, 2 * h + 16)
        small = total(keep_a[rows, 0:128], got_x[rows, 0:128], last_y[h:, 0:128])
        for out in (keep, send):
            out[:, width:] = jnp.zeros((h, 128), BF16)
            out[:16, width:] = small


def halve_kernel(width, meta, a, b, keep, send):
    h = keep.shape[0]
    place_at = pl.multiple_of(h * (meta[3] // 2), 16)
    other_at = pl.multiple_of(h * (1 - meta[3] // 2), 16)
    keep[:, :width] = total(a[pl.ds(place_at, h), :width], b[pl.ds(place_at, h), :width])
    send[:, :width] = total(a[pl.ds(other_at, h), :width], b[pl.ds(other_at, h), :width])
    if width < keep.shape[1]:
        extra = total(a[:h, width:], b[:h, width:])
        keep[:, width:] = extra
        send[:, width:] = extra


def last_kernel(meta, a, b, out, small):
    width = out.shape[1]
    out[...] = total(a[:, :width], b[:, :width])
    small[...] = a[:16, width:].astype(F32) + b[:16, width:].astype(F32)


def join_rows_kernel(meta, own, by_low, by_high, by_both, out):
    h = own.shape[0]
    low, high = meta[3] % 2, meta[3] // 2
    for value, at_low, at_high in (
        (own, low, high),
        (by_low, 1 - low, high),
        (by_high, low, 1 - high),
        (by_both, 1 - low, 1 - high),
    ):
        out[pl.ds(pl.multiple_of(h * (2 * at_low + at_high), 16), h), :] = value[...].astype(F32)


def join_kernel(meta, own, by_low, by_high, by_both, mine, other):
    h = own.shape[0]
    low, high = meta[3] % 2, meta[3] // 2
    for value, at_low, at_high in (
        (own, low, high),
        (by_low, 1 - low, high),
        (by_high, low, 1 - high),
        (by_both, 1 - low, 1 - high),
    ):
        rows = pl.ds(pl.multiple_of(h * at_high, 16), h)

        @pl.when(at_low == meta[2])
        def _(value=value, rows=rows):
            mine[rows, :] = value[...]

        @pl.when(at_low != meta[2])
        def _(value=value, rows=rows):
            other[rows, :] = value[...]


def weave_in_kernel(block, meta, mine, other, out):
    for which, ref in ((meta[2], mine), (1 - meta[2], other)):
        for n in range(ref.shape[1] // block):
            cols = pl.ds(pl.multiple_of((2 * n + which) * block, 128), block)
            out[:, cols] = ref[:, n * block : (n + 1) * block].astype(F32)


def weave_at_kernel(meta, mine, other, *outs):
    half = outs[0].shape[1] // 2
    for which, ref in ((meta[2], mine), (1 - meta[2], other)):
        cols = pl.ds(pl.multiple_of(which * half, 128), half)
        for n, out in enumerate(outs):
            out[:, cols] = ref[:, n * half : (n + 1) * half].astype(F32)


def swap(v, axis, count, far):
    return lax.ppermute(v, axis, [(i, i ^ far) for i in range(count)])


def message_plan(unit):
    h = unit // 2
    plan = []
    for dst, (near, far) in enumerate(((1, 3), (2, 3), (0, 2), (0, 1))):
        offset = 0 if dst in (0, 2) else h
        plan.append((dst, 0, h, unit, near, offset))
        plan.append((dst, h, h, unit, far, offset))
    return plan


class Link:
    def __init__(self, far):
        self.far = far
        self.sent = []

    def send(self, v):
        if len(self.sent) >= 2:
            v = after(v, self.sent[-2])
        got = swap(v, "fsdp", 8, self.far)
        self.sent.append(got)
        return got


def body(
    nf,
    nz,
    hidden_in,
    norm_gain_attn,
    w_query,
    w_key,
    w_value,
    w_out,
    rel_bias,
    norm_gain_ffn,
    w_in,
    w_ffout,
    bucket_index,
    row_lengths,
    prefix_lengths,
    out_cotangent,
    pool_cotangent,
):
    fast = nf == 8 and nz == 4
    size, width = hidden_in.shape
    shard = w_query.shape[0]
    heads = rel_bias.shape[1]
    levels = rel_bias.shape[0] * nf
    full_ff = w_in.shape[1]
    part_ff = full_ff // 2
    block = w_ffout.shape[0]
    half = width // 2
    few = heads // 2
    me = lax.axis_index("fsdp").astype(jnp.int32)
    where = lax.axis_index("dp").astype(jnp.int32)
    core = me & 1
    zero = jnp.zeros((), jnp.int32)

    def by_core(first, second):
        return jnp.where(core == 0, first, second)

    def peer(v):
        return swap(v, "fsdp", nf, 1)

    def dma(n):
        return pltpu.SemaphoreType.DMA((n,))

    def vm(*arrays):
        return [(a, "v") for a in arrays]

    meta = jnp.stack([me, me >> 1, core, where, row_lengths[0], prefix_lengths[0], zero, zero])
    hidden_peer = peer(hidden_in)
    wide = 3 * half
    buckets = jnp.concatenate([bucket_index[::-1], jnp.full((1,), -1, jnp.int32)])[None, :]

    if fast:
        kept_a, given_a, kept_b, given_b = call(
            functools.partial(pack_kernel, nf // 2),
            "pack",
            meta,
            [(a, "h") for a in (w_query, w_key, w_value, w_out, w_in)]
            + vm(norm_gain_attn[None], norm_gain_ffn[None], rel_bias),
            [((shard, 4 * half + 128), BF16, "v")] * 2 + [((shard, part_ff), BF16, "v")] * 2,
            [pltpu.VMEM(w.shape, BF16) for w in (w_query, w_key, w_value, w_out, w_in)] + [dma(5)],
            limit=56 * 2**20,
        )
        on_x, on_y = Link(2), Link(4)
        taken_a = peer(given_a)
        x_kept, y_taken = on_x.send(kept_a), on_y.send(taken_a)
        x_taken, y_kept = on_x.send(taken_a), on_y.send(kept_a)
        far_kept, far_taken = on_y.send(x_kept), on_x.send(y_taken)
        a_pieces = [kept_a, x_kept, y_kept, far_kept, taken_a, x_taken, y_taken, far_taken]
        a_copies = []
        for number in range(8):
            far, side = number % 4, 1 + number // 4
            a_copies.append((number, 0, shard, 0, 0, 0, 0, wide, 2 * shard, far, side))
            a_copies.append((number, 0, shard, wide, 1, 0, 0, half, 2 * shard, far, side))
        taken_b = peer(after(given_b, hidden_peer, taken_a))
        (both_b,) = call(
            stack_kernel,
            "stack",
            meta,
            vm(kept_b, taken_b),
            [((2 * shard, part_ff), BF16, "v")],
        )

        def near(v):
            return [v, on_x.send(v), on_y.send(v)]

        def distant(three, *deps):
            v, by_x, by_y = three
            h = v.shape[0] // 2
            upper, lower = call(
                cut_kernel, "cut", meta, vm(by_x, by_y), [((h, v.shape[1]), BF16, "v")] * 2, deps=deps
            )
            far_y, far_x = on_y.send(upper), on_x.send(lower)
            return three + [far_y, far_x]

        def rows_of(five):
            h = five[3].shape[0]
            return zip(five, (0, 0, 0, 0, h), (0, 1, 2, 3, 3))

    else:

        def whole(v):
            return lax.all_gather(v, "fsdp", axis=0, tiled=True)

        a_full = [whole(w) for w in (w_query, w_key, w_value, w_out)]
        a_full = [by_core(w[:, :half], w[:, half:]) for w in a_full]
        qkv_w, out_half = jnp.concatenate(a_full[:3], axis=1), a_full[3]
        b_full = whole(w_in).reshape(width, nf // 2, 2, block)
        b_pieces = [by_core(b_full[:, :, 0], b_full[:, :, 1]).reshape(width, part_ff)]
        b_copies = [(0, 0, width, 0, 0, 0, 0, part_ff, 0, 0, 0)]
        c_full = whole(w_ffout).reshape(nf // 2, 2, block, width)
        c_pieces = [by_core(c_full[:, 0], c_full[:, 1]).reshape(part_ff, width)]
        c_copies = [(0, 0, part_ff, 0, 0, 0, 0, width, 0, 0, 0)]
        length = row_lengths[0]
        split = jnp.stack([length // 256, length % 256]).astype(BF16)[None]
        rows = [norm_gain_attn[None], norm_gain_ffn[None], split, split, rel_bias]
        rows = [jnp.pad(r, ((0, 0), (0, 128 - r.shape[1]))) for r in rows]
        small = jnp.concatenate(rows, axis=0)
        a_pieces, a_copies = [whole(jnp.pad(small, ((0, 16 - small.shape[0]), (0, 0))))], ()

    (low,) = call(
        low_kernel, "low", meta, vm(out_cotangent, pool_cotangent), [((size, width), BF16, "v")]
    )
    normed, normed_peer, bias, gain_one, gain_two, length_peer, *weights = call(
        functools.partial(prepare_kernel, a_copies, len(a_pieces), levels),
        "prepare",
        meta,
        vm(hidden_in, hidden_peer, buckets, *a_pieces),
        [
            ((size, width), BF16, "v"),
            ((size, width), BF16, "v"),
            ((few, 128, 2 * size - 128), F32, "v"),
            ((1, width), F32, "v"),
            ((1, width), F32, "v"),
            ((1, 128), F32, "v"),
        ]
        + ([((width, wide), BF16, "v"), ((width, half), BF16, "v")] if fast else []),
        [pltpu.VMEM((levels, 128), F32), pltpu.VMEM((128, 2 * size), F32)],
        deps=(low,),
    )
    if fast:
        b_pieces = near(both_b)
        qkv_w, out_half = weights
    out_other = peer(out_half)

    def attend(x, length, name, *deps):
        return call(
            attend_kernel,
            name,
            meta,
            vm(x, bias, qkv_w, length),
            [
                ((size, wide), BF16, "v"),
                ((size, half), BF16, "v"),
                ((size // 2, half), BF16, "v"),
                ((size // 2, half), BF16, "v"),
                ((few, size, size), BF16, "v"),
                ((size, 128), F32, "v"),
            ],
            [pltpu.VMEM((size, size), F32)],
            deps=deps,
        )

    qkv_peer, given_att, *given_halves, powers_peer, sums_peer = attend(
        normed_peer, length_peer, "attend_peer"
    )
    low_peer = peer(after(low, given_att))
    if fast:
        b_pieces = distant(b_pieces, given_att)
        b_copies = [
            (number, 0, piece.shape[0], 0, 0, row, 0, part_ff, 2 * shard, far, 0)
            for number, (piece, row, far) in enumerate(rows_of(b_pieces))
        ]
        c_pieces = near(w_ffout)
    served = tuple(b_pieces[n] for n in (1, 2)) if fast else ()
    length_own = jnp.broadcast_to(row_lengths.astype(F32)[None], (1, 128))
    qkv_own, attended, *own_halves, powers_own, sums_own = attend(
        normed, length_own, "attend_own", given_att, out_other, *served
    )
    served = tuple(b_pieces[n] for n in (3, 4)) if fast else ()
    got_att = [peer(after(v, attended, *served)) for v in given_halves]
    residual, normed_two, *thirds, sums = call(
        residual_kernel,
        "residual",
        meta,
        vm(hidden_in, attended, *got_att, gain_two, out_half, out_other),
        [((size, width), F32, "v"), ((size, width), BF16, "v")]
        + [((size, width // 3), BF16, "v")] * 3
        + [((8, width), F32, "v")],
        [pltpu.VMEM((width, width), BF16)],
        deps=(low_peer,),
    )
    thirds = [peer(v) for v in thirds]
    shape_in = pltpu.VMEM((width, part_ff), BF16)
    shape_ff = pltpu.VMEM((part_ff, width), BF16)
    if fast:
        ff_plan, in_plan = message_plan(block), message_plan(2 * shard)
        ff_outs = [((block, width), BF16, "v")] * 4
        in_outs = [((2 * shard, part_ff), BF16, "v")] * 4
    else:
        ff_plan = [(0, 0, part_ff, 0, 0, 0)]
        in_plan = [(0, 0, width, 0, 0, 0)]
        ff_outs = [((part_ff, width), BF16, "v")]
        in_outs = [((width, part_ff), BF16, "v")]
    act_own, slope_own, in_w = call(
        functools.partial(expand_kernel, b_copies, len(b_pieces)),
        "expand_own",
        meta,
        vm(normed_two, *b_pieces),
        [((size, part_ff), BF16, "v")] * 2 + [((width, part_ff), BF16, "v")],
        deps=tuple(thirds),
    )
    if fast:
        c_pieces = distant(c_pieces, act_own)
        c_copies = [
            (number, 0, piece.shape[0], 0, 0, row, 0, width, block, far, 0)
            for number, (piece, row, far) in enumerate(rows_of(c_pieces))
        ]
    act_peer, slope_peer, normed_two_peer = call(
        functools.partial(expand_kernel, (), 3),
        "expand_peer",
        meta,
        vm(thirds[0], in_w, *thirds[1:]),
        [((size, part_ff), BF16, "v")] * 2 + [((size, width), BF16, "v")],
        deps=tuple(c_pieces[n] for n in (1, 2)) if fast else (),
    )
    ff_parts = call(
        functools.partial(product_kernel, ff_plan, len(ff_outs)),
        "product",
        meta,
        vm(act_own, act_peer, low, low_peer),
        ff_outs,
        [shape_ff],
    )
    ff_parts = list(ff_parts)
    if fast:
        ff_x = on_x.send(after(ff_parts[0], c_pieces[3], c_pieces[4]))
        ff_y = on_y.send(after(ff_parts[1], c_pieces[3], c_pieces[4]))
    pre_own, pre_peer, part_gn, *send_gn, ff_w = call(
        functools.partial(contract_kernel, c_copies, len(c_pieces)),
        "contract",
        meta,
        vm(slope_own, slope_peer, low, low_peer, in_w, *c_pieces),
        [((size, part_ff), BF16, "v")] * 2
        + [((size, width), F32, "v")]
        + [((size, width // 3), BF16, "v")] * 3
        + [((part_ff, width), BF16, "v")],
        deps=(ff_parts[0],),
    )
    in_parts = call(
        functools.partial(product_kernel, in_plan, len(in_outs)),
        "outer",
        meta,
        vm(normed_two, normed_two_peer, pre_own, pre_peer),
        in_outs,
        [shape_in],
    )
    in_parts = list(in_parts)
    last = in_parts[0]

    def turn(parts, by_x, by_y, *deps):
        h = parts[3].shape[0] // 2
        columns = parts[3].shape[1]
        to_y, to_x = call(
            turn_kernel,
            "turn",
            meta,
            vm(parts[2], by_x, parts[3], by_y),
            [((parts[2].shape[0] - h, columns), BF16, "v"), ((h, columns), BF16, "v")],
            deps=deps,
        )
        return on_y.send(to_y), on_x.send(to_x), to_y

    def add(a, b, *deps):
        (out,) = call(add_kernel, "add", meta, vm(a, b), [(a.shape, BF16, "v")], deps=deps)
        return out

    other_gn = [peer(v) for v in send_gn]
    grad_residual, low_mine, *low_given, grad_keep, grad_send, grad_gain_two = call(
        through_kernel,
        "through",
        meta,
        vm(residual, part_gn, *other_gn, out_cotangent, pool_cotangent, gain_two, out_half, out_other),
        [
            ((size, width), F32, "v"),
            ((size, half), BF16, "v"),
            ((size // 2, half), BF16, "v"),
            ((size // 2, half), BF16, "v"),
            ((size, half), BF16, "v"),
            ((size, half), BF16, "v"),
            ((1, width), F32, "v"),
        ],
        deps=(last,),
    )
    grad_got = peer(grad_send)
    last = grad_gain_two
    if fast:
        last_y, last_x, last = turn(ff_parts, ff_x, ff_y, last)
        ff_last = (last_y, last_x)
    head_rows = 8

    def halve_first(parts, by_x, by_y, last_y, last_x, *deps, extra=0):
        rows, columns = parts[3].shape
        keep, send = call(
            land_half_kernel,
            "land",
            meta,
            vm(parts[2], by_x, last_y, parts[3], by_y, last_x),
            [((rows // 2, columns + extra), BF16, "v")] * 2,
            deps=deps,
        )
        return keep, swap(send, "dp", nz, 1)

    def halve_next(keep, got, *deps, extra=0):
        rows, columns = keep.shape
        keep, send = call(
            functools.partial(halve_kernel, columns - extra),
            "halve",
            meta,
            vm(keep, got),
            [((rows // 2, columns), BF16, "v")] * 2,
            deps=deps,
        )
        return keep, swap(send, "dp", nz, 2)

    def quarter(keep, got, *deps):
        own = add(keep, got, *deps)
        return own, swap(own, "dp", nz, 1), swap(own, "dp", nz, 2)

    def quarters(own, by_low, by_high, *deps):
        return own, by_low, by_high, swap(after(by_high, *deps), "dp", nz, 1)

    def shards(four, *deps):
        columns = four[0].shape[1]
        return call(join_kernel, "join", meta, vm(*four), [((shard, columns), BF16, "v")] * 2, deps=deps)

    def attend_back(qkv, powers, g, att, sums, diag, name, *deps):
        return call(
            attend_back_kernel,
            name,
            meta,
            vm(qkv, powers, g, att, sums, diag),
            [((size, wide), BF16, "v"), ((head_rows, 2 * size), F32, "v")],
            [pltpu.VMEM((size, size), BF16), pltpu.VMEM((128, 2 * size), F32)],
            deps=deps,
        )

    diag = jnp.zeros((head_rows, 2 * size), F32)
    dqkv_own, diag = attend_back(
        qkv_own, powers_own, grad_keep, attended, sums_own, diag, "attend_back_own", last, grad_got
    )
    last = dqkv_own
    if fast:
        ff_keep, ff_one = halve_first(ff_parts, ff_x, ff_y, *ff_last, last)
        in_x = on_x.send(after(in_parts[0], dqkv_own))
        in_y = on_y.send(after(in_parts[1], dqkv_own))
        last = ff_keep
    dqkv_peer, diag = attend_back(
        qkv_peer, powers_peer, grad_got, given_att, sums_peer, diag, "attend_back_peer", last
    )
    last = diag
    if fast:
        ff_keep, ff_two = halve_next(ff_keep, ff_one, last)
        last = ff_keep
    got_att_peer = [peer(after(v, last)) for v in own_halves]
    if fast:
        at_plan = message_plan(2 * shard)
        at_plan = at_plan + [(n, 2 * shard, 16, 0, 0, width) for n in (0, 2)]
        at_outs = [((2 * shard + (16 if n in (0, 2) else 0), 4 * half), BF16, "v") for n in range(4)]
    else:
        at_plan = [(0, 0, width + 16, 0, 0, 0)]
        at_outs = [((width + 16, 4 * half), BF16, "v")]
    part_gh, *send_gh, small_grads = call(
        inputs_kernel,
        "inputs",
        meta,
        vm(dqkv_own, dqkv_peer, qkv_w, hidden_in, hidden_peer, grad_gain_two, diag, buckets),
        [((size, width), F32, "v")] + [((size, half), BF16, "v")] * 2 + [((16, 128), F32, "v")],
        [pltpu.VMEM((1, width), F32)],
        deps=(last,),
    )
    low_other = [peer(after(v, part_gh, *got_att_peer)) for v in low_given]
    last = part_gh
    if fast:
        last_y, last_x, last = turn(in_parts, in_x, in_y, last)
        in_last = (last_y, last_x)
    at_parts = call(
        functools.partial(weights_kernel, at_plan, len(at_outs)),
        "weights",
        meta,
        vm(
            normed,
            normed_peer,
            dqkv_own,
            dqkv_peer,
            attended,
            *got_att,
            given_att,
            *got_att_peer,
            low_mine,
            *low_other,
            small_grads,
        ),
        at_outs,
        [pltpu.VMEM((width + 16, 4 * half), BF16)],
        deps=(last,),
    )
    at_parts = list(at_parts)
    last = at_parts[0]
    if fast:
        at_x = on_x.send(at_parts[0])
        at_y = on_y.send(at_parts[1])
        in_keep, in_one = halve_first(in_parts, in_x, in_y, *in_last, last)
        ff_four = quarter(ff_keep, ff_two, in_keep)
        last = ff_four[0]
    other_gh = [peer(after(v, last)) for v in send_gh]
    part_branch, *send_branch = call(
        output_kernel,
        "output",
        meta,
        vm(act_own, act_peer, ff_w),
        [((size, width), F32, "v")] + [((size, half), BF16, "v")] * 2,
        deps=(last,),
    )
    last = part_branch
    (grad_hidden,) = call(
        hidden_kernel,
        "hidden",
        meta,
        vm(hidden_in, grad_residual, part_gh, *other_gh, gain_one),
        [((size, width), F32, "v")],
        deps=(last,),
    )
    last = grad_hidden

    if fast:
        in_keep, in_two = halve_next(in_keep, in_one, last)
        last_y, last_x, last = turn(at_parts, at_x, at_y, in_keep)
        at_last = (last_y, last_x)
        ff_four = quarters(*ff_four, last)
        (grad_ffout,) = call(
            join_rows_kernel,
            "join_rows",
            meta,
            vm(*ff_four),
            [((block, width), F32, "v")],
            deps=(last,),
        )
        at_keep, at_one = halve_first(at_parts, at_x, at_y, *at_last, grad_ffout, extra=128)
        in_four = quarter(in_keep, in_two, at_keep)
        last = in_four[0]
        other_branch = [peer(after(v, last)) for v in send_branch]
    else:
        other_branch = [peer(v) for v in send_branch]
    hidden_out, pooled, stats = call(
        finish_kernel,
        "finish",
        meta,
        vm(residual, part_branch, *other_branch, sums),
        [((size, width), BF16, "v"), ((1, width), F32, "v"), ((1, width), F32, "v")],
        deps=(last,),
    )
    last = stats
    if fast:
        at_keep, at_two = halve_next(at_keep, at_one, last, extra=128)
        in_four = quarters(*in_four, at_keep)
        mine_in, other_in = shards(in_four, at_keep)
        got_in = peer(other_in)
        own_at, small_grads = call(
            last_kernel,
            "last",
            meta,
            vm(at_keep, at_two),
            [((shard // 2, 4 * half), BF16, "v"), ((16, 128), F32, "v")],
            deps=(mine_in,),
        )
        at_four = own_at, swap(own_at, "dp", nz, 1), swap(own_at, "dp", nz, 2)
        small_grads = small_grads + peer(small_grads)
        (grad_in,) = call(
            functools.partial(weave_in_kernel, block),
            "weave_in",
            meta,
            vm(mine_in, got_in),
            [((shard, full_ff), F32, "v")],
            deps=(own_at,),
        )
        at_four = quarters(*at_four, grad_in)
        mine_at, other_at = shards(at_four, small_grads)
        got_at = peer(other_at)
        grad_at = call(
            weave_at_kernel, "weave_at", meta, vm(mine_at, got_at), [((shard, width), F32, "v")] * 4
        )
    else:

        def reduced(v):
            v = lax.psum_scatter(v, "fsdp", scatter_dimension=0, tiled=True)
            return lax.psum(v, "dp").astype(F32)

        def spread(v, axis):
            none = jnp.zeros_like(v)
            return by_core(jnp.stack([v, none], axis), jnp.stack([none, v], axis))

        grad_ffout = reduced(
            spread(ff_parts[0].reshape(nf // 2, block, width), 1).reshape(full_ff, width)
        )
        grad_in = reduced(
            spread(in_parts[0].reshape(width, nf // 2, block), 2).reshape(width, full_ff)
        )
        grads = spread(at_parts[0][:width].reshape(width, 4, half), 2).reshape(width, 4 * width)
        grads = reduced(grads)
        grad_at = [grads[:, n * width : (n + 1) * width] for n in range(4)]
        small_grads = lax.psum(small_grads, ("fsdp", "dp"))

    count = width // 128
    rows = levels // nf
    table = small_grads[2 * count :].reshape(-1)[: heads * levels].reshape(heads, levels)
    grad_table = lax.dynamic_slice_in_dim(table, me * rows, rows, 1).T
    gains = small_grads[: 2 * count].reshape(2, width)
    gains = lax.dynamic_slice_in_dim(gains, me * shard, shard, 1)
    return (
        hidden_out,
        pooled,
        grad_hidden,
        gains[0],
        grad_at[0],
        grad_at[1],
        grad_at[2],
        grad_at[3],
        grad_table,
        gains[1],
        grad_in,
        grad_ffout,
        stats[:, :3],
    )


def solution(mesh):
    token = P(("fsdp", "dp"), None)
    weight = P("fsdp", None)
    return jax.shard_map(
        functools.partial(body, mesh.shape["fsdp"], mesh.shape["dp"]),
        mesh=mesh,
        in_specs=(
            token,
            P("fsdp"),
            weight,
            weight,
            weight,
            weight,
            weight,
            P("fsdp"),
            weight,
            weight,
            P(),
            P(("fsdp", "dp")),
            P(("fsdp", "dp")),
            token,
            token,
        ),
        out_specs=(
            token,
            token,
            token,
            P("fsdp"),
            weight,
            weight,
            weight,
            weight,
            weight,
            P("fsdp"),
            weight,
            weight,
            token,
        ),
        check_vma=False,
    )
```

```python
import functools
import math

import jax
import jax.numpy as jnp
from jax import lax
from jax.experimental import pallas as pl
from jax.experimental.pallas import tpu as pltpu
from jax.sharding import PartitionSpec as P

EPS = 1e-06
F32 = jnp.float32
BF16 = jnp.bfloat16
VMEM_SPARE = 6 * 2**20
WEIGHTS = {"turn": 30.0, "expand_own": 30.0}
GELU_A = 0.7978845608028654
GELU_B = 0.044715


def dot(a, b):
    return lax.dot_general(a, b, (((1,), (0,)), ((), ())), preferred_element_type=F32)


def dot_right(a, b):
    return lax.dot_general(a, b, (((1,), (1,)), ((), ())), preferred_element_type=F32)


def dot_left(a, b):
    return lax.dot_general(a, b, (((0,), (0,)), ((), ())), preferred_element_type=F32)


def iota(shape, dim):
    return lax.broadcasted_iota(jnp.int32, shape, dim)


def call(kernel, name, meta, ins, outs, scratch=(), deps=(), limit=0):
    spaces = {"v": pltpu.VMEM, "s": pltpu.SMEM, "h": pl.ANY}
    held = [(a.shape, a.dtype) for a, m in ins if m == "v"]
    held += [(s, d) for s, d, m in outs if m == "v"]
    held += [(x.shape, x.dtype) for x in scratch if x.memory_space == pltpu.VMEM]
    need = sum(math.prod(s) * jnp.dtype(d).itemsize for s, d in held)
    ins = [(after(meta, *deps), "s")] + list(ins)
    return pl.pallas_call(
        kernel,
        name=name,
        out_shape=[jax.ShapeDtypeStruct(s, d) for s, d, _ in outs],
        in_specs=[pl.BlockSpec(memory_space=spaces[m]) for _, m in ins],
        out_specs=[pl.BlockSpec(memory_space=spaces[m]) for _, _, m in outs],
        scratch_shapes=list(scratch),
        compiler_params=pltpu.CompilerParams(vmem_limit_bytes=max(limit, need + VMEM_SPARE)),
        cost_estimate=pl.CostEstimate(
            flops=1000, bytes_accessed=int(3.7e6 * WEIGHTS.get(name, 0.0)) + 1000, transcendentals=0
        ),
    )(*[a for a, _ in ins])


def after(v, *deps):
    return lax.optimization_barrier((v,) + deps)[0] if deps else v


def place(meta, pieces, targets, copies):
    for src, row, rows, from_column, dst, base, column, width, unit, far, side in copies:
        start = base
        if unit:
            start = base + unit * jnp.bitwise_xor(meta[1], far)
            if side == 1:
                start = start + (unit // 2) * meta[2]
            if side == 2:
                start = start + (unit // 2) * (1 - meta[2])
            start = pl.multiple_of(start, 16)
        targets[dst][pl.ds(start, rows), column : column + width] = pieces[src][
            row : row + rows, from_column : from_column + width
        ]


def rows_loop(count, step, fn):
    def one(i, carry):
        fn(pl.ds(pl.multiple_of(i * step, step), step))
        return carry

    lax.fori_loop(0, count // step, one, 0)


def scatter_out(meta, scratch, outs, plan):
    for dst, row, rows, unit, far, offset in plan:
        start = offset
        if unit:
            start = pl.multiple_of(offset + unit * jnp.bitwise_xor(meta[1], far), 16)
        outs[dst][row : row + rows, :] = scratch[pl.ds(start, rows), :]


def small_block(meta, gain_one, gain_two, rel):
    row, lane = iota((16, 128), 0), iota((16, 128), 1)
    block = jnp.where((row == 2) & (lane == 0), (meta[4] // 256).astype(F32), 0.0)
    block = jnp.where((row == 2) & (lane == 1), (meta[4] % 256).astype(F32), block)
    parts = [(0, gain_one), (1, gain_two)] + [(4 + n, rel[n : n + 1, :]) for n in range(rel.shape[0])]
    for at, value in parts:
        value = value[...].astype(F32)
        wide = jnp.concatenate([value, jnp.zeros((1, 128 - value.shape[1]), F32)], axis=1)
        block = jnp.where(row == at, wide, block)
    return block.astype(BF16)


def pack_kernel(n_chips, meta, *refs):
    sources = refs[:5]
    gain_one, gain_two, rel = refs[5:8]
    kept_a, given_a, kept_b, given_b = refs[8:12]
    held, sems = refs[12:17], refs[17]
    handles = [pltpu.make_async_copy(a, b, sems.at[n]) for n, (a, b) in enumerate(zip(sources, held))]
    for handle in handles:
        handle.start()
    width = 4 * (held[0].shape[1] // 2)
    block = small_block(meta, gain_one, gain_two, rel)
    for out in (kept_a, given_a):
        out[:, width:] = jnp.zeros((out.shape[0], 128), BF16)
        out[0:16, width:] = block
    for handle in handles:
        handle.wait()
    wq, wk, wv, wo, w_in = held
    core = meta[2]
    half = wq.shape[1] // 2
    block = w_in.shape[1] // (2 * n_chips)
    for which, a_ref, b_ref in ((core, kept_a, kept_b), (1 - core, given_a, given_b)):
        for n, w in enumerate((wq, wk, wv, wo)):
            cols = pl.ds(pl.multiple_of(which * half, 128), half)
            a_ref[:, n * half : (n + 1) * half] = w[:, cols]
        for n in range(b_ref.shape[1] // block):
            cols = pl.ds(pl.multiple_of((2 * n + which) * block, 128), block)
            b_ref[:, n * block : (n + 1) * block] = w_in[:, cols]


def stack_kernel(meta, kept, taken, both):
    shard = kept.shape[0]
    both[pl.ds(pl.multiple_of(shard * meta[2], 16), shard), :] = kept[...]
    both[pl.ds(pl.multiple_of(shard * (1 - meta[2]), 16), shard), :] = taken[...]


def cut_kernel(meta, by_x, by_y, upper, lower):
    h = upper.shape[0]
    upper[...] = by_x[:h, :]
    lower[...] = by_y[h:, :]


def low_kernel(meta, out_cot, pool_cot, low):
    size = low.shape[0]
    length, prefix = meta[4], meta[5]
    count = (length - prefix).astype(F32)

    def lows(ds):
        t = iota((256, 1), 0) + ds.start
        pool = jnp.where((t >= prefix) & (t < length), 1.0, 0.0) / count
        low[ds, :] = (out_cot[ds, :].astype(F32) + pool * pool_cot[...]).astype(BF16)

    rows_loop(size, 256, lows)


def prepare_kernel(copies, n_pieces, levels, meta, hidden, hidden_peer, buckets, *refs):
    pieces = refs[:n_pieces]
    normed, normed_peer, bias, gain_one, gain_two, length_peer = refs[n_pieces : n_pieces + 6]
    rest = refs[n_pieces + 6 :]
    if copies:
        qkv, w_half, table, table_rows = rest
        place(meta, pieces, (qkv, w_half), copies)
        count = n_pieces
        column = pieces[0].shape[1] - 128
        blocks = [ref[0:16, column:].astype(F32) for ref in pieces]
        places = [jnp.bitwise_xor(meta[0], 2 * (p % 4) + p // 4) for p in range(count)]
    else:
        table, table_rows = rest
        count = pieces[0].shape[0] // 16
        blocks = [pieces[0][16 * p : 16 * p + 16, :].astype(F32) for p in range(count)]
        places = [jnp.int32(p) for p in range(count)]
    size, width = hidden.shape
    shard = width // count
    some = levels // count
    table[...] = jnp.zeros_like(table)
    first = jnp.zeros((1, width), F32)
    second = jnp.zeros((1, width), F32)
    rest = jnp.zeros((1, width - 128), F32)
    peers = jnp.zeros((1, 1), F32)
    for where, piece in zip(places, blocks):
        first += pltpu.roll(jnp.concatenate([piece[0:1], rest], axis=1), shard * where, 1)
        second += pltpu.roll(jnp.concatenate([piece[1:2], rest], axis=1), shard * where, 1)
        length = 256.0 * piece[2:3, 0:1] + piece[2:3, 1:2]
        peers += jnp.where(where == jnp.bitwise_xor(meta[0], 1), length, 0.0)
        for b in range(some):
            table[pl.ds(some * where + b, 1), :] = piece[4 + b : 5 + b]
    length_peer[...] = jnp.broadcast_to(peers, (1, 128))
    gain_one[...] = first
    gain_two[...] = second

    for x_ref, n_ref in ((hidden, normed), (hidden_peer, normed_peer)):

        def rows(ds, x_ref=x_ref, n_ref=n_ref):
            x = x_ref[ds, :].astype(F32)
            inv = lax.rsqrt(jnp.mean(x * x, axis=-1, keepdims=True) + EPS)
            n_ref[ds, :] = (x * inv * gain_one[...]).astype(BF16)

        rows_loop(size, 256, rows)

    span = 2 * size
    hot = (buckets[...] == iota((levels, span), 0)).astype(BF16)
    table_rows[...] = dot_left(table[...].astype(BF16), hot)
    heads, _, wide = bias.shape
    base = heads * meta[2]

    def head(h, carry):
        row = table_rows[pl.ds(base + h, 1), :]
        first = jnp.broadcast_to(pltpu.roll(row, span - 127, 1), (8, span))
        sub = iota((8, span), 0)
        full = first
        for k in range(1, 8):
            full = jnp.where(sub == k, pltpu.roll(first, k, 1), full)
        bias[h, 0:8, :] = full[:, :wide]
        have = 8
        while have < 128:
            more = pltpu.roll(full, have, 1)
            bias[h, have : 2 * have, :] = more[:, :wide]
            full = jnp.concatenate([full, more], axis=0)
            have *= 2
        return carry

    lax.fori_loop(0, heads, head, 0)


def attend_kernel(meta, x_ref, bias, w, length, qkv, out, upper, lower, powers, inv_sums, scores):
    size = x_ref.shape[0]
    part = w.shape[1] // 3
    pairs = part // 128
    lane = iota((1, 128), 1)
    half = lane < 64
    strips = size // 128
    inv_sums[...] = jnp.zeros_like(inv_sums)

    def project(ds):
        for n in range(3):
            cols = slice(n * part, (n + 1) * part)
            qkv[ds, cols] = dot(x_ref[ds, :], w[:, cols]).astype(BF16)

    rows_loop(size, size, project)
    masked = jnp.where(iota((size, 1), 0).astype(F32) < length[0:1, 0:1], 0.0, -1e30).astype(F32)

    def pair(p, carry):
        base = pl.multiple_of(p * 128, 128)
        qp = qkv[:, pl.ds(base, 128)].astype(F32)
        kp = qkv[:, pl.ds(base + part, 128)].astype(F32)
        vp = qkv[:, pl.ds(base + 2 * part, 128)].astype(F32)
        joined = None
        for side in range(2):
            head = 2 * p + side
            own = half if side == 0 else jnp.logical_not(half)
            spare = lane == (64 if side == 0 else 0)
            qa = jnp.where(own, qp, jnp.where(spare, 1.0, 0.0)).astype(BF16)
            ka = jnp.where(own, kp, jnp.where(spare, masked, 0.0)).astype(BF16)
            va = jnp.where(own, vp, jnp.where(spare, 1.0, 0.0)).astype(BF16)
            top = None
            for a in range(strips):
                rows = slice(128 * a, 128 * a + 128)
                off = 128 * (strips - 1 - a)
                s = dot_right(ka[rows], qa) + bias[head, :, off : off + size]
                scores[rows, :] = s
                peak = jnp.max(s, axis=0, keepdims=True)
                top = peak if top is None else jnp.maximum(top, peak)
            for a in range(strips):
                rows = slice(128 * a, 128 * a + 128)
                powers[head, rows, :] = jnp.exp(scores[rows, :] - top).astype(BF16)
            mixed = dot_left(va, powers[head]).T
            sums = jnp.sum(jnp.where(spare, mixed, 0.0), axis=1, keepdims=True)
            inv = 1.0 / sums
            inv_sums[...] = jnp.where(lane == head, inv, inv_sums[...])
            mixed = mixed * inv
            joined = mixed if side == 0 else jnp.where(half, joined, mixed)
        joined = joined.astype(BF16)
        cols = pl.ds(base, 128)
        out[:, cols] = joined
        upper[:, cols] = joined[: size // 2]
        lower[:, cols] = joined[size // 2 :]
        return carry

    lax.fori_loop(0, pairs, pair, 0, unroll=True)


def residual_kernel(meta, hidden, attended, upper, lower, gain, w_half, w_other, residual, normed, left, middle, right, sums, w_out):
    size, width = hidden.shape
    half = width // 2
    length = meta[4]
    core = meta[2]
    w_out[:, pl.ds(pl.multiple_of(core * half, 128), half)] = w_half[...]
    w_out[:, pl.ds(pl.multiple_of((1 - core) * half, 128), half)] = w_other[...]
    mine = pl.ds(pl.multiple_of(core * half, 128), half)
    other = pl.ds(pl.multiple_of((1 - core) * half, 128), half)
    sums[...] = jnp.zeros_like(sums)

    for first, got in ((0, upper), (size // 2, lower)):
        ds = slice(first, first + size // 2)
        x = hidden[ds, :].astype(F32)
        branch = dot(attended[ds, :], w_out[mine, :]) + dot(got[...], w_out[other, :])
        live = (iota((size // 2, 1), 0) + first) < length
        sums[0:1, :] += jnp.sum(jnp.where(live, x * x, 0.0), axis=0, keepdims=True)
        sums[1:2, :] += jnp.sum(jnp.where(live, branch * branch, 0.0), axis=0, keepdims=True)
        r = x + branch
        residual[ds, :] = r
        inv = lax.rsqrt(jnp.mean(r * r, axis=-1, keepdims=True) + EPS)
        value = (r * inv * gain[...]).astype(BF16)
        normed[ds, :] = value
        third = left.shape[1]
        for n, ref in enumerate((left, middle, right)):
            ref[ds, :] = value[:, n * third : (n + 1) * third]


def expand_kernel(copies, n_pieces, *refs):
    meta, x_ref = refs[:2]
    pieces = refs[2 : 2 + n_pieces]
    if copies:
        activated, slope, w_in = refs[2 + n_pieces :]
        place(meta, pieces, (w_in,), copies)
    else:
        w_in = pieces[0]
        activated, slope, whole = refs[2 + n_pieces :]
        third = x_ref.shape[1]
        for n, ref in enumerate((x_ref, *pieces[1:])):
            whole[:, n * third : (n + 1) * third] = ref[...]
        x_ref = whole
    chunk = 512 if w_in.shape[1] % 512 == 0 else 256

    def rows(ds):
        x = x_ref[ds, :]
        for c in range(0, w_in.shape[1], chunk):
            t = dot(x, w_in[:, c : c + chunk])
            square = t * t
            th = jnp.tanh(t * (GELU_A + (GELU_A * GELU_B) * square))
            phi = 0.5 + 0.5 * th
            activated[ds, c : c + chunk] = (t * phi).astype(BF16)
            inner = GELU_A + (3.0 * GELU_A * GELU_B) * square
            slope[ds, c : c + chunk] = (phi + 0.5 * t * (1.0 - th * th) * inner).astype(BF16)

    rows_loop(x_ref.shape[0], x_ref.shape[0], rows)


def product_kernel(plan, n_out, *refs):
    meta, left_own, left_peer, right_own, right_peer = refs[:5]
    outs = refs[5 : 5 + n_out]
    grads = refs[5 + n_out]
    step = 512 if grads.shape[0] % 512 == 0 else 384
    for c in range(0, grads.shape[0], step):
        part = dot_left(left_own[:, c : c + step], right_own[...])
        part += dot_left(left_peer[:, c : c + step], right_peer[...])
        grads[c : c + step, :] = part.astype(BF16)
    scatter_out(meta, grads, outs, plan)


def contract_kernel(copies, n_pieces, *refs):
    meta, slope_own, slope_peer, low_own, low_peer, w_in = refs[:6]
    pieces = refs[6 : 6 + n_pieces]
    pre_own, pre_peer, part_own, *sends, w_ffout = refs[6 + n_pieces :]
    third = sends[0].shape[1]
    place(meta, pieces, (w_ffout,), copies)
    size = low_own.shape[0]
    chunk = 512 if w_in.shape[1] % 512 == 0 else 256
    for slope, low, grad_pre, part in (
        (slope_peer, low_peer, pre_peer, sends),
        (slope_own, low_own, pre_own, (part_own,)),
    ):

        def rows(ds, slope=slope, low=low, grad_pre=grad_pre, part=part):
            y = low[ds, :]
            total = None
            for c in range(0, w_in.shape[1], chunk):
                g = dot_right(y, w_ffout[c : c + chunk, :])
                g = (slope[ds, c : c + chunk].astype(F32) * g).astype(BF16)
                grad_pre[ds, c : c + chunk] = g
                t = dot_right(g, w_in[:, c : c + chunk])
                total = t if total is None else total + t
            if len(part) > 1:
                for n, ref in enumerate(part):
                    ref[ds, :] = total[:, n * third : (n + 1) * third].astype(BF16)
            else:
                part[0][ds, :] = total

        rows_loop(size, size, rows)


def through_kernel(meta, residual, part, left, center, right, out_cot, pool_cot, gain, w_half, w_other,
                   grad_residual, low_mine, upper, lower, grad_keep, grad_send, grad_gain):
    size, width = residual.shape
    half = width // 2
    core = meta[2]
    mine = pl.ds(pl.multiple_of(core * half, 128), half)
    theirs = pl.ds(pl.multiple_of((1 - core) * half, 128), half)
    length, prefix = meta[4], meta[5]
    count = (length - prefix).astype(F32)
    grad_gain[...] = jnp.zeros_like(grad_gain)

    def rows(ds, low_given, start):
        x = residual[ds, :]
        gn = part[ds, :] + jnp.concatenate([left[ds, :], center[ds, :], right[ds, :]], axis=1).astype(F32)
        inv = lax.rsqrt(jnp.mean(x * x, axis=-1, keepdims=True) + EPS)
        u = gain[...] * gn
        xr = x * inv
        t = iota((256, 1), 0) + ds.start
        pool = jnp.where((t >= prefix) & (t < length), 1.0, 0.0) / count
        go = out_cot[ds, :].astype(F32) + pool * pool_cot[...]
        g = go + inv * (u - xr * jnp.mean(xr * u, axis=-1, keepdims=True))
        grad_gain[...] += jnp.sum(xr * gn, axis=0, keepdims=True)
        grad_residual[ds, :] = g
        first, second = g[:, :half].astype(BF16), g[:, half:].astype(BF16)
        on_first = jnp.broadcast_to(core == 0, first.shape)
        a = jnp.where(on_first, g[:, :half], g[:, half:]).astype(BF16)
        b = jnp.where(on_first, g[:, half:], g[:, :half]).astype(BF16)
        low_mine[ds, :] = a
        low_given[pl.ds(ds.start - start, 256), :] = b
        grad_keep[ds, :] = (dot_right(a, w_half[mine, :]) + dot_right(b, w_other[mine, :])).astype(BF16)
        grad_send[ds, :] = (dot_right(a, w_half[theirs, :]) + dot_right(b, w_other[theirs, :])).astype(BF16)

    middle = size // 2
    for first, low_given in ((0, upper), (middle, lower)):

        def some(i, carry, first=first, low_given=low_given):
            rows(pl.ds(pl.multiple_of(first + 256 * i, 256), 256), low_given, first)
            return carry

        lax.fori_loop(0, middle // 256, some, 0)


def attend_back_kernel(meta, qkv, powers, g_ref, a_ref, inv_sums, diag_in, out, diag, grads, slant):
    size = g_ref.shape[0]
    part = qkv.shape[1] // 3
    pairs = part // 128
    strips = size // 128
    span = 2 * size
    lane = iota((1, 128), 1)
    half = lane < 64
    diag[...] = diag_in[...]

    def pair(p, carry):
        base = pl.multiple_of(p * 128, 128)
        cols = pl.ds(base, 128)
        kcols = pl.ds(base + part, 128)
        vcols = pl.ds(base + 2 * part, 128)
        qp, kp = qkv[:, cols], qkv[:, kcols]
        vp = qkv[:, vcols].astype(F32)
        do = g_ref[:, cols].astype(F32)
        prod = do * a_ref[:, cols].astype(F32)
        dq_all = dk_all = dv_all = None
        for side in range(2):
            head = 2 * p + side
            own = half if side == 0 else jnp.logical_not(half)
            one = 64 if side == 0 else 0
            inv = jnp.sum(jnp.where(lane == head, inv_sums[...], 0.0), axis=1, keepdims=True)
            inner = jnp.sum(jnp.where(own, prod, 0.0), axis=1, keepdims=True) * inv
            upper = inner.astype(BF16).astype(F32)
            dos = jnp.where(
                own,
                do * inv,
                jnp.where(lane == one, -upper, jnp.where(lane == one + 1, upper - inner, 0.0)),
            ).astype(BF16)
            ones = (lane == one) | (lane == one + 1)
            va = jnp.where(own, vp, jnp.where(ones, 1.0, 0.0)).astype(BF16)
            slant[...] = jnp.zeros_like(slant)
            for a in range(strips):
                rows = slice(128 * a, 128 * a + 128)
                off = 128 * (strips - 1 - a)
                ds = (powers[head, rows, :].astype(F32) * dot_right(va[rows], dos)).astype(BF16)
                grads[rows, :] = ds
                slant[:, off : off + size] += ds.astype(F32)
            dk = dot(grads[...], qp)
            dv = dot(powers[head], dos)
            dk_all = dk if side == 0 else jnp.where(half, dk_all, dk)
            dv_all = dv if side == 0 else jnp.where(half, dv_all, dv)
            dq = dot_left(kp, grads[...]).T
            dq_all = dq if side == 0 else jnp.where(half, dq_all, dq)
            y = slant[...]
            rest = 64
            while rest >= 1:
                y = y[:rest] + pltpu.roll(y[rest:], span - rest, 1)
                rest //= 2
            diag[pl.ds(head, 1), :] += pltpu.roll(y, 127, 1)
        out[:, cols] = dq_all.astype(BF16)
        out[:, kcols] = dk_all.astype(BF16)
        out[:, vcols] = dv_all.astype(BF16)
        return carry

    lax.fori_loop(0, pairs, pair, 0, unroll=True)


def weights_kernel(plan, n_out, *refs):
    meta, x_own, x_peer, dqkv_own, dqkv_peer, att_own, upper, lower, att_peer, got_upper, got_lower, low_own, low_upper, low_lower, small = refs[:15]
    outs = refs[15 : 15 + n_out]
    (grads,) = refs[15 + n_out :]
    middle = upper.shape[0]
    part = dqkv_own.shape[1]
    depth = x_own.shape[1]
    half = depth // 2
    for c in range(0, depth, 384):
        cols = slice(c, c + 384)
        g = dot_left(x_own[:, cols], dqkv_own[...]) + dot_left(x_peer[:, cols], dqkv_peer[...])
        grads[cols, 0:part] = g.astype(BF16)
    core = meta[2]
    mine = pl.multiple_of(core * half, 16)
    theirs = pl.multiple_of((1 - core) * half, 16)
    for c in range(0, half, 384):
        cols = slice(c, c + 384)
        g = dot_left(att_own[:, cols], low_own[...]) + dot_left(att_peer[:middle, cols], low_upper[...])
        g += dot_left(att_peer[middle:, cols], low_lower[...])
        grads[pl.ds(mine + c, 384), part:] = g.astype(BF16)
        g = dot_left(upper[:, cols], low_own[:middle]) + dot_left(lower[:, cols], low_own[middle:])
        g += dot_left(got_upper[:, cols], low_upper[...])
        g += dot_left(got_lower[:, cols], low_lower[...])
        grads[pl.ds(theirs + c, 384), part:] = g.astype(BF16)
    grads[depth:, :] = jnp.zeros((16, grads.shape[1]), BF16)
    grads[depth:, 0:128] = small[...].astype(BF16)
    scatter_out(meta, grads, outs, plan)


def inputs_kernel(meta, dqkv_own, dqkv_peer, w, hidden, hidden_peer, gain_two, diag, buckets,
                  part_own, left, right, small, gain_one):
    size, width = part_own.shape
    half = width // 2
    small[...] = jnp.zeros_like(small)
    gain_one[...] = jnp.zeros_like(gain_one)

    def share(x_ref, ds, value):
        x = x_ref[ds, :].astype(F32)
        inv = lax.rsqrt(jnp.mean(x * x, axis=-1, keepdims=True) + EPS)
        gain_one[...] += jnp.sum(x * inv * value, axis=0, keepdims=True)

    def peers(ds):
        value = dot_right(dqkv_peer[ds, :], w[...])
        share(hidden_peer, ds, value)
        value = value.astype(BF16)
        left[ds, :] = value[:, :half]
        right[ds, :] = value[:, half:]

    def own(ds):
        value = dot_right(dqkv_own[ds, :], w[...])
        share(hidden, ds, value)
        part_own[ds, :] = value

    rows_loop(size, size, peers)
    rows_loop(size, size, own)
    count = width // 128
    for n in range(count):
        small[n : n + 1, :] = gain_one[:, 128 * n : 128 * n + 128]
        small[count + n : count + n + 1, :] = gain_two[:, 128 * n : 128 * n + 128]
    hot = (buckets[...] == iota((128, diag.shape[1]), 0)).astype(F32)
    table = lax.dot_general(
        diag[...],
        hot,
        (((1,), (1,)), ((), ())),
        preferred_element_type=F32,
        precision=lax.Precision.HIGHEST,
    )
    lane = iota((1, 128), 1)
    few = (16 - 2 * count) * 2 - 2
    for n in range(few):
        head = few * meta[2] + n
        row = jnp.where(lane < 32, table[n : n + 1, :], 0.0)
        small[pl.ds(2 * count + head // 4, 1), :] += pltpu.roll(row, 32 * (head % 4), 1)


def hidden_kernel(meta, hidden, grad_residual, part, left, right, gain, grad_hidden):
    def rows(ds):
        total = part[ds, :] + jnp.concatenate([left[ds, :], right[ds, :]], axis=1).astype(F32)
        x = hidden[ds, :].astype(F32)
        inv = lax.rsqrt(jnp.mean(x * x, axis=-1, keepdims=True) + EPS)
        u = gain[...] * total
        xr = x * inv
        grad_hidden[ds, :] = grad_residual[ds, :] + inv * (
            u - xr * jnp.mean(xr * u, axis=-1, keepdims=True)
        )

    rows_loop(hidden.shape[0], 256, rows)


def output_kernel(meta, act_own, act_peer, w_ffout, part_own, left, right):
    size, width = part_own.shape
    half = width // 2

    def peers(ds):
        value = dot(act_peer[ds, :], w_ffout[...]).astype(BF16)
        left[ds, :] = value[:, :half]
        right[ds, :] = value[:, half:]

    def own(ds):
        part_own[ds, :] = dot(act_own[ds, :], w_ffout[...])

    rows_loop(size, size, peers)
    rows_loop(size, size, own)


def finish_kernel(meta, residual, part, left, right, sums, hidden_out, pooled, stats):
    size, width = residual.shape
    length, prefix = meta[4], meta[5]
    count = (length - prefix).astype(F32)
    pooled[...] = jnp.zeros_like(pooled)
    stats[...] = jnp.zeros_like(stats)

    def rows(ds):
        branch = part[ds, :] + jnp.concatenate([left[ds, :], right[ds, :]], axis=1).astype(F32)
        out = residual[ds, :] + branch
        hidden_out[ds, :] = out.astype(BF16)
        t = iota((128, 1), 0) + ds.start
        live = t < length
        stats[0:1, :] += jnp.sum(jnp.where(live, branch * branch, 0.0), axis=0, keepdims=True)
        pooled[...] += jnp.sum(jnp.where((t >= prefix) & live, out, 0.0), axis=0, keepdims=True)

    rows_loop(size, 128, rows)
    pooled[...] = pooled[...] / count
    total = jnp.sum(stats[0:1, :])
    first = jnp.sum(sums[0:1, :])
    second = jnp.sum(sums[1:2, :])
    denominator = length.astype(F32) * width
    column = iota(stats.shape, 1)
    values = jnp.where(column == 0, first, jnp.where(column == 1, second, total))
    stats[...] = jnp.sqrt(values / denominator)


def total(*parts):
    value = parts[0].astype(F32)
    for part in parts[1:]:
        value = value + part.astype(F32)
    return value.astype(BF16)


def turn_kernel(meta, keep_a, got_x, keep_b, got_y, on_y, on_x):
    h = on_x.shape[0]
    on_y[...] = total(keep_a[h:], got_x[h:])
    on_x[...] = total(keep_b[h:], got_y[h:])


def add_kernel(meta, a, b, out):
    out[...] = total(a[...], b[...])


def land_half_kernel(meta, keep_a, got_x, last_y, keep_b, got_y, last_x, keep, send):
    h, width = last_x.shape
    upper = total(keep_a[:h], got_x[:h], last_y[:h])
    lower = total(keep_b[:h], got_y[:h], last_x[...])
    first = jnp.broadcast_to(meta[3] % 2 == 0, upper.shape)
    keep[:, :width] = jnp.where(first, upper.astype(F32), lower.astype(F32)).astype(BF16)
    send[:, :width] = jnp.where(first, lower.astype(F32), upper.astype(F32)).astype(BF16)
    if keep.shape[1] > width:
        rows = slice(2 * h, 2 * h + 16)
        small = total(keep_a[rows, 0:128], got_x[rows, 0:128], last_y[h:, 0:128])
        for out in (keep, send):
            out[:, width:] = jnp.zeros((h, 128), BF16)
            out[:16, width:] = small


def halve_kernel(width, meta, a, b, keep, send):
    h = keep.shape[0]
    place_at = pl.multiple_of(h * (meta[3] // 2), 16)
    other_at = pl.multiple_of(h * (1 - meta[3] // 2), 16)
    keep[:, :width] = total(a[pl.ds(place_at, h), :width], b[pl.ds(place_at, h), :width])
    send[:, :width] = total(a[pl.ds(other_at, h), :width], b[pl.ds(other_at, h), :width])
    if width < keep.shape[1]:
        extra = total(a[:h, width:], b[:h, width:])
        keep[:, width:] = extra
        send[:, width:] = extra


def last_kernel(meta, a, b, out, small):
    width = out.shape[1]
    out[...] = total(a[:, :width], b[:, :width])
    small[...] = a[:16, width:].astype(F32) + b[:16, width:].astype(F32)


def join_rows_kernel(meta, own, by_low, by_high, by_both, out):
    h = own.shape[0]
    low, high = meta[3] % 2, meta[3] // 2
    for value, at_low, at_high in (
        (own, low, high),
        (by_low, 1 - low, high),
        (by_high, low, 1 - high),
        (by_both, 1 - low, 1 - high),
    ):
        out[pl.ds(pl.multiple_of(h * (2 * at_low + at_high), 16), h), :] = value[...].astype(F32)


def join_kernel(meta, own, by_low, by_high, by_both, mine, other):
    h = own.shape[0]
    low, high = meta[3] % 2, meta[3] // 2
    for value, at_low, at_high in (
        (own, low, high),
        (by_low, 1 - low, high),
        (by_high, low, 1 - high),
        (by_both, 1 - low, 1 - high),
    ):
        rows = pl.ds(pl.multiple_of(h * at_high, 16), h)

        @pl.when(at_low == meta[2])
        def _(value=value, rows=rows):
            mine[rows, :] = value[...]

        @pl.when(at_low != meta[2])
        def _(value=value, rows=rows):
            other[rows, :] = value[...]


def weave_in_kernel(block, meta, mine, other, out):
    for which, ref in ((meta[2], mine), (1 - meta[2], other)):
        for n in range(ref.shape[1] // block):
            cols = pl.ds(pl.multiple_of((2 * n + which) * block, 128), block)
            out[:, cols] = ref[:, n * block : (n + 1) * block].astype(F32)


def weave_at_kernel(meta, mine, other, *outs):
    half = outs[0].shape[1] // 2
    for which, ref in ((meta[2], mine), (1 - meta[2], other)):
        cols = pl.ds(pl.multiple_of(which * half, 128), half)
        for n, out in enumerate(outs):
            out[:, cols] = ref[:, n * half : (n + 1) * half].astype(F32)


def swap(v, axis, count, far):
    return lax.ppermute(v, axis, [(i, i ^ far) for i in range(count)])


def message_plan(unit):
    h = unit // 2
    plan = []
    for dst, (near, far) in enumerate(((1, 3), (2, 3), (0, 2), (0, 1))):
        offset = 0 if dst in (0, 2) else h
        plan.append((dst, 0, h, unit, near, offset))
        plan.append((dst, h, h, unit, far, offset))
    return plan


class Link:
    def __init__(self, far):
        self.far = far
        self.sent = []

    def send(self, v):
        if len(self.sent) >= 2:
            v = after(v, self.sent[-2])
        got = swap(v, "fsdp", 8, self.far)
        self.sent.append(got)
        return got


def body(
    nf,
    nz,
    hidden_in,
    norm_gain_attn,
    w_query,
    w_key,
    w_value,
    w_out,
    rel_bias,
    norm_gain_ffn,
    w_in,
    w_ffout,
    bucket_index,
    row_lengths,
    prefix_lengths,
    out_cotangent,
    pool_cotangent,
):
    fast = nf == 8 and nz == 4
    size, width = hidden_in.shape
    shard = w_query.shape[0]
    heads = rel_bias.shape[1]
    levels = rel_bias.shape[0] * nf
    full_ff = w_in.shape[1]
    part_ff = full_ff // 2
    block = w_ffout.shape[0]
    half = width // 2
    few = heads // 2
    me = lax.axis_index("fsdp").astype(jnp.int32)
    where = lax.axis_index("dp").astype(jnp.int32)
    core = me & 1
    zero = jnp.zeros((), jnp.int32)

    def by_core(first, second):
        return jnp.where(core == 0, first, second)

    def peer(v):
        return swap(v, "fsdp", nf, 1)

    def dma(n):
        return pltpu.SemaphoreType.DMA((n,))

    def vm(*arrays):
        return [(a, "v") for a in arrays]

    meta = jnp.stack([me, me >> 1, core, where, row_lengths[0], prefix_lengths[0], zero, zero])
    hidden_peer = peer(hidden_in)
    wide = 3 * half
    buckets = jnp.concatenate([bucket_index[::-1], jnp.full((1,), -1, jnp.int32)])[None, :]

    if fast:
        kept_a, given_a, kept_b, given_b = call(
            functools.partial(pack_kernel, nf // 2),
            "pack",
            meta,
            [(a, "h") for a in (w_query, w_key, w_value, w_out, w_in)]
            + vm(norm_gain_attn[None], norm_gain_ffn[None], rel_bias),
            [((shard, 4 * half + 128), BF16, "v")] * 2 + [((shard, part_ff), BF16, "v")] * 2,
            [pltpu.VMEM(w.shape, BF16) for w in (w_query, w_key, w_value, w_out, w_in)] + [dma(5)],
            limit=56 * 2**20,
        )
        on_x, on_y = Link(2), Link(4)
        taken_a = peer(given_a)
        x_kept, y_taken = on_x.send(kept_a), on_y.send(taken_a)
        x_taken, y_kept = on_x.send(taken_a), on_y.send(kept_a)
        far_kept, far_taken = on_y.send(x_kept), on_x.send(y_taken)
        a_pieces = [kept_a, x_kept, y_kept, far_kept, taken_a, x_taken, y_taken, far_taken]
        a_copies = []
        for number in range(8):
            far, side = number % 4, 1 + number // 4
            a_copies.append((number, 0, shard, 0, 0, 0, 0, wide, 2 * shard, far, side))
            a_copies.append((number, 0, shard, wide, 1, 0, 0, half, 2 * shard, far, side))
        taken_b = peer(after(given_b, hidden_peer, taken_a))
        (both_b,) = call(
            stack_kernel,
            "stack",
            meta,
            vm(kept_b, taken_b),
            [((2 * shard, part_ff), BF16, "v")],
        )

        def near(v):
            return [v, on_x.send(v), on_y.send(v)]

        def distant(three, *deps):
            v, by_x, by_y = three
            h = v.shape[0] // 2
            upper, lower = call(
                cut_kernel, "cut", meta, vm(by_x, by_y), [((h, v.shape[1]), BF16, "v")] * 2, deps=deps
            )
            far_y, far_x = on_y.send(upper), on_x.send(lower)
            return three + [far_y, far_x]

        def rows_of(five):
            h = five[3].shape[0]
            return zip(five, (0, 0, 0, 0, h), (0, 1, 2, 3, 3))

    else:

        def whole(v):
            return lax.all_gather(v, "fsdp", axis=0, tiled=True)

        a_full = [whole(w) for w in (w_query, w_key, w_value, w_out)]
        a_full = [by_core(w[:, :half], w[:, half:]) for w in a_full]
        qkv_w, out_half = jnp.concatenate(a_full[:3], axis=1), a_full[3]
        b_full = whole(w_in).reshape(width, nf // 2, 2, block)
        b_pieces = [by_core(b_full[:, :, 0], b_full[:, :, 1]).reshape(width, part_ff)]
        b_copies = [(0, 0, width, 0, 0, 0, 0, part_ff, 0, 0, 0)]
        c_full = whole(w_ffout).reshape(nf // 2, 2, block, width)
        c_pieces = [by_core(c_full[:, 0], c_full[:, 1]).reshape(part_ff, width)]
        c_copies = [(0, 0, part_ff, 0, 0, 0, 0, width, 0, 0, 0)]
        length = row_lengths[0]
        split = jnp.stack([length // 256, length % 256]).astype(BF16)[None]
        rows = [norm_gain_attn[None], norm_gain_ffn[None], split, split, rel_bias]
        rows = [jnp.pad(r, ((0, 0), (0, 128 - r.shape[1]))) for r in rows]
        small = jnp.concatenate(rows, axis=0)
        a_pieces, a_copies = [whole(jnp.pad(small, ((0, 16 - small.shape[0]), (0, 0))))], ()

    (low,) = call(
        low_kernel, "low", meta, vm(out_cotangent, pool_cotangent), [((size, width), BF16, "v")]
    )
    normed, normed_peer, bias, gain_one, gain_two, length_peer, *weights = call(
        functools.partial(prepare_kernel, a_copies, len(a_pieces), levels),
        "prepare",
        meta,
        vm(hidden_in, hidden_peer, buckets, *a_pieces),
        [
            ((size, width), BF16, "v"),
            ((size, width), BF16, "v"),
            ((few, 128, 2 * size - 128), F32, "v"),
            ((1, width), F32, "v"),
            ((1, width), F32, "v"),
            ((1, 128), F32, "v"),
        ]
        + ([((width, wide), BF16, "v"), ((width, half), BF16, "v")] if fast else []),
        [pltpu.VMEM((levels, 128), F32), pltpu.VMEM((128, 2 * size), F32)],
        deps=(low,),
    )
    if fast:
        b_pieces = near(both_b)
        qkv_w, out_half = weights
    out_other = peer(out_half)

    def attend(x, length, name, *deps):
        return call(
            attend_kernel,
            name,
            meta,
            vm(x, bias, qkv_w, length),
            [
                ((size, wide), BF16, "v"),
                ((size, half), BF16, "v"),
                ((size // 2, half), BF16, "v"),
                ((size // 2, half), BF16, "v"),
                ((few, size, size), BF16, "v"),
                ((size, 128), F32, "v"),
            ],
            [pltpu.VMEM((size, size), F32)],
            deps=deps,
        )

    qkv_peer, given_att, *given_halves, powers_peer, sums_peer = attend(
        normed_peer, length_peer, "attend_peer"
    )
    low_peer = peer(after(low, given_att))
    if fast:
        b_pieces = distant(b_pieces, given_att)
        b_copies = [
            (number, 0, piece.shape[0], 0, 0, row, 0, part_ff, 2 * shard, far, 0)
            for number, (piece, row, far) in enumerate(rows_of(b_pieces))
        ]
        c_pieces = near(w_ffout)
    served = tuple(b_pieces[n] for n in (1, 2)) if fast else ()
    length_own = jnp.broadcast_to(row_lengths.astype(F32)[None], (1, 128))
    qkv_own, attended, *own_halves, powers_own, sums_own = attend(
        normed, length_own, "attend_own", given_att, out_other, *served
    )
    served = tuple(b_pieces[n] for n in (3, 4)) if fast else ()
    got_att = [peer(after(v, attended, *served)) for v in given_halves]
    residual, normed_two, *thirds, sums = call(
        residual_kernel,
        "residual",
        meta,
        vm(hidden_in, attended, *got_att, gain_two, out_half, out_other),
        [((size, width), F32, "v"), ((size, width), BF16, "v")]
        + [((size, width // 3), BF16, "v")] * 3
        + [((8, width), F32, "v")],
        [pltpu.VMEM((width, width), BF16)],
        deps=(low_peer,),
    )
    thirds = [peer(v) for v in thirds]
    shape_in = pltpu.VMEM((width, part_ff), BF16)
    shape_ff = pltpu.VMEM((part_ff, width), BF16)
    if fast:
        ff_plan, in_plan = message_plan(block), message_plan(2 * shard)
        ff_outs = [((block, width), BF16, "v")] * 4
        in_outs = [((2 * shard, part_ff), BF16, "v")] * 4
    else:
        ff_plan = [(0, 0, part_ff, 0, 0, 0)]
        in_plan = [(0, 0, width, 0, 0, 0)]
        ff_outs = [((part_ff, width), BF16, "v")]
        in_outs = [((width, part_ff), BF16, "v")]
    act_own, slope_own, in_w = call(
        functools.partial(expand_kernel, b_copies, len(b_pieces)),
        "expand_own",
        meta,
        vm(normed_two, *b_pieces),
        [((size, part_ff), BF16, "v")] * 2 + [((width, part_ff), BF16, "v")],
        deps=tuple(thirds),
    )
    if fast:
        c_pieces = distant(c_pieces, act_own)
        c_copies = [
            (number, 0, piece.shape[0], 0, 0, row, 0, width, block, far, 0)
            for number, (piece, row, far) in enumerate(rows_of(c_pieces))
        ]
    act_peer, slope_peer, normed_two_peer = call(
        functools.partial(expand_kernel, (), 3),
        "expand_peer",
        meta,
        vm(thirds[0], in_w, *thirds[1:]),
        [((size, part_ff), BF16, "v")] * 2 + [((size, width), BF16, "v")],
        deps=tuple(c_pieces[n] for n in (1, 2)) if fast else (),
    )
    ff_parts = call(
        functools.partial(product_kernel, ff_plan, len(ff_outs)),
        "product",
        meta,
        vm(act_own, act_peer, low, low_peer),
        ff_outs,
        [shape_ff],
    )
    ff_parts = list(ff_parts)
    if fast:
        ff_x = on_x.send(after(ff_parts[0], c_pieces[3], c_pieces[4]))
        ff_y = on_y.send(after(ff_parts[1], c_pieces[3], c_pieces[4]))
    pre_own, pre_peer, part_gn, *send_gn, ff_w = call(
        functools.partial(contract_kernel, c_copies, len(c_pieces)),
        "contract",
        meta,
        vm(slope_own, slope_peer, low, low_peer, in_w, *c_pieces),
        [((size, part_ff), BF16, "v")] * 2
        + [((size, width), F32, "v")]
        + [((size, width // 3), BF16, "v")] * 3
        + [((part_ff, width), BF16, "v")],
        deps=(ff_parts[0],),
    )
    in_parts = call(
        functools.partial(product_kernel, in_plan, len(in_outs)),
        "outer",
        meta,
        vm(normed_two, normed_two_peer, pre_own, pre_peer),
        in_outs,
        [shape_in],
    )
    in_parts = list(in_parts)
    last = in_parts[0]

    def turn(parts, by_x, by_y, *deps):
        h = parts[3].shape[0] // 2
        columns = parts[3].shape[1]
        to_y, to_x = call(
            turn_kernel,
            "turn",
            meta,
            vm(parts[2], by_x, parts[3], by_y),
            [((parts[2].shape[0] - h, columns), BF16, "v"), ((h, columns), BF16, "v")],
            deps=deps,
        )
        return on_y.send(to_y), on_x.send(to_x), to_y

    def add(a, b, *deps):
        (out,) = call(add_kernel, "add", meta, vm(a, b), [(a.shape, BF16, "v")], deps=deps)
        return out

    other_gn = [peer(v) for v in send_gn]
    grad_residual, low_mine, *low_given, grad_keep, grad_send, grad_gain_two = call(
        through_kernel,
        "through",
        meta,
        vm(residual, part_gn, *other_gn, out_cotangent, pool_cotangent, gain_two, out_half, out_other),
        [
            ((size, width), F32, "v"),
            ((size, half), BF16, "v"),
            ((size // 2, half), BF16, "v"),
            ((size // 2, half), BF16, "v"),
            ((size, half), BF16, "v"),
            ((size, half), BF16, "v"),
            ((1, width), F32, "v"),
        ],
        deps=(last,),
    )
    grad_got = peer(grad_send)
    last = grad_gain_two
    if fast:
        last_y, last_x, last = turn(ff_parts, ff_x, ff_y, last)
        ff_last = (last_y, last_x)
    head_rows = 8

    def halve_first(parts, by_x, by_y, last_y, last_x, *deps, extra=0):
        rows, columns = parts[3].shape
        keep, send = call(
            land_half_kernel,
            "land",
            meta,
            vm(parts[2], by_x, last_y, parts[3], by_y, last_x),
            [((rows // 2, columns + extra), BF16, "v")] * 2,
            deps=deps,
        )
        return keep, swap(send, "dp", nz, 1)

    def halve_next(keep, got, *deps, extra=0):
        rows, columns = keep.shape
        keep, send = call(
            functools.partial(halve_kernel, columns - extra),
            "halve",
            meta,
            vm(keep, got),
            [((rows // 2, columns), BF16, "v")] * 2,
            deps=deps,
        )
        return keep, swap(send, "dp", nz, 2)

    def quarter(keep, got, *deps):
        own = add(keep, got, *deps)
        return own, swap(own, "dp", nz, 1), swap(own, "dp", nz, 2)

    def quarters(own, by_low, by_high, *deps):
        return own, by_low, by_high, swap(after(by_high, *deps), "dp", nz, 1)

    def shards(four, *deps):
        columns = four[0].shape[1]
        return call(join_kernel, "join", meta, vm(*four), [((shard, columns), BF16, "v")] * 2, deps=deps)

    def attend_back(qkv, powers, g, att, sums, diag, name, *deps):
        return call(
            attend_back_kernel,
            name,
            meta,
            vm(qkv, powers, g, att, sums, diag),
            [((size, wide), BF16, "v"), ((head_rows, 2 * size), F32, "v")],
            [pltpu.VMEM((size, size), BF16), pltpu.VMEM((128, 2 * size), F32)],
            deps=deps,
        )

    diag = jnp.zeros((head_rows, 2 * size), F32)
    dqkv_own, diag = attend_back(
        qkv_own, powers_own, grad_keep, attended, sums_own, diag, "attend_back_own", last, grad_got
    )
    last = dqkv_own
    if fast:
        ff_keep, ff_one = halve_first(ff_parts, ff_x, ff_y, *ff_last, last)
        in_x = on_x.send(after(in_parts[0], dqkv_own))
        in_y = on_y.send(after(in_parts[1], dqkv_own))
        last = ff_keep
    dqkv_peer, diag = attend_back(
        qkv_peer, powers_peer, grad_got, given_att, sums_peer, diag, "attend_back_peer", last
    )
    last = diag
    if fast:
        ff_keep, ff_two = halve_next(ff_keep, ff_one, last)
        last = ff_keep
    got_att_peer = [peer(after(v, last)) for v in own_halves]
    if fast:
        at_plan = message_plan(2 * shard)
        at_plan = at_plan + [(n, 2 * shard, 16, 0, 0, width) for n in (0, 2)]
        at_outs = [((2 * shard + (16 if n in (0, 2) else 0), 4 * half), BF16, "v") for n in range(4)]
    else:
        at_plan = [(0, 0, width + 16, 0, 0, 0)]
        at_outs = [((width + 16, 4 * half), BF16, "v")]
    part_gh, *send_gh, small_grads = call(
        inputs_kernel,
        "inputs",
        meta,
        vm(dqkv_own, dqkv_peer, qkv_w, hidden_in, hidden_peer, grad_gain_two, diag, buckets),
        [((size, width), F32, "v")] + [((size, half), BF16, "v")] * 2 + [((16, 128), F32, "v")],
        [pltpu.VMEM((1, width), F32)],
        deps=(last,),
    )
    low_other = [peer(after(v, part_gh, *got_att_peer)) for v in low_given]
    last = part_gh
    if fast:
        last_y, last_x, last = turn(in_parts, in_x, in_y, last)
        in_last = (last_y, last_x)
    at_parts = call(
        functools.partial(weights_kernel, at_plan, len(at_outs)),
        "weights",
        meta,
        vm(
            normed,
            normed_peer,
            dqkv_own,
            dqkv_peer,
            attended,
            *got_att,
            given_att,
            *got_att_peer,
            low_mine,
            *low_other,
            small_grads,
        ),
        at_outs,
        [pltpu.VMEM((width + 16, 4 * half), BF16)],
        deps=(last,),
    )
    at_parts = list(at_parts)
    last = at_parts[0]
    if fast:
        at_x = on_x.send(at_parts[0])
        at_y = on_y.send(at_parts[1])
        in_keep, in_one = halve_first(in_parts, in_x, in_y, *in_last, last)
        last = in_keep
    other_gh = [peer(after(v, last)) for v in send_gh]
    part_branch, *send_branch = call(
        output_kernel,
        "output",
        meta,
        vm(act_own, act_peer, ff_w),
        [((size, width), F32, "v")] + [((size, half), BF16, "v")] * 2,
        deps=(last,),
    )
    last = part_branch
    (grad_hidden,) = call(
        hidden_kernel,
        "hidden",
        meta,
        vm(hidden_in, grad_residual, part_gh, *other_gh, gain_one),
        [((size, width), F32, "v")],
        deps=(last,),
    )
    last = grad_hidden

    if fast:
        ff_four = quarter(ff_keep, ff_two, last)
        last_y, last_x, last = turn(at_parts, at_x, at_y, ff_four[0])
        at_last = (last_y, last_x)
        in_keep, in_two = halve_next(in_keep, in_one, last)
        ff_four = quarters(*ff_four, in_keep)
        at_keep, at_one = halve_first(at_parts, at_x, at_y, *at_last, in_keep, extra=128)
        in_four = quarter(in_keep, in_two, at_keep)
        (grad_ffout,) = call(
            join_rows_kernel,
            "join_rows",
            meta,
            vm(*ff_four),
            [((block, width), F32, "v")],
            deps=(in_four[0],),
        )
        last = grad_ffout
        other_branch = [peer(after(v, last)) for v in send_branch]
    else:
        other_branch = [peer(v) for v in send_branch]
    hidden_out, pooled, stats = call(
        finish_kernel,
        "finish",
        meta,
        vm(residual, part_branch, *other_branch, sums),
        [((size, width), BF16, "v"), ((1, width), F32, "v"), ((1, width), F32, "v")],
        deps=(last,),
    )
    last = stats
    if fast:
        at_keep, at_two = halve_next(at_keep, at_one, last, extra=128)
        in_four = quarters(*in_four, at_keep)
        mine_in, other_in = shards(in_four, at_keep)
        got_in = peer(other_in)
        own_at, small_grads = call(
            last_kernel,
            "last",
            meta,
            vm(at_keep, at_two),
            [((shard // 2, 4 * half), BF16, "v"), ((16, 128), F32, "v")],
            deps=(mine_in,),
        )
        at_four = own_at, swap(own_at, "dp", nz, 1), swap(own_at, "dp", nz, 2)
        small_grads = small_grads + peer(small_grads)
        (grad_in,) = call(
            functools.partial(weave_in_kernel, block),
            "weave_in",
            meta,
            vm(mine_in, got_in),
            [((shard, full_ff), F32, "v")],
            deps=(own_at,),
        )
        at_four = quarters(*at_four, grad_in)
        mine_at, other_at = shards(at_four, small_grads)
        got_at = peer(other_at)
        grad_at = call(
            weave_at_kernel, "weave_at", meta, vm(mine_at, got_at), [((shard, width), F32, "v")] * 4
        )
    else:

        def reduced(v):
            v = lax.psum_scatter(v, "fsdp", scatter_dimension=0, tiled=True)
            return lax.psum(v, "dp").astype(F32)

        def spread(v, axis):
            none = jnp.zeros_like(v)
            return by_core(jnp.stack([v, none], axis), jnp.stack([none, v], axis))

        grad_ffout = reduced(
            spread(ff_parts[0].reshape(nf // 2, block, width), 1).reshape(full_ff, width)
        )
        grad_in = reduced(
            spread(in_parts[0].reshape(width, nf // 2, block), 2).reshape(width, full_ff)
        )
        grads = spread(at_parts[0][:width].reshape(width, 4, half), 2).reshape(width, 4 * width)
        grads = reduced(grads)
        grad_at = [grads[:, n * width : (n + 1) * width] for n in range(4)]
        small_grads = lax.psum(small_grads, ("fsdp", "dp"))

    count = width // 128
    rows = levels // nf
    table = small_grads[2 * count :].reshape(-1)[: heads * levels].reshape(heads, levels)
    grad_table = lax.dynamic_slice_in_dim(table, me * rows, rows, 1).T
    gains = small_grads[: 2 * count].reshape(2, width)
    gains = lax.dynamic_slice_in_dim(gains, me * shard, shard, 1)
    return (
        hidden_out,
        pooled,
        grad_hidden,
        gains[0],
        grad_at[0],
        grad_at[1],
        grad_at[2],
        grad_at[3],
        grad_table,
        gains[1],
        grad_in,
        grad_ffout,
        stats[:, :3],
    )


def solution(mesh):
    token = P(("fsdp", "dp"), None)
    weight = P("fsdp", None)
    return jax.shard_map(
        functools.partial(body, mesh.shape["fsdp"], mesh.shape["dp"]),
        mesh=mesh,
        in_specs=(
            token,
            P("fsdp"),
            weight,
            weight,
            weight,
            weight,
            weight,
            P("fsdp"),
            weight,
            weight,
            P(),
            P(("fsdp", "dp")),
            P(("fsdp", "dp")),
            token,
            token,
        ),
        out_specs=(
            token,
            token,
            token,
            P("fsdp"),
            weight,
            weight,
            weight,
            weight,
            weight,
            P("fsdp"),
            weight,
            weight,
            token,
        ),
        check_vma=False,
    )
```

```python
import functools
import math

import jax
import jax.numpy as jnp
from jax import lax
from jax.experimental import pallas as pl
from jax.experimental.pallas import tpu as pltpu
from jax.sharding import PartitionSpec as P

EPS = 1e-06
F32 = jnp.float32
BF16 = jnp.bfloat16
VMEM_SPARE = 6 * 2**20
WEIGHTS = {"turn": 30.0, "expand_own": 30.0}
GELU_A = 0.7978845608028654
GELU_B = 0.044715


def dot(a, b):
    return lax.dot_general(a, b, (((1,), (0,)), ((), ())), preferred_element_type=F32)


def dot_right(a, b):
    return lax.dot_general(a, b, (((1,), (1,)), ((), ())), preferred_element_type=F32)


def dot_left(a, b):
    return lax.dot_general(a, b, (((0,), (0,)), ((), ())), preferred_element_type=F32)


def iota(shape, dim):
    return lax.broadcasted_iota(jnp.int32, shape, dim)


def call(kernel, name, meta, ins, outs, scratch=(), deps=(), limit=0):
    spaces = {"v": pltpu.VMEM, "s": pltpu.SMEM, "h": pl.ANY}
    held = [(a.shape, a.dtype) for a, m in ins if m == "v"]
    held += [(s, d) for s, d, m in outs if m == "v"]
    held += [(x.shape, x.dtype) for x in scratch if x.memory_space == pltpu.VMEM]
    need = sum(math.prod(s) * jnp.dtype(d).itemsize for s, d in held)
    ins = [(after(meta, *deps), "s")] + list(ins)
    return pl.pallas_call(
        kernel,
        name=name,
        out_shape=[jax.ShapeDtypeStruct(s, d) for s, d, _ in outs],
        in_specs=[pl.BlockSpec(memory_space=spaces[m]) for _, m in ins],
        out_specs=[pl.BlockSpec(memory_space=spaces[m]) for _, _, m in outs],
        scratch_shapes=list(scratch),
        compiler_params=pltpu.CompilerParams(vmem_limit_bytes=max(limit, need + VMEM_SPARE)),
        cost_estimate=pl.CostEstimate(
            flops=1000, bytes_accessed=int(3.7e6 * WEIGHTS.get(name, 0.0)) + 1000, transcendentals=0
        ),
    )(*[a for a, _ in ins])


def after(v, *deps):
    return lax.optimization_barrier((v,) + deps)[0] if deps else v


def place(meta, pieces, targets, copies):
    for src, row, rows, from_column, dst, base, column, width, unit, far, side in copies:
        start = base
        if unit:
            start = base + unit * jnp.bitwise_xor(meta[1], far)
            if side == 1:
                start = start + (unit // 2) * meta[2]
            if side == 2:
                start = start + (unit // 2) * (1 - meta[2])
            start = pl.multiple_of(start, 16)
        targets[dst][pl.ds(start, rows), column : column + width] = pieces[src][
            row : row + rows, from_column : from_column + width
        ]


def rows_loop(count, step, fn):
    def one(i, carry):
        fn(pl.ds(pl.multiple_of(i * step, step), step))
        return carry

    lax.fori_loop(0, count // step, one, 0)


def scatter_out(meta, scratch, outs, plan):
    for dst, row, rows, unit, far, offset in plan:
        start = offset
        if unit:
            start = pl.multiple_of(offset + unit * jnp.bitwise_xor(meta[1], far), 16)
        outs[dst][row : row + rows, :] = scratch[pl.ds(start, rows), :]


def small_block(meta, gain_one, gain_two, rel):
    row, lane = iota((16, 128), 0), iota((16, 128), 1)
    block = jnp.where((row == 2) & (lane == 0), (meta[4] // 256).astype(F32), 0.0)
    block = jnp.where((row == 2) & (lane == 1), (meta[4] % 256).astype(F32), block)
    parts = [(0, gain_one), (1, gain_two)] + [(4 + n, rel[n : n + 1, :]) for n in range(rel.shape[0])]
    for at, value in parts:
        value = value[...].astype(F32)
        wide = jnp.concatenate([value, jnp.zeros((1, 128 - value.shape[1]), F32)], axis=1)
        block = jnp.where(row == at, wide, block)
    return block.astype(BF16)


def pack_kernel(n_chips, meta, *refs):
    sources = refs[:5]
    gain_one, gain_two, rel = refs[5:8]
    kept_a, given_a, kept_b, given_b = refs[8:12]
    held, sems = refs[12:17], refs[17]
    handles = [pltpu.make_async_copy(a, b, sems.at[n]) for n, (a, b) in enumerate(zip(sources, held))]
    for handle in handles:
        handle.start()
    width = 4 * (held[0].shape[1] // 2)
    block = small_block(meta, gain_one, gain_two, rel)
    for out in (kept_a, given_a):
        out[:, width:] = jnp.zeros((out.shape[0], 128), BF16)
        out[0:16, width:] = block
    for handle in handles:
        handle.wait()
    wq, wk, wv, wo, w_in = held
    core = meta[2]
    half = wq.shape[1] // 2
    block = w_in.shape[1] // (2 * n_chips)
    for which, a_ref, b_ref in ((core, kept_a, kept_b), (1 - core, given_a, given_b)):
        for n, w in enumerate((wq, wk, wv, wo)):
            cols = pl.ds(pl.multiple_of(which * half, 128), half)
            a_ref[:, n * half : (n + 1) * half] = w[:, cols]
        for n in range(b_ref.shape[1] // block):
            cols = pl.ds(pl.multiple_of((2 * n + which) * block, 128), block)
            b_ref[:, n * block : (n + 1) * block] = w_in[:, cols]


def stack_kernel(meta, kept, taken, both):
    shard = kept.shape[0]
    both[pl.ds(pl.multiple_of(shard * meta[2], 16), shard), :] = kept[...]
    both[pl.ds(pl.multiple_of(shard * (1 - meta[2]), 16), shard), :] = taken[...]


def cut_kernel(meta, by_x, by_y, upper, lower):
    h = upper.shape[0]
    upper[...] = by_x[:h, :]
    lower[...] = by_y[h:, :]


def low_kernel(meta, out_cot, pool_cot, low):
    size = low.shape[0]
    length, prefix = meta[4], meta[5]
    count = (length - prefix).astype(F32)

    def lows(ds):
        t = iota((256, 1), 0) + ds.start
        pool = jnp.where((t >= prefix) & (t < length), 1.0, 0.0) / count
        low[ds, :] = (out_cot[ds, :].astype(F32) + pool * pool_cot[...]).astype(BF16)

    rows_loop(size, 256, lows)


def prepare_kernel(copies, n_pieces, levels, meta, hidden, hidden_peer, buckets, *refs):
    pieces = refs[:n_pieces]
    normed, normed_peer, bias, gain_one, gain_two, length_peer = refs[n_pieces : n_pieces + 6]
    rest = refs[n_pieces + 6 :]
    if copies:
        qkv, w_half, table, table_rows = rest
        place(meta, pieces, (qkv, w_half), copies)
        count = n_pieces
        column = pieces[0].shape[1] - 128
        blocks = [ref[0:16, column:].astype(F32) for ref in pieces]
        places = [jnp.bitwise_xor(meta[0], 2 * (p % 4) + p // 4) for p in range(count)]
    else:
        table, table_rows = rest
        count = pieces[0].shape[0] // 16
        blocks = [pieces[0][16 * p : 16 * p + 16, :].astype(F32) for p in range(count)]
        places = [jnp.int32(p) for p in range(count)]
    size, width = hidden.shape
    shard = width // count
    some = levels // count
    table[...] = jnp.zeros_like(table)
    first = jnp.zeros((1, width), F32)
    second = jnp.zeros((1, width), F32)
    rest = jnp.zeros((1, width - 128), F32)
    peers = jnp.zeros((1, 1), F32)
    for where, piece in zip(places, blocks):
        first += pltpu.roll(jnp.concatenate([piece[0:1], rest], axis=1), shard * where, 1)
        second += pltpu.roll(jnp.concatenate([piece[1:2], rest], axis=1), shard * where, 1)
        length = 256.0 * piece[2:3, 0:1] + piece[2:3, 1:2]
        peers += jnp.where(where == jnp.bitwise_xor(meta[0], 1), length, 0.0)
        for b in range(some):
            table[pl.ds(some * where + b, 1), :] = piece[4 + b : 5 + b]
    length_peer[...] = jnp.broadcast_to(peers, (1, 128))
    gain_one[...] = first
    gain_two[...] = second

    for x_ref, n_ref in ((hidden, normed), (hidden_peer, normed_peer)):

        def rows(ds, x_ref=x_ref, n_ref=n_ref):
            x = x_ref[ds, :].astype(F32)
            inv = lax.rsqrt(jnp.mean(x * x, axis=-1, keepdims=True) + EPS)
            n_ref[ds, :] = (x * inv * gain_one[...]).astype(BF16)

        rows_loop(size, 256, rows)

    span = 2 * size
    hot = (buckets[...] == iota((levels, span), 0)).astype(BF16)
    table_rows[...] = dot_left(table[...].astype(BF16), hot)
    heads, _, wide = bias.shape
    base = heads * meta[2]

    def head(h, carry):
        row = table_rows[pl.ds(base + h, 1), :]
        first = jnp.broadcast_to(pltpu.roll(row, span - 127, 1), (8, span))
        sub = iota((8, span), 0)
        full = first
        for k in range(1, 8):
            full = jnp.where(sub == k, pltpu.roll(first, k, 1), full)
        bias[h, 0:8, :] = full[:, :wide]
        have = 8
        while have < 128:
            more = pltpu.roll(full, have, 1)
            bias[h, have : 2 * have, :] = more[:, :wide]
            full = jnp.concatenate([full, more], axis=0)
            have *= 2
        return carry

    lax.fori_loop(0, heads, head, 0, unroll=True)


def attend_kernel(meta, x_ref, bias, w, length, qkv, out, upper, lower, powers, inv_sums, scores):
    size = x_ref.shape[0]
    part = w.shape[1] // 3
    pairs = part // 128
    lane = iota((1, 128), 1)
    half = lane < 64
    strips = size // 128
    inv_sums[...] = jnp.zeros_like(inv_sums)

    def project(ds):
        for n in range(3):
            cols = slice(n * part, (n + 1) * part)
            qkv[ds, cols] = dot(x_ref[ds, :], w[:, cols]).astype(BF16)

    rows_loop(size, size, project)
    masked = jnp.where(iota((size, 1), 0).astype(F32) < length[0:1, 0:1], 0.0, -1e30).astype(F32)

    def pair(p, carry):
        base = pl.multiple_of(p * 128, 128)
        qp = qkv[:, pl.ds(base, 128)].astype(F32)
        kp = qkv[:, pl.ds(base + part, 128)].astype(F32)
        vp = qkv[:, pl.ds(base + 2 * part, 128)].astype(F32)
        joined = None
        for side in range(2):
            head = 2 * p + side
            own = half if side == 0 else jnp.logical_not(half)
            spare = lane == (64 if side == 0 else 0)
            qa = jnp.where(own, qp, jnp.where(spare, 1.0, 0.0)).astype(BF16)
            ka = jnp.where(own, kp, jnp.where(spare, masked, 0.0)).astype(BF16)
            va = jnp.where(own, vp, jnp.where(spare, 1.0, 0.0)).astype(BF16)
            top = None
            for a in range(strips):
                rows = slice(128 * a, 128 * a + 128)
                off = 128 * (strips - 1 - a)
                s = dot_right(ka[rows], qa) + bias[head, :, off : off + size]
                scores[rows, :] = s
                peak = jnp.max(s, axis=0, keepdims=True)
                top = peak if top is None else jnp.maximum(top, peak)
            for a in range(strips):
                rows = slice(128 * a, 128 * a + 128)
                powers[head, rows, :] = jnp.exp(scores[rows, :] - top).astype(BF16)
            mixed = dot_left(va, powers[head]).T
            sums = jnp.sum(jnp.where(spare, mixed, 0.0), axis=1, keepdims=True)
            inv = 1.0 / sums
            inv_sums[...] = jnp.where(lane == head, inv, inv_sums[...])
            mixed = mixed * inv
            joined = mixed if side == 0 else jnp.where(half, joined, mixed)
        joined = joined.astype(BF16)
        cols = pl.ds(base, 128)
        out[:, cols] = joined
        upper[:, cols] = joined[: size // 2]
        lower[:, cols] = joined[size // 2 :]
        return carry

    lax.fori_loop(0, pairs, pair, 0, unroll=True)


def residual_kernel(meta, hidden, attended, upper, lower, gain, w_half, w_other, residual, normed, left, middle, right, sums, w_out):
    size, width = hidden.shape
    half = width // 2
    length = meta[4]
    core = meta[2]
    w_out[:, pl.ds(pl.multiple_of(core * half, 128), half)] = w_half[...]
    w_out[:, pl.ds(pl.multiple_of((1 - core) * half, 128), half)] = w_other[...]
    mine = pl.ds(pl.multiple_of(core * half, 128), half)
    other = pl.ds(pl.multiple_of((1 - core) * half, 128), half)
    sums[...] = jnp.zeros_like(sums)

    for first, got in ((0, upper), (size // 2, lower)):
        ds = slice(first, first + size // 2)
        x = hidden[ds, :].astype(F32)
        branch = dot(attended[ds, :], w_out[mine, :]) + dot(got[...], w_out[other, :])
        live = (iota((size // 2, 1), 0) + first) < length
        sums[0:1, :] += jnp.sum(jnp.where(live, x * x, 0.0), axis=0, keepdims=True)
        sums[1:2, :] += jnp.sum(jnp.where(live, branch * branch, 0.0), axis=0, keepdims=True)
        r = x + branch
        residual[ds, :] = r
        inv = lax.rsqrt(jnp.mean(r * r, axis=-1, keepdims=True) + EPS)
        value = (r * inv * gain[...]).astype(BF16)
        normed[ds, :] = value
        third = left.shape[1]
        for n, ref in enumerate((left, middle, right)):
            ref[ds, :] = value[:, n * third : (n + 1) * third]


def expand_kernel(copies, n_pieces, *refs):
    meta, x_ref = refs[:2]
    pieces = refs[2 : 2 + n_pieces]
    if copies:
        activated, slope, w_in = refs[2 + n_pieces :]
        place(meta, pieces, (w_in,), copies)
    else:
        w_in = pieces[0]
        activated, slope, whole = refs[2 + n_pieces :]
        third = x_ref.shape[1]
        for n, ref in enumerate((x_ref, *pieces[1:])):
            whole[:, n * third : (n + 1) * third] = ref[...]
        x_ref = whole
    chunk = 512 if w_in.shape[1] % 512 == 0 else 256

    def rows(ds):
        x = x_ref[ds, :]
        for c in range(0, w_in.shape[1], chunk):
            t = dot(x, w_in[:, c : c + chunk])
            square = t * t
            th = jnp.tanh(t * (GELU_A + (GELU_A * GELU_B) * square))
            phi = 0.5 + 0.5 * th
            activated[ds, c : c + chunk] = (t * phi).astype(BF16)
            inner = GELU_A + (3.0 * GELU_A * GELU_B) * square
            slope[ds, c : c + chunk] = (phi + 0.5 * t * (1.0 - th * th) * inner).astype(BF16)

    rows_loop(x_ref.shape[0], x_ref.shape[0], rows)


def product_kernel(plan, n_out, *refs):
    meta, left_own, left_peer, right_own, right_peer = refs[:5]
    outs = refs[5 : 5 + n_out]
    grads = refs[5 + n_out]
    step = 512 if grads.shape[0] % 512 == 0 else 256
    for c in range(0, grads.shape[0], step):
        part = dot_left(left_own[:, c : c + step], right_own[...])
        part += dot_left(left_peer[:, c : c + step], right_peer[...])
        grads[c : c + step, :] = part.astype(BF16)
    scatter_out(meta, grads, outs, plan)


def contract_kernel(copies, n_pieces, *refs):
    meta, slope_own, slope_peer, low_own, low_peer, w_in = refs[:6]
    pieces = refs[6 : 6 + n_pieces]
    pre_own, pre_peer, part_own, *sends, w_ffout = refs[6 + n_pieces :]
    third = sends[0].shape[1]
    place(meta, pieces, (w_ffout,), copies)
    size = low_own.shape[0]
    chunk = 512 if w_in.shape[1] % 512 == 0 else 256
    for slope, low, grad_pre, part in (
        (slope_peer, low_peer, pre_peer, sends),
        (slope_own, low_own, pre_own, (part_own,)),
    ):

        def rows(ds, slope=slope, low=low, grad_pre=grad_pre, part=part):
            y = low[ds, :]
            total = None
            for c in range(0, w_in.shape[1], chunk):
                g = dot_right(y, w_ffout[c : c + chunk, :])
                g = (slope[ds, c : c + chunk].astype(F32) * g).astype(BF16)
                grad_pre[ds, c : c + chunk] = g
                t = dot_right(g, w_in[:, c : c + chunk])
                total = t if total is None else total + t
            if len(part) > 1:
                for n, ref in enumerate(part):
                    ref[ds, :] = total[:, n * third : (n + 1) * third].astype(BF16)
            else:
                part[0][ds, :] = total

        rows_loop(size, size, rows)


def through_kernel(meta, residual, part, left, center, right, out_cot, pool_cot, gain, w_half, w_other,
                   grad_residual, low_mine, upper, lower, grad_keep, grad_send, grad_gain):
    size, width = residual.shape
    half = width // 2
    core = meta[2]
    mine = pl.ds(pl.multiple_of(core * half, 128), half)
    theirs = pl.ds(pl.multiple_of((1 - core) * half, 128), half)
    length, prefix = meta[4], meta[5]
    count = (length - prefix).astype(F32)
    grad_gain[...] = jnp.zeros_like(grad_gain)

    def rows(ds, low_given, start):
        x = residual[ds, :]
        gn = part[ds, :] + jnp.concatenate([left[ds, :], center[ds, :], right[ds, :]], axis=1).astype(F32)
        inv = lax.rsqrt(jnp.mean(x * x, axis=-1, keepdims=True) + EPS)
        u = gain[...] * gn
        xr = x * inv
        t = iota((256, 1), 0) + ds.start
        pool = jnp.where((t >= prefix) & (t < length), 1.0, 0.0) / count
        go = out_cot[ds, :].astype(F32) + pool * pool_cot[...]
        g = go + inv * (u - xr * jnp.mean(xr * u, axis=-1, keepdims=True))
        grad_gain[...] += jnp.sum(xr * gn, axis=0, keepdims=True)
        grad_residual[ds, :] = g
        first, second = g[:, :half].astype(BF16), g[:, half:].astype(BF16)
        on_first = jnp.broadcast_to(core == 0, first.shape)
        a = jnp.where(on_first, g[:, :half], g[:, half:]).astype(BF16)
        b = jnp.where(on_first, g[:, half:], g[:, :half]).astype(BF16)
        low_mine[ds, :] = a
        low_given[pl.ds(ds.start - start, 256), :] = b
        grad_keep[ds, :] = (dot_right(a, w_half[mine, :]) + dot_right(b, w_other[mine, :])).astype(BF16)
        grad_send[ds, :] = (dot_right(a, w_half[theirs, :]) + dot_right(b, w_other[theirs, :])).astype(BF16)

    middle = size // 2
    for first, low_given in ((0, upper), (middle, lower)):

        def some(i, carry, first=first, low_given=low_given):
            rows(pl.ds(pl.multiple_of(first + 256 * i, 256), 256), low_given, first)
            return carry

        lax.fori_loop(0, middle // 256, some, 0)


def attend_back_kernel(meta, qkv, powers, g_ref, a_ref, inv_sums, diag_in, out, diag, grads, slant):
    size = g_ref.shape[0]
    part = qkv.shape[1] // 3
    pairs = part // 128
    strips = size // 128
    span = 2 * size
    lane = iota((1, 128), 1)
    half = lane < 64
    diag[...] = diag_in[...]

    def pair(p, carry):
        base = pl.multiple_of(p * 128, 128)
        cols = pl.ds(base, 128)
        kcols = pl.ds(base + part, 128)
        vcols = pl.ds(base + 2 * part, 128)
        qp, kp = qkv[:, cols], qkv[:, kcols]
        vp = qkv[:, vcols].astype(F32)
        do = g_ref[:, cols].astype(F32)
        prod = do * a_ref[:, cols].astype(F32)
        dq_all = dk_all = dv_all = None
        for side in range(2):
            head = 2 * p + side
            own = half if side == 0 else jnp.logical_not(half)
            one = 64 if side == 0 else 0
            inv = jnp.sum(jnp.where(lane == head, inv_sums[...], 0.0), axis=1, keepdims=True)
            inner = jnp.sum(jnp.where(own, prod, 0.0), axis=1, keepdims=True) * inv
            upper = inner.astype(BF16).astype(F32)
            dos = jnp.where(
                own,
                do * inv,
                jnp.where(lane == one, -upper, jnp.where(lane == one + 1, upper - inner, 0.0)),
            ).astype(BF16)
            ones = (lane == one) | (lane == one + 1)
            va = jnp.where(own, vp, jnp.where(ones, 1.0, 0.0)).astype(BF16)
            slant[...] = jnp.zeros_like(slant)
            for a in range(strips):
                rows = slice(128 * a, 128 * a + 128)
                off = 128 * (strips - 1 - a)
                ds = (powers[head, rows, :].astype(F32) * dot_right(va[rows], dos)).astype(BF16)
                grads[rows, :] = ds
                slant[:, off : off + size] += ds.astype(F32)
            dk = dot(grads[...], qp)
            dv = dot(powers[head], dos)
            dk_all = dk if side == 0 else jnp.where(half, dk_all, dk)
            dv_all = dv if side == 0 else jnp.where(half, dv_all, dv)
            dq = dot_left(kp, grads[...]).T
            dq_all = dq if side == 0 else jnp.where(half, dq_all, dq)
            y = slant[...]
            rest = 64
            while rest >= 1:
                y = y[:rest] + pltpu.roll(y[rest:], span - rest, 1)
                rest //= 2
            diag[pl.ds(head, 1), :] += pltpu.roll(y, 127, 1)
        out[:, cols] = dq_all.astype(BF16)
        out[:, kcols] = dk_all.astype(BF16)
        out[:, vcols] = dv_all.astype(BF16)
        return carry

    lax.fori_loop(0, pairs, pair, 0, unroll=True)


def weights_kernel(plan, n_out, *refs):
    meta, x_own, x_peer, dqkv_own, dqkv_peer, att_own, upper, lower, att_peer, got_upper, got_lower, low_own, low_upper, low_lower, small = refs[:15]
    outs = refs[15 : 15 + n_out]
    (grads,) = refs[15 + n_out :]
    middle = upper.shape[0]
    part = dqkv_own.shape[1]
    depth = x_own.shape[1]
    half = depth // 2
    for c in range(0, depth, 384):
        cols = slice(c, c + 384)
        g = dot_left(x_own[:, cols], dqkv_own[...]) + dot_left(x_peer[:, cols], dqkv_peer[...])
        grads[cols, 0:part] = g.astype(BF16)
    core = meta[2]
    mine = pl.multiple_of(core * half, 16)
    theirs = pl.multiple_of((1 - core) * half, 16)
    for c in range(0, half, 384):
        cols = slice(c, c + 384)
        g = dot_left(att_own[:, cols], low_own[...]) + dot_left(att_peer[:middle, cols], low_upper[...])
        g += dot_left(att_peer[middle:, cols], low_lower[...])
        grads[pl.ds(mine + c, 384), part:] = g.astype(BF16)
        g = dot_left(upper[:, cols], low_own[:middle]) + dot_left(lower[:, cols], low_own[middle:])
        g += dot_left(got_upper[:, cols], low_upper[...])
        g += dot_left(got_lower[:, cols], low_lower[...])
        grads[pl.ds(theirs + c, 384), part:] = g.astype(BF16)
    grads[depth:, :] = jnp.zeros((16, grads.shape[1]), BF16)
    grads[depth:, 0:128] = small[...].astype(BF16)
    scatter_out(meta, grads, outs, plan)


def inputs_kernel(meta, dqkv_own, dqkv_peer, w, hidden, hidden_peer, gain_two, diag, buckets,
                  part_own, left, right, small, gain_one):
    size, width = part_own.shape
    half = width // 2
    small[...] = jnp.zeros_like(small)
    gain_one[...] = jnp.zeros_like(gain_one)

    def share(x_ref, ds, value):
        x = x_ref[ds, :].astype(F32)
        inv = lax.rsqrt(jnp.mean(x * x, axis=-1, keepdims=True) + EPS)
        gain_one[...] += jnp.sum(x * inv * value, axis=0, keepdims=True)

    def peers(ds):
        value = dot_right(dqkv_peer[ds, :], w[...])
        share(hidden_peer, ds, value)
        value = value.astype(BF16)
        left[ds, :] = value[:, :half]
        right[ds, :] = value[:, half:]

    def own(ds):
        value = dot_right(dqkv_own[ds, :], w[...])
        share(hidden, ds, value)
        part_own[ds, :] = value

    rows_loop(size, size, peers)
    rows_loop(size, size, own)
    count = width // 128
    for n in range(count):
        small[n : n + 1, :] = gain_one[:, 128 * n : 128 * n + 128]
        small[count + n : count + n + 1, :] = gain_two[:, 128 * n : 128 * n + 128]
    hot = (buckets[...] == iota((128, diag.shape[1]), 0)).astype(F32)
    table = lax.dot_general(
        diag[...],
        hot,
        (((1,), (1,)), ((), ())),
        preferred_element_type=F32,
        precision=lax.Precision.HIGHEST,
    )
    lane = iota((1, 128), 1)
    few = (16 - 2 * count) * 2 - 2
    for n in range(few):
        head = few * meta[2] + n
        row = jnp.where(lane < 32, table[n : n + 1, :], 0.0)
        small[pl.ds(2 * count + head // 4, 1), :] += pltpu.roll(row, 32 * (head % 4), 1)


def hidden_kernel(meta, hidden, grad_residual, part, left, right, gain, grad_hidden):
    def rows(ds):
        total = part[ds, :] + jnp.concatenate([left[ds, :], right[ds, :]], axis=1).astype(F32)
        x = hidden[ds, :].astype(F32)
        inv = lax.rsqrt(jnp.mean(x * x, axis=-1, keepdims=True) + EPS)
        u = gain[...] * total
        xr = x * inv
        grad_hidden[ds, :] = grad_residual[ds, :] + inv * (
            u - xr * jnp.mean(xr * u, axis=-1, keepdims=True)
        )

    rows_loop(hidden.shape[0], 256, rows)


def output_kernel(meta, act_own, act_peer, w_ffout, part_own, left, right):
    size, width = part_own.shape
    half = width // 2

    def peers(ds):
        value = dot(act_peer[ds, :], w_ffout[...]).astype(BF16)
        left[ds, :] = value[:, :half]
        right[ds, :] = value[:, half:]

    def own(ds):
        part_own[ds, :] = dot(act_own[ds, :], w_ffout[...])

    rows_loop(size, size, peers)
    rows_loop(size, size, own)


def finish_kernel(meta, residual, part, left, right, sums, hidden_out, pooled, stats):
    size, width = residual.shape
    length, prefix = meta[4], meta[5]
    count = (length - prefix).astype(F32)
    pooled[...] = jnp.zeros_like(pooled)
    stats[...] = jnp.zeros_like(stats)

    def rows(ds):
        branch = part[ds, :] + jnp.concatenate([left[ds, :], right[ds, :]], axis=1).astype(F32)
        out = residual[ds, :] + branch
        hidden_out[ds, :] = out.astype(BF16)
        t = iota((128, 1), 0) + ds.start
        live = t < length
        stats[0:1, :] += jnp.sum(jnp.where(live, branch * branch, 0.0), axis=0, keepdims=True)
        pooled[...] += jnp.sum(jnp.where((t >= prefix) & live, out, 0.0), axis=0, keepdims=True)

    rows_loop(size, 128, rows)
    pooled[...] = pooled[...] / count
    total = jnp.sum(stats[0:1, :])
    first = jnp.sum(sums[0:1, :])
    second = jnp.sum(sums[1:2, :])
    denominator = length.astype(F32) * width
    column = iota(stats.shape, 1)
    values = jnp.where(column == 0, first, jnp.where(column == 1, second, total))
    stats[...] = jnp.sqrt(values / denominator)


def total(*parts):
    value = parts[0].astype(F32)
    for part in parts[1:]:
        value = value + part.astype(F32)
    return value.astype(BF16)


def turn_kernel(meta, keep_a, got_x, keep_b, got_y, on_y, on_x):
    h = on_x.shape[0]
    on_y[...] = total(keep_a[h:], got_x[h:])
    on_x[...] = total(keep_b[h:], got_y[h:])


def add_kernel(meta, a, b, out):
    out[...] = total(a[...], b[...])


def land_half_kernel(meta, keep_a, got_x, last_y, keep_b, got_y, last_x, keep, send):
    h, width = last_x.shape
    upper = total(keep_a[:h], got_x[:h], last_y[:h])
    lower = total(keep_b[:h], got_y[:h], last_x[...])
    first = jnp.broadcast_to(meta[3] % 2 == 0, upper.shape)
    keep[:, :width] = jnp.where(first, upper.astype(F32), lower.astype(F32)).astype(BF16)
    send[:, :width] = jnp.where(first, lower.astype(F32), upper.astype(F32)).astype(BF16)
    if keep.shape[1] > width:
        rows = slice(2 * h, 2 * h + 16)
        small = total(keep_a[rows, 0:128], got_x[rows, 0:128], last_y[h:, 0:128])
        for out in (keep, send):
            out[:, width:] = jnp.zeros((h, 128), BF16)
            out[:16, width:] = small


def halve_kernel(width, meta, a, b, keep, send):
    h = keep.shape[0]
    place_at = pl.multiple_of(h * (meta[3] // 2), 16)
    other_at = pl.multiple_of(h * (1 - meta[3] // 2), 16)
    keep[:, :width] = total(a[pl.ds(place_at, h), :width], b[pl.ds(place_at, h), :width])
    send[:, :width] = total(a[pl.ds(other_at, h), :width], b[pl.ds(other_at, h), :width])
    if width < keep.shape[1]:
        extra = total(a[:h, width:], b[:h, width:])
        keep[:, width:] = extra
        send[:, width:] = extra


def last_kernel(meta, a, b, out, small):
    width = out.shape[1]
    out[...] = total(a[:, :width], b[:, :width])
    small[...] = a[:16, width:].astype(F32) + b[:16, width:].astype(F32)


def join_rows_kernel(meta, own, by_low, by_high, by_both, out):
    h = own.shape[0]
    low, high = meta[3] % 2, meta[3] // 2
    for value, at_low, at_high in (
        (own, low, high),
        (by_low, 1 - low, high),
        (by_high, low, 1 - high),
        (by_both, 1 - low, 1 - high),
    ):
        out[pl.ds(pl.multiple_of(h * (2 * at_low + at_high), 16), h), :] = value[...].astype(F32)


def join_kernel(meta, own, by_low, by_high, by_both, mine, other):
    h = own.shape[0]
    low, high = meta[3] % 2, meta[3] // 2
    for value, at_low, at_high in (
        (own, low, high),
        (by_low, 1 - low, high),
        (by_high, low, 1 - high),
        (by_both, 1 - low, 1 - high),
    ):
        rows = pl.ds(pl.multiple_of(h * at_high, 16), h)

        @pl.when(at_low == meta[2])
        def _(value=value, rows=rows):
            mine[rows, :] = value[...]

        @pl.when(at_low != meta[2])
        def _(value=value, rows=rows):
            other[rows, :] = value[...]


def weave_in_kernel(block, meta, mine, other, out):
    for which, ref in ((meta[2], mine), (1 - meta[2], other)):
        for n in range(ref.shape[1] // block):
            cols = pl.ds(pl.multiple_of((2 * n + which) * block, 128), block)
            out[:, cols] = ref[:, n * block : (n + 1) * block].astype(F32)


def weave_at_kernel(meta, mine, other, *outs):
    half = outs[0].shape[1] // 2
    for which, ref in ((meta[2], mine), (1 - meta[2], other)):
        cols = pl.ds(pl.multiple_of(which * half, 128), half)
        for n, out in enumerate(outs):
            out[:, cols] = ref[:, n * half : (n + 1) * half].astype(F32)


def swap(v, axis, count, far):
    return lax.ppermute(v, axis, [(i, i ^ far) for i in range(count)])


def message_plan(unit):
    h = unit // 2
    plan = []
    for dst, (near, far) in enumerate(((1, 3), (2, 3), (0, 2), (0, 1))):
        offset = 0 if dst in (0, 2) else h
        plan.append((dst, 0, h, unit, near, offset))
        plan.append((dst, h, h, unit, far, offset))
    return plan


class Link:
    def __init__(self, far):
        self.far = far
        self.sent = []

    def send(self, v):
        if len(self.sent) >= 2:
            v = after(v, self.sent[-2])
        got = swap(v, "fsdp", 8, self.far)
        self.sent.append(got)
        return got


def body(
    nf,
    nz,
    hidden_in,
    norm_gain_attn,
    w_query,
    w_key,
    w_value,
    w_out,
    rel_bias,
    norm_gain_ffn,
    w_in,
    w_ffout,
    bucket_index,
    row_lengths,
    prefix_lengths,
    out_cotangent,
    pool_cotangent,
):
    fast = nf == 8 and nz == 4
    size, width = hidden_in.shape
    shard = w_query.shape[0]
    heads = rel_bias.shape[1]
    levels = rel_bias.shape[0] * nf
    full_ff = w_in.shape[1]
    part_ff = full_ff // 2
    block = w_ffout.shape[0]
    half = width // 2
    few = heads // 2
    me = lax.axis_index("fsdp").astype(jnp.int32)
    where = lax.axis_index("dp").astype(jnp.int32)
    core = me & 1
    zero = jnp.zeros((), jnp.int32)

    def by_core(first, second):
        return jnp.where(core == 0, first, second)

    def peer(v):
        return swap(v, "fsdp", nf, 1)

    def dma(n):
        return pltpu.SemaphoreType.DMA((n,))

    def vm(*arrays):
        return [(a, "v") for a in arrays]

    meta = jnp.stack([me, me >> 1, core, where, row_lengths[0], prefix_lengths[0], zero, zero])
    hidden_peer = peer(hidden_in)
    wide = 3 * half
    buckets = jnp.concatenate([bucket_index[::-1], jnp.full((1,), -1, jnp.int32)])[None, :]

    if fast:
        kept_a, given_a, kept_b, given_b = call(
            functools.partial(pack_kernel, nf // 2),
            "pack",
            meta,
            [(a, "h") for a in (w_query, w_key, w_value, w_out, w_in)]
            + vm(norm_gain_attn[None], norm_gain_ffn[None], rel_bias),
            [((shard, 4 * half + 128), BF16, "v")] * 2 + [((shard, part_ff), BF16, "v")] * 2,
            [pltpu.VMEM(w.shape, BF16) for w in (w_query, w_key, w_value, w_out, w_in)] + [dma(5)],
            limit=56 * 2**20,
        )
        on_x, on_y = Link(2), Link(4)
        taken_a = peer(given_a)
        x_kept, y_taken = on_x.send(kept_a), on_y.send(taken_a)
        x_taken, y_kept = on_x.send(taken_a), on_y.send(kept_a)
        far_kept, far_taken = on_y.send(x_kept), on_x.send(y_taken)
        a_pieces = [kept_a, x_kept, y_kept, far_kept, taken_a, x_taken, y_taken, far_taken]
        a_copies = []
        for number in range(8):
            far, side = number % 4, 1 + number // 4
            a_copies.append((number, 0, shard, 0, 0, 0, 0, wide, 2 * shard, far, side))
            a_copies.append((number, 0, shard, wide, 1, 0, 0, half, 2 * shard, far, side))
        taken_b = peer(after(given_b, hidden_peer, taken_a))
        (both_b,) = call(
            stack_kernel,
            "stack",
            meta,
            vm(kept_b, taken_b),
            [((2 * shard, part_ff), BF16, "v")],
        )

        def near(v):
            return [v, on_x.send(v), on_y.send(v)]

        def distant(three, *deps):
            v, by_x, by_y = three
            h = v.shape[0] // 2
            upper, lower = call(
                cut_kernel, "cut", meta, vm(by_x, by_y), [((h, v.shape[1]), BF16, "v")] * 2, deps=deps
            )
            far_y, far_x = on_y.send(upper), on_x.send(lower)
            return three + [far_y, far_x]

        def rows_of(five):
            h = five[3].shape[0]
            return zip(five, (0, 0, 0, 0, h), (0, 1, 2, 3, 3))

    else:

        def whole(v):
            return lax.all_gather(v, "fsdp", axis=0, tiled=True)

        a_full = [whole(w) for w in (w_query, w_key, w_value, w_out)]
        a_full = [by_core(w[:, :half], w[:, half:]) for w in a_full]
        qkv_w, out_half = jnp.concatenate(a_full[:3], axis=1), a_full[3]
        b_full = whole(w_in).reshape(width, nf // 2, 2, block)
        b_pieces = [by_core(b_full[:, :, 0], b_full[:, :, 1]).reshape(width, part_ff)]
        b_copies = [(0, 0, width, 0, 0, 0, 0, part_ff, 0, 0, 0)]
        c_full = whole(w_ffout).reshape(nf // 2, 2, block, width)
        c_pieces = [by_core(c_full[:, 0], c_full[:, 1]).reshape(part_ff, width)]
        c_copies = [(0, 0, part_ff, 0, 0, 0, 0, width, 0, 0, 0)]
        length = row_lengths[0]
        split = jnp.stack([length // 256, length % 256]).astype(BF16)[None]
        rows = [norm_gain_attn[None], norm_gain_ffn[None], split, split, rel_bias]
        rows = [jnp.pad(r, ((0, 0), (0, 128 - r.shape[1]))) for r in rows]
        small = jnp.concatenate(rows, axis=0)
        a_pieces, a_copies = [whole(jnp.pad(small, ((0, 16 - small.shape[0]), (0, 0))))], ()

    (low,) = call(
        low_kernel, "low", meta, vm(out_cotangent, pool_cotangent), [((size, width), BF16, "v")]
    )
    normed, normed_peer, bias, gain_one, gain_two, length_peer, *weights = call(
        functools.partial(prepare_kernel, a_copies, len(a_pieces), levels),
        "prepare",
        meta,
        vm(hidden_in, hidden_peer, buckets, *a_pieces),
        [
            ((size, width), BF16, "v"),
            ((size, width), BF16, "v"),
            ((few, 128, 2 * size - 128), F32, "v"),
            ((1, width), F32, "v"),
            ((1, width), F32, "v"),
            ((1, 128), F32, "v"),
        ]
        + ([((width, wide), BF16, "v"), ((width, half), BF16, "v")] if fast else []),
        [pltpu.VMEM((levels, 128), F32), pltpu.VMEM((128, 2 * size), F32)],
        deps=(low,),
    )
    if fast:
        b_pieces = near(both_b)
        qkv_w, out_half = weights
    out_other = peer(out_half)

    def attend(x, length, name, *deps):
        return call(
            attend_kernel,
            name,
            meta,
            vm(x, bias, qkv_w, length),
            [
                ((size, wide), BF16, "v"),
                ((size, half), BF16, "v"),
                ((size // 2, half), BF16, "v"),
                ((size // 2, half), BF16, "v"),
                ((few, size, size), BF16, "v"),
                ((size, 128), F32, "v"),
            ],
            [pltpu.VMEM((size, size), F32)],
            deps=deps,
        )

    qkv_peer, given_att, *given_halves, powers_peer, sums_peer = attend(
        normed_peer, length_peer, "attend_peer"
    )
    low_peer = peer(after(low, given_att))
    if fast:
        b_pieces = distant(b_pieces, given_att)
        b_copies = [
            (number, 0, piece.shape[0], 0, 0, row, 0, part_ff, 2 * shard, far, 0)
            for number, (piece, row, far) in enumerate(rows_of(b_pieces))
        ]
        c_pieces = near(w_ffout)
    served = tuple(b_pieces[n] for n in (1, 2)) if fast else ()
    length_own = jnp.broadcast_to(row_lengths.astype(F32)[None], (1, 128))
    qkv_own, attended, *own_halves, powers_own, sums_own = attend(
        normed, length_own, "attend_own", given_att, out_other, *served
    )
    served = tuple(b_pieces[n] for n in (3, 4)) if fast else ()
    got_att = [peer(after(v, attended, *served)) for v in given_halves]
    residual, normed_two, *thirds, sums = call(
        residual_kernel,
        "residual",
        meta,
        vm(hidden_in, attended, *got_att, gain_two, out_half, out_other),
        [((size, width), F32, "v"), ((size, width), BF16, "v")]
        + [((size, width // 3), BF16, "v")] * 3
        + [((8, width), F32, "v")],
        [pltpu.VMEM((width, width), BF16)],
        deps=(low_peer,),
    )
    thirds = [peer(v) for v in thirds]
    shape_in = pltpu.VMEM((width, part_ff), BF16)
    shape_ff = pltpu.VMEM((part_ff, width), BF16)
    if fast:
        ff_plan, in_plan = message_plan(block), message_plan(2 * shard)
        ff_outs = [((block, width), BF16, "v")] * 4
        in_outs = [((2 * shard, part_ff), BF16, "v")] * 4
    else:
        ff_plan = [(0, 0, part_ff, 0, 0, 0)]
        in_plan = [(0, 0, width, 0, 0, 0)]
        ff_outs = [((part_ff, width), BF16, "v")]
        in_outs = [((width, part_ff), BF16, "v")]
    act_own, slope_own, in_w = call(
        functools.partial(expand_kernel, b_copies, len(b_pieces)),
        "expand_own",
        meta,
        vm(normed_two, *b_pieces),
        [((size, part_ff), BF16, "v")] * 2 + [((width, part_ff), BF16, "v")],
        deps=tuple(thirds),
    )
    if fast:
        c_pieces = distant(c_pieces, act_own)
        c_copies = [
            (number, 0, piece.shape[0], 0, 0, row, 0, width, block, far, 0)
            for number, (piece, row, far) in enumerate(rows_of(c_pieces))
        ]
    act_peer, slope_peer, normed_two_peer = call(
        functools.partial(expand_kernel, (), 3),
        "expand_peer",
        meta,
        vm(thirds[0], in_w, *thirds[1:]),
        [((size, part_ff), BF16, "v")] * 2 + [((size, width), BF16, "v")],
        deps=tuple(c_pieces[n] for n in (1, 2)) if fast else (),
    )
    ff_parts = call(
        functools.partial(product_kernel, ff_plan, len(ff_outs)),
        "product",
        meta,
        vm(act_own, act_peer, low, low_peer),
        ff_outs,
        [shape_ff],
    )
    ff_parts = list(ff_parts)
    if fast:
        ff_x = on_x.send(after(ff_parts[0], c_pieces[3], c_pieces[4]))
        ff_y = on_y.send(after(ff_parts[1], c_pieces[3], c_pieces[4]))
    pre_own, pre_peer, part_gn, *send_gn, ff_w = call(
        functools.partial(contract_kernel, c_copies, len(c_pieces)),
        "contract",
        meta,
        vm(slope_own, slope_peer, low, low_peer, in_w, *c_pieces),
        [((size, part_ff), BF16, "v")] * 2
        + [((size, width), F32, "v")]
        + [((size, width // 3), BF16, "v")] * 3
        + [((part_ff, width), BF16, "v")],
        deps=(ff_parts[0],),
    )
    in_parts = call(
        functools.partial(product_kernel, in_plan, len(in_outs)),
        "outer",
        meta,
        vm(normed_two, normed_two_peer, pre_own, pre_peer),
        in_outs,
        [shape_in],
    )
    in_parts = list(in_parts)
    last = in_parts[0]

    def turn(parts, by_x, by_y, *deps):
        h = parts[3].shape[0] // 2
        columns = parts[3].shape[1]
        to_y, to_x = call(
            turn_kernel,
            "turn",
            meta,
            vm(parts[2], by_x, parts[3], by_y),
            [((parts[2].shape[0] - h, columns), BF16, "v"), ((h, columns), BF16, "v")],
            deps=deps,
        )
        return on_y.send(to_y), on_x.send(to_x), to_y

    def add(a, b, *deps):
        (out,) = call(add_kernel, "add", meta, vm(a, b), [(a.shape, BF16, "v")], deps=deps)
        return out

    other_gn = [peer(v) for v in send_gn]
    grad_residual, low_mine, *low_given, grad_keep, grad_send, grad_gain_two = call(
        through_kernel,
        "through",
        meta,
        vm(residual, part_gn, *other_gn, out_cotangent, pool_cotangent, gain_two, out_half, out_other),
        [
            ((size, width), F32, "v"),
            ((size, half), BF16, "v"),
            ((size // 2, half), BF16, "v"),
            ((size // 2, half), BF16, "v"),
            ((size, half), BF16, "v"),
            ((size, half), BF16, "v"),
            ((1, width), F32, "v"),
        ],
        deps=(last,),
    )
    grad_got = peer(grad_send)
    last = grad_gain_two
    if fast:
        last_y, last_x, last = turn(ff_parts, ff_x, ff_y, last)
        ff_last = (last_y, last_x)
    head_rows = 8

    def halve_first(parts, by_x, by_y, last_y, last_x, *deps, extra=0):
        rows, columns = parts[3].shape
        keep, send = call(
            land_half_kernel,
            "land",
            meta,
            vm(parts[2], by_x, last_y, parts[3], by_y, last_x),
            [((rows // 2, columns + extra), BF16, "v")] * 2,
            deps=deps,
        )
        return keep, swap(send, "dp", nz, 1)

    def halve_next(keep, got, *deps, extra=0):
        rows, columns = keep.shape
        keep, send = call(
            functools.partial(halve_kernel, columns - extra),
            "halve",
            meta,
            vm(keep, got),
            [((rows // 2, columns), BF16, "v")] * 2,
            deps=deps,
        )
        return keep, swap(send, "dp", nz, 2)

    def quarter(keep, got, *deps):
        own = add(keep, got, *deps)
        return own, swap(own, "dp", nz, 1), swap(own, "dp", nz, 2)

    def quarters(own, by_low, by_high, *deps):
        return own, by_low, by_high, swap(after(by_high, *deps), "dp", nz, 1)

    def shards(four, *deps):
        columns = four[0].shape[1]
        return call(join_kernel, "join", meta, vm(*four), [((shard, columns), BF16, "v")] * 2, deps=deps)

    def attend_back(qkv, powers, g, att, sums, diag, name, *deps):
        return call(
            attend_back_kernel,
            name,
            meta,
            vm(qkv, powers, g, att, sums, diag),
            [((size, wide), BF16, "v"), ((head_rows, 2 * size), F32, "v")],
            [pltpu.VMEM((size, size), BF16), pltpu.VMEM((128, 2 * size), F32)],
            deps=deps,
        )

    diag = jnp.zeros((head_rows, 2 * size), F32)
    dqkv_own, diag = attend_back(
        qkv_own, powers_own, grad_keep, attended, sums_own, diag, "attend_back_own", last, grad_got
    )
    last = dqkv_own
    if fast:
        ff_keep, ff_one = halve_first(ff_parts, ff_x, ff_y, *ff_last, last)
        in_x = on_x.send(after(in_parts[0], dqkv_own))
        in_y = on_y.send(after(in_parts[1], dqkv_own))
        last = ff_keep
    dqkv_peer, diag = attend_back(
        qkv_peer, powers_peer, grad_got, given_att, sums_peer, diag, "attend_back_peer", last
    )
    last = diag
    if fast:
        ff_keep, ff_two = halve_next(ff_keep, ff_one, last)
        last = ff_keep
    got_att_peer = [peer(after(v, last)) for v in own_halves]
    if fast:
        at_plan = message_plan(2 * shard)
        at_plan = at_plan + [(n, 2 * shard, 16, 0, 0, width) for n in (0, 2)]
        at_outs = [((2 * shard + (16 if n in (0, 2) else 0), 4 * half), BF16, "v") for n in range(4)]
    else:
        at_plan = [(0, 0, width + 16, 0, 0, 0)]
        at_outs = [((width + 16, 4 * half), BF16, "v")]
    part_gh, *send_gh, small_grads = call(
        inputs_kernel,
        "inputs",
        meta,
        vm(dqkv_own, dqkv_peer, qkv_w, hidden_in, hidden_peer, grad_gain_two, diag, buckets),
        [((size, width), F32, "v")] + [((size, half), BF16, "v")] * 2 + [((16, 128), F32, "v")],
        [pltpu.VMEM((1, width), F32)],
        deps=(last,),
    )
    low_other = [peer(after(v, part_gh, *got_att_peer)) for v in low_given]
    last = part_gh
    if fast:
        last_y, last_x, last = turn(in_parts, in_x, in_y, last)
        in_last = (last_y, last_x)
    at_parts = call(
        functools.partial(weights_kernel, at_plan, len(at_outs)),
        "weights",
        meta,
        vm(
            normed,
            normed_peer,
            dqkv_own,
            dqkv_peer,
            attended,
            *got_att,
            given_att,
            *got_att_peer,
            low_mine,
            *low_other,
            small_grads,
        ),
        at_outs,
        [pltpu.VMEM((width + 16, 4 * half), BF16)],
        deps=(last,),
    )
    at_parts = list(at_parts)
    last = at_parts[0]
    if fast:
        at_x = on_x.send(at_parts[0])
        at_y = on_y.send(at_parts[1])
        in_keep, in_one = halve_first(in_parts, in_x, in_y, *in_last, last)
        last = in_keep
    other_gh = [peer(after(v, last)) for v in send_gh]
    part_branch, *send_branch = call(
        output_kernel,
        "output",
        meta,
        vm(act_own, act_peer, ff_w),
        [((size, width), F32, "v")] + [((size, half), BF16, "v")] * 2,
        deps=(last,),
    )
    last = part_branch
    (grad_hidden,) = call(
        hidden_kernel,
        "hidden",
        meta,
        vm(hidden_in, grad_residual, part_gh, *other_gh, gain_one),
        [((size, width), F32, "v")],
        deps=(last,),
    )
    last = grad_hidden

    if fast:
        ff_four = quarter(ff_keep, ff_two, last)
        last_y, last_x, last = turn(at_parts, at_x, at_y, ff_four[0])
        at_last = (last_y, last_x)
        in_keep, in_two = halve_next(in_keep, in_one, last)
        ff_four = quarters(*ff_four, in_keep)
        at_keep, at_one = halve_first(at_parts, at_x, at_y, *at_last, in_keep, extra=128)
        in_four = quarter(in_keep, in_two, at_keep)
        (grad_ffout,) = call(
            join_rows_kernel,
            "join_rows",
            meta,
            vm(*ff_four),
            [((block, width), F32, "v")],
            deps=(in_four[0],),
        )
        last = grad_ffout
        other_branch = [peer(after(v, last)) for v in send_branch]
    else:
        other_branch = [peer(v) for v in send_branch]
    hidden_out, pooled, stats = call(
        finish_kernel,
        "finish",
        meta,
        vm(residual, part_branch, *other_branch, sums),
        [((size, width), BF16, "v"), ((1, width), F32, "v"), ((1, width), F32, "v")],
        deps=(last,),
    )
    last = stats
    if fast:
        at_keep, at_two = halve_next(at_keep, at_one, last, extra=128)
        in_four = quarters(*in_four, at_keep)
        mine_in, other_in = shards(in_four, at_keep)
        got_in = peer(other_in)
        own_at, small_grads = call(
            last_kernel,
            "last",
            meta,
            vm(at_keep, at_two),
            [((shard // 2, 4 * half), BF16, "v"), ((16, 128), F32, "v")],
            deps=(mine_in,),
        )
        at_four = own_at, swap(own_at, "dp", nz, 1), swap(own_at, "dp", nz, 2)
        small_grads = small_grads + peer(small_grads)
        (grad_in,) = call(
            functools.partial(weave_in_kernel, block),
            "weave_in",
            meta,
            vm(mine_in, got_in),
            [((shard, full_ff), F32, "v")],
            deps=(own_at,),
        )
        at_four = quarters(*at_four, grad_in)
        mine_at, other_at = shards(at_four, small_grads)
        got_at = peer(other_at)
        grad_at = call(
            weave_at_kernel, "weave_at", meta, vm(mine_at, got_at), [((shard, width), F32, "v")] * 4
        )
    else:

        def reduced(v):
            v = lax.psum_scatter(v, "fsdp", scatter_dimension=0, tiled=True)
            return lax.psum(v, "dp").astype(F32)

        def spread(v, axis):
            none = jnp.zeros_like(v)
            return by_core(jnp.stack([v, none], axis), jnp.stack([none, v], axis))

        grad_ffout = reduced(
            spread(ff_parts[0].reshape(nf // 2, block, width), 1).reshape(full_ff, width)
        )
        grad_in = reduced(
            spread(in_parts[0].reshape(width, nf // 2, block), 2).reshape(width, full_ff)
        )
        grads = spread(at_parts[0][:width].reshape(width, 4, half), 2).reshape(width, 4 * width)
        grads = reduced(grads)
        grad_at = [grads[:, n * width : (n + 1) * width] for n in range(4)]
        small_grads = lax.psum(small_grads, ("fsdp", "dp"))

    count = width // 128
    rows = levels // nf
    table = small_grads[2 * count :].reshape(-1)[: heads * levels].reshape(heads, levels)
    grad_table = lax.dynamic_slice_in_dim(table, me * rows, rows, 1).T
    gains = small_grads[: 2 * count].reshape(2, width)
    gains = lax.dynamic_slice_in_dim(gains, me * shard, shard, 1)
    return (
        hidden_out,
        pooled,
        grad_hidden,
        gains[0],
        grad_at[0],
        grad_at[1],
        grad_at[2],
        grad_at[3],
        grad_table,
        gains[1],
        grad_in,
        grad_ffout,
        stats[:, :3],
    )


def solution(mesh):
    token = P(("fsdp", "dp"), None)
    weight = P("fsdp", None)
    return jax.shard_map(
        functools.partial(body, mesh.shape["fsdp"], mesh.shape["dp"]),
        mesh=mesh,
        in_specs=(
            token,
            P("fsdp"),
            weight,
            weight,
            weight,
            weight,
            weight,
            P("fsdp"),
            weight,
            weight,
            P(),
            P(("fsdp", "dp")),
            P(("fsdp", "dp")),
            token,
            token,
        ),
        out_specs=(
            token,
            token,
            token,
            P("fsdp"),
            weight,
            weight,
            weight,
            weight,
            weight,
            P("fsdp"),
            weight,
            weight,
            token,
        ),
        check_vma=False,
    )
```

```python
import functools
import math

import jax
import jax.numpy as jnp
from jax import lax
from jax.experimental import pallas as pl
from jax.experimental.pallas import tpu as pltpu
from jax.sharding import PartitionSpec as P

EPS = 1e-06
F32 = jnp.float32
BF16 = jnp.bfloat16
VMEM_SPARE = 3 * 2**20
WEIGHTS = {"turn": 30.0, "expand_own": 30.0}
GELU_A = 0.7978845608028654
GELU_B = 0.044715


def dot(a, b):
    return lax.dot_general(a, b, (((1,), (0,)), ((), ())), preferred_element_type=F32)


def dot_right(a, b):
    return lax.dot_general(a, b, (((1,), (1,)), ((), ())), preferred_element_type=F32)


def dot_left(a, b):
    return lax.dot_general(a, b, (((0,), (0,)), ((), ())), preferred_element_type=F32)


def iota(shape, dim):
    return lax.broadcasted_iota(jnp.int32, shape, dim)


def call(kernel, name, meta, ins, outs, scratch=(), deps=(), limit=0):
    spaces = {"v": pltpu.VMEM, "s": pltpu.SMEM, "h": pl.ANY}
    held = [(a.shape, a.dtype) for a, m in ins if m == "v"]
    held += [(s, d) for s, d, m in outs if m == "v"]
    held += [(x.shape, x.dtype) for x in scratch if x.memory_space == pltpu.VMEM]
    need = sum(math.prod(s) * jnp.dtype(d).itemsize for s, d in held)
    ins = [(after(meta, *deps), "s")] + list(ins)
    return pl.pallas_call(
        kernel,
        name=name,
        out_shape=[jax.ShapeDtypeStruct(s, d) for s, d, _ in outs],
        in_specs=[pl.BlockSpec(memory_space=spaces[m]) for _, m in ins],
        out_specs=[pl.BlockSpec(memory_space=spaces[m]) for _, _, m in outs],
        scratch_shapes=list(scratch),
        compiler_params=pltpu.CompilerParams(vmem_limit_bytes=max(limit, need + VMEM_SPARE)),
        cost_estimate=pl.CostEstimate(
            flops=1000, bytes_accessed=int(3.7e6 * WEIGHTS.get(name, 0.0)) + 1000, transcendentals=0
        ),
    )(*[a for a, _ in ins])


def after(v, *deps):
    return lax.optimization_barrier((v,) + deps)[0] if deps else v


def place(meta, pieces, targets, copies):
    for src, row, rows, from_column, dst, base, column, width, unit, far, side in copies:
        start = base
        if unit:
            start = base + unit * jnp.bitwise_xor(meta[1], far)
            if side == 1:
                start = start + (unit // 2) * meta[2]
            if side == 2:
                start = start + (unit // 2) * (1 - meta[2])
            start = pl.multiple_of(start, 16)
        targets[dst][pl.ds(start, rows), column : column + width] = pieces[src][
            row : row + rows, from_column : from_column + width
        ]


def rows_loop(count, step, fn):
    def one(i, carry):
        fn(pl.ds(pl.multiple_of(i * step, step), step))
        return carry

    lax.fori_loop(0, count // step, one, 0)


def scatter_out(meta, scratch, outs, plan):
    for dst, row, rows, unit, far, offset in plan:
        start = offset
        if unit:
            start = pl.multiple_of(offset + unit * jnp.bitwise_xor(meta[1], far), 16)
        outs[dst][row : row + rows, :] = scratch[pl.ds(start, rows), :]


def small_block(meta, gain_one, gain_two, rel):
    row, lane = iota((16, 128), 0), iota((16, 128), 1)
    block = jnp.where((row == 2) & (lane == 0), (meta[4] // 256).astype(F32), 0.0)
    block = jnp.where((row == 2) & (lane == 1), (meta[4] % 256).astype(F32), block)
    parts = [(0, gain_one), (1, gain_two)] + [(4 + n, rel[n : n + 1, :]) for n in range(rel.shape[0])]
    for at, value in parts:
        value = value[...].astype(F32)
        wide = jnp.concatenate([value, jnp.zeros((1, 128 - value.shape[1]), F32)], axis=1)
        block = jnp.where(row == at, wide, block)
    return block.astype(BF16)


def pack_kernel(n_chips, meta, *refs):
    sources = refs[:5]
    gain_one, gain_two, rel = refs[5:8]
    kept_a, given_a, kept_b, given_b = refs[8:12]
    held, sems = refs[12:17], refs[17]
    handles = [pltpu.make_async_copy(a, b, sems.at[n]) for n, (a, b) in enumerate(zip(sources, held))]
    for handle in handles:
        handle.start()
    width = 4 * (held[0].shape[1] // 2)
    block = small_block(meta, gain_one, gain_two, rel)
    for out in (kept_a, given_a):
        out[:, width:] = jnp.zeros((out.shape[0], 128), BF16)
        out[0:16, width:] = block
    for handle in handles:
        handle.wait()
    wq, wk, wv, wo, w_in = held
    core = meta[2]
    half = wq.shape[1] // 2
    block = w_in.shape[1] // (2 * n_chips)
    for which, a_ref, b_ref in ((core, kept_a, kept_b), (1 - core, given_a, given_b)):
        for n, w in enumerate((wq, wk, wv, wo)):
            cols = pl.ds(pl.multiple_of(which * half, 128), half)
            a_ref[:, n * half : (n + 1) * half] = w[:, cols]
        for n in range(b_ref.shape[1] // block):
            cols = pl.ds(pl.multiple_of((2 * n + which) * block, 128), block)
            b_ref[:, n * block : (n + 1) * block] = w_in[:, cols]


def stack_kernel(meta, kept, taken, both):
    shard = kept.shape[0]
    both[pl.ds(pl.multiple_of(shard * meta[2], 16), shard), :] = kept[...]
    both[pl.ds(pl.multiple_of(shard * (1 - meta[2]), 16), shard), :] = taken[...]


def cut_kernel(meta, by_x, by_y, upper, lower):
    h = upper.shape[0]
    upper[...] = by_x[:h, :]
    lower[...] = by_y[h:, :]


def low_kernel(meta, out_cot, pool_cot, low):
    size = low.shape[0]
    length, prefix = meta[4], meta[5]
    count = (length - prefix).astype(F32)

    def lows(ds):
        t = iota((256, 1), 0) + ds.start
        pool = jnp.where((t >= prefix) & (t < length), 1.0, 0.0) / count
        low[ds, :] = (out_cot[ds, :].astype(F32) + pool * pool_cot[...]).astype(BF16)

    rows_loop(size, 256, lows)


def prepare_kernel(copies, n_pieces, levels, meta, hidden, hidden_peer, buckets, *refs):
    pieces = refs[:n_pieces]
    normed, normed_peer, bias, gain_one, gain_two, length_peer = refs[n_pieces : n_pieces + 6]
    rest = refs[n_pieces + 6 :]
    if copies:
        qkv, w_half, table, table_rows = rest
        place(meta, pieces, (qkv, w_half), copies)
        count = n_pieces
        column = pieces[0].shape[1] - 128
        blocks = [ref[0:16, column:].astype(F32) for ref in pieces]
        places = [jnp.bitwise_xor(meta[0], 2 * (p % 4) + p // 4) for p in range(count)]
    else:
        table, table_rows = rest
        count = pieces[0].shape[0] // 16
        blocks = [pieces[0][16 * p : 16 * p + 16, :].astype(F32) for p in range(count)]
        places = [jnp.int32(p) for p in range(count)]
    size, width = hidden.shape
    shard = width // count
    some = levels // count
    table[...] = jnp.zeros_like(table)
    first = jnp.zeros((1, width), F32)
    second = jnp.zeros((1, width), F32)
    rest = jnp.zeros((1, width - 128), F32)
    peers = jnp.zeros((1, 1), F32)
    for where, piece in zip(places, blocks):
        first += pltpu.roll(jnp.concatenate([piece[0:1], rest], axis=1), shard * where, 1)
        second += pltpu.roll(jnp.concatenate([piece[1:2], rest], axis=1), shard * where, 1)
        length = 256.0 * piece[2:3, 0:1] + piece[2:3, 1:2]
        peers += jnp.where(where == jnp.bitwise_xor(meta[0], 1), length, 0.0)
        for b in range(some):
            table[pl.ds(some * where + b, 1), :] = piece[4 + b : 5 + b]
    length_peer[...] = jnp.broadcast_to(peers, (1, 128))
    gain_one[...] = first
    gain_two[...] = second

    for x_ref, n_ref in ((hidden, normed), (hidden_peer, normed_peer)):

        def rows(ds, x_ref=x_ref, n_ref=n_ref):
            x = x_ref[ds, :].astype(F32)
            inv = lax.rsqrt(jnp.mean(x * x, axis=-1, keepdims=True) + EPS)
            n_ref[ds, :] = (x * inv * gain_one[...]).astype(BF16)

        rows_loop(size, 256, rows)

    span = 2 * size
    hot = (buckets[...] == iota((levels, span), 0)).astype(BF16)
    table_rows[...] = dot_left(table[...].astype(BF16), hot)
    heads, _, wide = bias.shape
    base = heads * meta[2]

    def head(h, carry):
        row = table_rows[pl.ds(base + h, 1), :]
        first = jnp.broadcast_to(pltpu.roll(row, span - 127, 1), (8, span))
        sub = iota((8, span), 0)
        full = first
        for k in range(1, 8):
            full = jnp.where(sub == k, pltpu.roll(first, k, 1), full)
        bias[h, 0:8, :] = full[:, :wide]
        have = 8
        while have < 128:
            more = pltpu.roll(full, have, 1)
            bias[h, have : 2 * have, :] = more[:, :wide]
            full = jnp.concatenate([full, more], axis=0)
            have *= 2
        return carry

    lax.fori_loop(0, heads, head, 0)


def attend_kernel(meta, x_ref, bias, w, length, qkv, out, upper, lower, powers, inv_sums, scores):
    size = x_ref.shape[0]
    part = w.shape[1] // 3
    pairs = part // 128
    lane = iota((1, 128), 1)
    half = lane < 64
    strips = size // 128
    inv_sums[...] = jnp.zeros_like(inv_sums)

    def project(ds):
        for n in range(3):
            cols = slice(n * part, (n + 1) * part)
            qkv[ds, cols] = dot(x_ref[ds, :], w[:, cols]).astype(BF16)

    rows_loop(size, size, project)
    masked = jnp.where(iota((size, 1), 0).astype(F32) < length[0:1, 0:1], 0.0, -1e30).astype(F32)

    def pair(p, carry):
        base = pl.multiple_of(p * 128, 128)
        qp = qkv[:, pl.ds(base, 128)].astype(F32)
        kp = qkv[:, pl.ds(base + part, 128)].astype(F32)
        vp = qkv[:, pl.ds(base + 2 * part, 128)].astype(F32)
        joined = None
        for side in range(2):
            head = 2 * p + side
            own = half if side == 0 else jnp.logical_not(half)
            spare = lane == (64 if side == 0 else 0)
            qa = jnp.where(own, qp, jnp.where(spare, 1.0, 0.0)).astype(BF16)
            ka = jnp.where(own, kp, jnp.where(spare, masked, 0.0)).astype(BF16)
            va = jnp.where(own, vp, jnp.where(spare, 1.0, 0.0)).astype(BF16)
            top = None
            for a in range(strips):
                rows = slice(128 * a, 128 * a + 128)
                off = 128 * (strips - 1 - a)
                s = dot_right(ka[rows], qa) + bias[head, :, off : off + size]
                scores[rows, :] = s
                peak = jnp.max(s, axis=0, keepdims=True)
                top = peak if top is None else jnp.maximum(top, peak)
            for a in range(strips):
                rows = slice(128 * a, 128 * a + 128)
                powers[head, rows, :] = jnp.exp(scores[rows, :] - top).astype(BF16)
            mixed = dot_left(va, powers[head]).T
            sums = jnp.sum(jnp.where(spare, mixed, 0.0), axis=1, keepdims=True)
            inv = 1.0 / sums
            inv_sums[...] = jnp.where(lane == head, inv, inv_sums[...])
            mixed = mixed * inv
            joined = mixed if side == 0 else jnp.where(half, joined, mixed)
        joined = joined.astype(BF16)
        cols = pl.ds(base, 128)
        out[:, cols] = joined
        upper[:, cols] = joined[: size // 2]
        lower[:, cols] = joined[size // 2 :]
        return carry

    lax.fori_loop(0, pairs, pair, 0, unroll=True)


def residual_kernel(meta, hidden, attended, upper, lower, gain, w_half, w_other, residual, normed, left, middle, right, sums, w_out):
    size, width = hidden.shape
    half = width // 2
    length = meta[4]
    core = meta[2]
    w_out[:, pl.ds(pl.multiple_of(core * half, 128), half)] = w_half[...]
    w_out[:, pl.ds(pl.multiple_of((1 - core) * half, 128), half)] = w_other[...]
    mine = pl.ds(pl.multiple_of(core * half, 128), half)
    other = pl.ds(pl.multiple_of((1 - core) * half, 128), half)
    sums[...] = jnp.zeros_like(sums)

    for first, got in ((0, upper), (size // 2, lower)):
        ds = slice(first, first + size // 2)
        x = hidden[ds, :].astype(F32)
        branch = dot(attended[ds, :], w_out[mine, :]) + dot(got[...], w_out[other, :])
        live = (iota((size // 2, 1), 0) + first) < length
        sums[0:1, :] += jnp.sum(jnp.where(live, x * x, 0.0), axis=0, keepdims=True)
        sums[1:2, :] += jnp.sum(jnp.where(live, branch * branch, 0.0), axis=0, keepdims=True)
        r = x + branch
        residual[ds, :] = r
        inv = lax.rsqrt(jnp.mean(r * r, axis=-1, keepdims=True) + EPS)
        value = (r * inv * gain[...]).astype(BF16)
        normed[ds, :] = value
        third = left.shape[1]
        for n, ref in enumerate((left, middle, right)):
            ref[ds, :] = value[:, n * third : (n + 1) * third]


def expand_kernel(copies, n_pieces, *refs):
    meta, x_ref = refs[:2]
    pieces = refs[2 : 2 + n_pieces]
    if copies:
        activated, slope, w_in = refs[2 + n_pieces :]
        place(meta, pieces, (w_in,), copies)
    else:
        w_in = pieces[0]
        activated, slope, whole = refs[2 + n_pieces :]
        third = x_ref.shape[1]
        for n, ref in enumerate((x_ref, *pieces[1:])):
            whole[:, n * third : (n + 1) * third] = ref[...]
        x_ref = whole
    chunk = 512 if w_in.shape[1] % 512 == 0 else 256

    def rows(ds):
        x = x_ref[ds, :]
        for c in range(0, w_in.shape[1], chunk):
            t = dot(x, w_in[:, c : c + chunk])
            square = t * t
            th = jnp.tanh(t * (GELU_A + (GELU_A * GELU_B) * square))
            phi = 0.5 + 0.5 * th
            activated[ds, c : c + chunk] = (t * phi).astype(BF16)
            inner = GELU_A + (3.0 * GELU_A * GELU_B) * square
            slope[ds, c : c + chunk] = (phi + 0.5 * t * (1.0 - th * th) * inner).astype(BF16)

    rows_loop(x_ref.shape[0], x_ref.shape[0], rows)


def product_kernel(plan, n_out, *refs):
    meta, left_own, left_peer, right_own, right_peer = refs[:5]
    outs = refs[5 : 5 + n_out]
    grads = refs[5 + n_out]
    step = 512 if grads.shape[0] % 512 == 0 else 384
    for c in range(0, grads.shape[0], step):
        part = dot_left(left_own[:, c : c + step], right_own[...])
        part += dot_left(left_peer[:, c : c + step], right_peer[...])
        grads[c : c + step, :] = part.astype(BF16)
    scatter_out(meta, grads, outs, plan)


def contract_kernel(copies, n_pieces, *refs):
    meta, slope_own, slope_peer, low_own, low_peer, w_in = refs[:6]
    pieces = refs[6 : 6 + n_pieces]
    pre_own, pre_peer, part_own, *sends, w_ffout = refs[6 + n_pieces :]
    third = sends[0].shape[1]
    place(meta, pieces, (w_ffout,), copies)
    size = low_own.shape[0]
    chunk = 512 if w_in.shape[1] % 512 == 0 else 256
    for slope, low, grad_pre, part in (
        (slope_peer, low_peer, pre_peer, sends),
        (slope_own, low_own, pre_own, (part_own,)),
    ):

        def rows(ds, slope=slope, low=low, grad_pre=grad_pre, part=part):
            y = low[ds, :]
            total = None
            for c in range(0, w_in.shape[1], chunk):
                g = dot_right(y, w_ffout[c : c + chunk, :])
                g = (slope[ds, c : c + chunk].astype(F32) * g).astype(BF16)
                grad_pre[ds, c : c + chunk] = g
                t = dot_right(g, w_in[:, c : c + chunk])
                total = t if total is None else total + t
            if len(part) > 1:
                for n, ref in enumerate(part):
                    ref[ds, :] = total[:, n * third : (n + 1) * third].astype(BF16)
            else:
                part[0][ds, :] = total

        rows_loop(size, size, rows)


def through_kernel(meta, residual, part, left, center, right, out_cot, pool_cot, gain, w_half, w_other,
                   grad_residual, low_mine, upper, lower, grad_keep, grad_send, grad_gain):
    size, width = residual.shape
    half = width // 2
    core = meta[2]
    mine = pl.ds(pl.multiple_of(core * half, 128), half)
    theirs = pl.ds(pl.multiple_of((1 - core) * half, 128), half)
    length, prefix = meta[4], meta[5]
    count = (length - prefix).astype(F32)
    grad_gain[...] = jnp.zeros_like(grad_gain)

    def rows(ds, low_given, start):
        x = residual[ds, :]
        gn = part[ds, :] + jnp.concatenate([left[ds, :], center[ds, :], right[ds, :]], axis=1).astype(F32)
        inv = lax.rsqrt(jnp.mean(x * x, axis=-1, keepdims=True) + EPS)
        u = gain[...] * gn
        xr = x * inv
        t = iota((256, 1), 0) + ds.start
        pool = jnp.where((t >= prefix) & (t < length), 1.0, 0.0) / count
        go = out_cot[ds, :].astype(F32) + pool * pool_cot[...]
        g = go + inv * (u - xr * jnp.mean(xr * u, axis=-1, keepdims=True))
        grad_gain[...] += jnp.sum(xr * gn, axis=0, keepdims=True)
        grad_residual[ds, :] = g
        first, second = g[:, :half].astype(BF16), g[:, half:].astype(BF16)
        on_first = jnp.broadcast_to(core == 0, first.shape)
        a = jnp.where(on_first, g[:, :half], g[:, half:]).astype(BF16)
        b = jnp.where(on_first, g[:, half:], g[:, :half]).astype(BF16)
        low_mine[ds, :] = a
        low_given[pl.ds(ds.start - start, 256), :] = b
        grad_keep[ds, :] = (dot_right(a, w_half[mine, :]) + dot_right(b, w_other[mine, :])).astype(BF16)
        grad_send[ds, :] = (dot_right(a, w_half[theirs, :]) + dot_right(b, w_other[theirs, :])).astype(BF16)

    middle = size // 2
    for first, low_given in ((0, upper), (middle, lower)):

        def some(i, carry, first=first, low_given=low_given):
            rows(pl.ds(pl.multiple_of(first + 256 * i, 256), 256), low_given, first)
            return carry

        lax.fori_loop(0, middle // 256, some, 0)


def attend_back_kernel(meta, qkv, powers, g_ref, a_ref, inv_sums, diag_in, out, diag, grads, slant):
    size = g_ref.shape[0]
    part = qkv.shape[1] // 3
    pairs = part // 128
    strips = size // 128
    span = 2 * size
    lane = iota((1, 128), 1)
    half = lane < 64
    diag[...] = diag_in[...]

    def pair(p, carry):
        base = pl.multiple_of(p * 128, 128)
        cols = pl.ds(base, 128)
        kcols = pl.ds(base + part, 128)
        vcols = pl.ds(base + 2 * part, 128)
        qp, kp = qkv[:, cols], qkv[:, kcols]
        vp = qkv[:, vcols].astype(F32)
        do = g_ref[:, cols].astype(F32)
        prod = do * a_ref[:, cols].astype(F32)
        dq_all = dk_all = dv_all = None
        for side in range(2):
            head = 2 * p + side
            own = half if side == 0 else jnp.logical_not(half)
            one = 64 if side == 0 else 0
            inv = jnp.sum(jnp.where(lane == head, inv_sums[...], 0.0), axis=1, keepdims=True)
            inner = jnp.sum(jnp.where(own, prod, 0.0), axis=1, keepdims=True) * inv
            upper = inner.astype(BF16).astype(F32)
            dos = jnp.where(
                own,
                do * inv,
                jnp.where(lane == one, -upper, jnp.where(lane == one + 1, upper - inner, 0.0)),
            ).astype(BF16)
            ones = (lane == one) | (lane == one + 1)
            va = jnp.where(own, vp, jnp.where(ones, 1.0, 0.0)).astype(BF16)
            slant[...] = jnp.zeros_like(slant)
            for a in range(strips):
                rows = slice(128 * a, 128 * a + 128)
                off = 128 * (strips - 1 - a)
                ds = (powers[head, rows, :].astype(F32) * dot_right(va[rows], dos)).astype(BF16)
                grads[rows, :] = ds
                slant[:, off : off + size] += ds.astype(F32)
            dk = dot(grads[...], qp)
            dv = dot(powers[head], dos)
            dk_all = dk if side == 0 else jnp.where(half, dk_all, dk)
            dv_all = dv if side == 0 else jnp.where(half, dv_all, dv)
            dq = dot_left(kp, grads[...]).T
            dq_all = dq if side == 0 else jnp.where(half, dq_all, dq)
            y = slant[...]
            rest = 64
            while rest >= 1:
                y = y[:rest] + pltpu.roll(y[rest:], span - rest, 1)
                rest //= 2
            diag[pl.ds(head, 1), :] += pltpu.roll(y, 127, 1)
        out[:, cols] = dq_all.astype(BF16)
        out[:, kcols] = dk_all.astype(BF16)
        out[:, vcols] = dv_all.astype(BF16)
        return carry

    lax.fori_loop(0, pairs, pair, 0, unroll=True)


def weights_kernel(plan, n_out, *refs):
    meta, x_own, x_peer, dqkv_own, dqkv_peer, att_own, upper, lower, att_peer, got_upper, got_lower, low_own, low_upper, low_lower, small = refs[:15]
    outs = refs[15 : 15 + n_out]
    (grads,) = refs[15 + n_out :]
    middle = upper.shape[0]
    part = dqkv_own.shape[1]
    depth = x_own.shape[1]
    half = depth // 2
    for c in range(0, depth, 384):
        cols = slice(c, c + 384)
        g = dot_left(x_own[:, cols], dqkv_own[...]) + dot_left(x_peer[:, cols], dqkv_peer[...])
        grads[cols, 0:part] = g.astype(BF16)
    core = meta[2]
    mine = pl.multiple_of(core * half, 16)
    theirs = pl.multiple_of((1 - core) * half, 16)
    for c in range(0, half, 384):
        cols = slice(c, c + 384)
        g = dot_left(att_own[:, cols], low_own[...]) + dot_left(att_peer[:middle, cols], low_upper[...])
        g += dot_left(att_peer[middle:, cols], low_lower[...])
        grads[pl.ds(mine + c, 384), part:] = g.astype(BF16)
        g = dot_left(upper[:, cols], low_own[:middle]) + dot_left(lower[:, cols], low_own[middle:])
        g += dot_left(got_upper[:, cols], low_upper[...])
        g += dot_left(got_lower[:, cols], low_lower[...])
        grads[pl.ds(theirs + c, 384), part:] = g.astype(BF16)
    grads[depth:, :] = jnp.zeros((16, grads.shape[1]), BF16)
    grads[depth:, 0:128] = small[...].astype(BF16)
    scatter_out(meta, grads, outs, plan)


def inputs_kernel(meta, dqkv_own, dqkv_peer, w, hidden, hidden_peer, gain_two, diag, buckets,
                  part_own, left, right, small, gain_one):
    size, width = part_own.shape
    half = width // 2
    small[...] = jnp.zeros_like(small)
    gain_one[...] = jnp.zeros_like(gain_one)

    def share(x_ref, ds, value):
        x = x_ref[ds, :].astype(F32)
        inv = lax.rsqrt(jnp.mean(x * x, axis=-1, keepdims=True) + EPS)
        gain_one[...] += jnp.sum(x * inv * value, axis=0, keepdims=True)

    def peers(ds):
        value = dot_right(dqkv_peer[ds, :], w[...])
        share(hidden_peer, ds, value)
        value = value.astype(BF16)
        left[ds, :] = value[:, :half]
        right[ds, :] = value[:, half:]

    def own(ds):
        value = dot_right(dqkv_own[ds, :], w[...])
        share(hidden, ds, value)
        part_own[ds, :] = value

    rows_loop(size, size, peers)
    rows_loop(size, size, own)
    count = width // 128
    for n in range(count):
        small[n : n + 1, :] = gain_one[:, 128 * n : 128 * n + 128]
        small[count + n : count + n + 1, :] = gain_two[:, 128 * n : 128 * n + 128]
    hot = (buckets[...] == iota((128, diag.shape[1]), 0)).astype(F32)
    table = lax.dot_general(
        diag[...],
        hot,
        (((1,), (1,)), ((), ())),
        preferred_element_type=F32,
        precision=lax.Precision.HIGHEST,
    )
    lane = iota((1, 128), 1)
    few = (16 - 2 * count) * 2 - 2
    for n in range(few):
        head = few * meta[2] + n
        row = jnp.where(lane < 32, table[n : n + 1, :], 0.0)
        small[pl.ds(2 * count + head // 4, 1), :] += pltpu.roll(row, 32 * (head % 4), 1)


def hidden_kernel(meta, hidden, grad_residual, part, left, right, gain, grad_hidden):
    def rows(ds):
        total = part[ds, :] + jnp.concatenate([left[ds, :], right[ds, :]], axis=1).astype(F32)
        x = hidden[ds, :].astype(F32)
        inv = lax.rsqrt(jnp.mean(x * x, axis=-1, keepdims=True) + EPS)
        u = gain[...] * total
        xr = x * inv
        grad_hidden[ds, :] = grad_residual[ds, :] + inv * (
            u - xr * jnp.mean(xr * u, axis=-1, keepdims=True)
        )

    rows_loop(hidden.shape[0], 256, rows)


def output_kernel(meta, act_own, act_peer, w_ffout, part_own, left, right):
    size, width = part_own.shape
    half = width // 2

    def peers(ds):
        value = dot(act_peer[ds, :], w_ffout[...]).astype(BF16)
        left[ds, :] = value[:, :half]
        right[ds, :] = value[:, half:]

    def own(ds):
        part_own[ds, :] = dot(act_own[ds, :], w_ffout[...])

    rows_loop(size, size, peers)
    rows_loop(size, size, own)


def finish_kernel(meta, residual, part, left, right, sums, hidden_out, pooled, stats):
    size, width = residual.shape
    length, prefix = meta[4], meta[5]
    count = (length - prefix).astype(F32)
    pooled[...] = jnp.zeros_like(pooled)
    stats[...] = jnp.zeros_like(stats)

    def rows(ds):
        branch = part[ds, :] + jnp.concatenate([left[ds, :], right[ds, :]], axis=1).astype(F32)
        out = residual[ds, :] + branch
        hidden_out[ds, :] = out.astype(BF16)
        t = iota((128, 1), 0) + ds.start
        live = t < length
        stats[0:1, :] += jnp.sum(jnp.where(live, branch * branch, 0.0), axis=0, keepdims=True)
        pooled[...] += jnp.sum(jnp.where((t >= prefix) & live, out, 0.0), axis=0, keepdims=True)

    rows_loop(size, 128, rows)
    pooled[...] = pooled[...] / count
    total = jnp.sum(stats[0:1, :])
    first = jnp.sum(sums[0:1, :])
    second = jnp.sum(sums[1:2, :])
    denominator = length.astype(F32) * width
    column = iota(stats.shape, 1)
    values = jnp.where(column == 0, first, jnp.where(column == 1, second, total))
    stats[...] = jnp.sqrt(values / denominator)


def total(*parts):
    value = parts[0].astype(F32)
    for part in parts[1:]:
        value = value + part.astype(F32)
    return value.astype(BF16)


def turn_kernel(meta, keep_a, got_x, keep_b, got_y, on_y, on_x):
    h = on_x.shape[0]
    on_y[...] = total(keep_a[h:], got_x[h:])
    on_x[...] = total(keep_b[h:], got_y[h:])


def add_kernel(meta, a, b, out):
    out[...] = total(a[...], b[...])


def land_half_kernel(meta, keep_a, got_x, last_y, keep_b, got_y, last_x, keep, send):
    h, width = last_x.shape
    upper = total(keep_a[:h], got_x[:h], last_y[:h])
    lower = total(keep_b[:h], got_y[:h], last_x[...])
    first = jnp.broadcast_to(meta[3] % 2 == 0, upper.shape)
    keep[:, :width] = jnp.where(first, upper.astype(F32), lower.astype(F32)).astype(BF16)
    send[:, :width] = jnp.where(first, lower.astype(F32), upper.astype(F32)).astype(BF16)
    if keep.shape[1] > width:
        rows = slice(2 * h, 2 * h + 16)
        small = total(keep_a[rows, 0:128], got_x[rows, 0:128], last_y[h:, 0:128])
        for out in (keep, send):
            out[:, width:] = jnp.zeros((h, 128), BF16)
            out[:16, width:] = small


def halve_kernel(width, meta, a, b, keep, send):
    h = keep.shape[0]
    place_at = pl.multiple_of(h * (meta[3] // 2), 16)
    other_at = pl.multiple_of(h * (1 - meta[3] // 2), 16)
    keep[:, :width] = total(a[pl.ds(place_at, h), :width], b[pl.ds(place_at, h), :width])
    send[:, :width] = total(a[pl.ds(other_at, h), :width], b[pl.ds(other_at, h), :width])
    if width < keep.shape[1]:
        extra = total(a[:h, width:], b[:h, width:])
        keep[:, width:] = extra
        send[:, width:] = extra


def last_kernel(meta, a, b, out, small):
    width = out.shape[1]
    out[...] = total(a[:, :width], b[:, :width])
    small[...] = a[:16, width:].astype(F32) + b[:16, width:].astype(F32)


def join_rows_kernel(meta, own, by_low, by_high, by_both, out):
    h = own.shape[0]
    low, high = meta[3] % 2, meta[3] // 2
    for value, at_low, at_high in (
        (own, low, high),
        (by_low, 1 - low, high),
        (by_high, low, 1 - high),
        (by_both, 1 - low, 1 - high),
    ):
        out[pl.ds(pl.multiple_of(h * (2 * at_low + at_high), 16), h), :] = value[...].astype(F32)


def join_kernel(meta, own, by_low, by_high, by_both, mine, other):
    h = own.shape[0]
    low, high = meta[3] % 2, meta[3] // 2
    for value, at_low, at_high in (
        (own, low, high),
        (by_low, 1 - low, high),
        (by_high, low, 1 - high),
        (by_both, 1 - low, 1 - high),
    ):
        rows = pl.ds(pl.multiple_of(h * at_high, 16), h)

        @pl.when(at_low == meta[2])
        def _(value=value, rows=rows):
            mine[rows, :] = value[...]

        @pl.when(at_low != meta[2])
        def _(value=value, rows=rows):
            other[rows, :] = value[...]


def weave_in_kernel(block, meta, mine, other, out):
    for which, ref in ((meta[2], mine), (1 - meta[2], other)):
        for n in range(ref.shape[1] // block):
            cols = pl.ds(pl.multiple_of((2 * n + which) * block, 128), block)
            out[:, cols] = ref[:, n * block : (n + 1) * block].astype(F32)


def weave_at_kernel(meta, mine, other, *outs):
    half = outs[0].shape[1] // 2
    for which, ref in ((meta[2], mine), (1 - meta[2], other)):
        cols = pl.ds(pl.multiple_of(which * half, 128), half)
        for n, out in enumerate(outs):
            out[:, cols] = ref[:, n * half : (n + 1) * half].astype(F32)


def swap(v, axis, count, far):
    return lax.ppermute(v, axis, [(i, i ^ far) for i in range(count)])


def message_plan(unit):
    h = unit // 2
    plan = []
    for dst, (near, far) in enumerate(((1, 3), (2, 3), (0, 2), (0, 1))):
        offset = 0 if dst in (0, 2) else h
        plan.append((dst, 0, h, unit, near, offset))
        plan.append((dst, h, h, unit, far, offset))
    return plan


class Link:
    def __init__(self, far):
        self.far = far
        self.sent = []

    def send(self, v):
        if len(self.sent) >= 2:
            v = after(v, self.sent[-2])
        got = swap(v, "fsdp", 8, self.far)
        self.sent.append(got)
        return got


def body(
    nf,
    nz,
    hidden_in,
    norm_gain_attn,
    w_query,
    w_key,
    w_value,
    w_out,
    rel_bias,
    norm_gain_ffn,
    w_in,
    w_ffout,
    bucket_index,
    row_lengths,
    prefix_lengths,
    out_cotangent,
    pool_cotangent,
):
    fast = nf == 8 and nz == 4
    size, width = hidden_in.shape
    shard = w_query.shape[0]
    heads = rel_bias.shape[1]
    levels = rel_bias.shape[0] * nf
    full_ff = w_in.shape[1]
    part_ff = full_ff // 2
    block = w_ffout.shape[0]
    half = width // 2
    few = heads // 2
    me = lax.axis_index("fsdp").astype(jnp.int32)
    where = lax.axis_index("dp").astype(jnp.int32)
    core = me & 1
    zero = jnp.zeros((), jnp.int32)

    def by_core(first, second):
        return jnp.where(core == 0, first, second)

    def peer(v):
        return swap(v, "fsdp", nf, 1)

    def dma(n):
        return pltpu.SemaphoreType.DMA((n,))

    def vm(*arrays):
        return [(a, "v") for a in arrays]

    meta = jnp.stack([me, me >> 1, core, where, row_lengths[0], prefix_lengths[0], zero, zero])
    hidden_peer = peer(hidden_in)
    wide = 3 * half
    buckets = jnp.concatenate([bucket_index[::-1], jnp.full((1,), -1, jnp.int32)])[None, :]

    if fast:
        kept_a, given_a, kept_b, given_b = call(
            functools.partial(pack_kernel, nf // 2),
            "pack",
            meta,
            [(a, "h") for a in (w_query, w_key, w_value, w_out, w_in)]
            + vm(norm_gain_attn[None], norm_gain_ffn[None], rel_bias),
            [((shard, 4 * half + 128), BF16, "v")] * 2 + [((shard, part_ff), BF16, "v")] * 2,
            [pltpu.VMEM(w.shape, BF16) for w in (w_query, w_key, w_value, w_out, w_in)] + [dma(5)],
            limit=56 * 2**20,
        )
        on_x, on_y = Link(2), Link(4)
        taken_a = peer(given_a)
        x_kept, y_taken = on_x.send(kept_a), on_y.send(taken_a)
        x_taken, y_kept = on_x.send(taken_a), on_y.send(kept_a)
        far_kept, far_taken = on_y.send(x_kept), on_x.send(y_taken)
        a_pieces = [kept_a, x_kept, y_kept, far_kept, taken_a, x_taken, y_taken, far_taken]
        a_copies = []
        for number in range(8):
            far, side = number % 4, 1 + number // 4
            a_copies.append((number, 0, shard, 0, 0, 0, 0, wide, 2 * shard, far, side))
            a_copies.append((number, 0, shard, wide, 1, 0, 0, half, 2 * shard, far, side))
        taken_b = peer(after(given_b, hidden_peer, taken_a))
        (both_b,) = call(
            stack_kernel,
            "stack",
            meta,
            vm(kept_b, taken_b),
            [((2 * shard, part_ff), BF16, "v")],
        )

        def near(v):
            return [v, on_x.send(v), on_y.send(v)]

        def distant(three, *deps):
            v, by_x, by_y = three
            h = v.shape[0] // 2
            upper, lower = call(
                cut_kernel, "cut", meta, vm(by_x, by_y), [((h, v.shape[1]), BF16, "v")] * 2, deps=deps
            )
            far_y, far_x = on_y.send(upper), on_x.send(lower)
            return three + [far_y, far_x]

        def rows_of(five):
            h = five[3].shape[0]
            return zip(five, (0, 0, 0, 0, h), (0, 1, 2, 3, 3))

    else:

        def whole(v):
            return lax.all_gather(v, "fsdp", axis=0, tiled=True)

        a_full = [whole(w) for w in (w_query, w_key, w_value, w_out)]
        a_full = [by_core(w[:, :half], w[:, half:]) for w in a_full]
        qkv_w, out_half = jnp.concatenate(a_full[:3], axis=1), a_full[3]
        b_full = whole(w_in).reshape(width, nf // 2, 2, block)
        b_pieces = [by_core(b_full[:, :, 0], b_full[:, :, 1]).reshape(width, part_ff)]
        b_copies = [(0, 0, width, 0, 0, 0, 0, part_ff, 0, 0, 0)]
        c_full = whole(w_ffout).reshape(nf // 2, 2, block, width)
        c_pieces = [by_core(c_full[:, 0], c_full[:, 1]).reshape(part_ff, width)]
        c_copies = [(0, 0, part_ff, 0, 0, 0, 0, width, 0, 0, 0)]
        length = row_lengths[0]
        split = jnp.stack([length // 256, length % 256]).astype(BF16)[None]
        rows = [norm_gain_attn[None], norm_gain_ffn[None], split, split, rel_bias]
        rows = [jnp.pad(r, ((0, 0), (0, 128 - r.shape[1]))) for r in rows]
        small = jnp.concatenate(rows, axis=0)
        a_pieces, a_copies = [whole(jnp.pad(small, ((0, 16 - small.shape[0]), (0, 0))))], ()

    (low,) = call(
        low_kernel, "low", meta, vm(out_cotangent, pool_cotangent), [((size, width), BF16, "v")]
    )
    normed, normed_peer, bias, gain_one, gain_two, length_peer, *weights = call(
        functools.partial(prepare_kernel, a_copies, len(a_pieces), levels),
        "prepare",
        meta,
        vm(hidden_in, hidden_peer, buckets, *a_pieces),
        [
            ((size, width), BF16, "v"),
            ((size, width), BF16, "v"),
            ((few, 128, 2 * size - 128), F32, "v"),
            ((1, width), F32, "v"),
            ((1, width), F32, "v"),
            ((1, 128), F32, "v"),
        ]
        + ([((width, wide), BF16, "v"), ((width, half), BF16, "v")] if fast else []),
        [pltpu.VMEM((levels, 128), F32), pltpu.VMEM((128, 2 * size), F32)],
        deps=(low,),
    )
    if fast:
        b_pieces = near(both_b)
        qkv_w, out_half = weights
    out_other = peer(out_half)

    def attend(x, length, name, *deps):
        return call(
            attend_kernel,
            name,
            meta,
            vm(x, bias, qkv_w, length),
            [
                ((size, wide), BF16, "v"),
                ((size, half), BF16, "v"),
                ((size // 2, half), BF16, "v"),
                ((size // 2, half), BF16, "v"),
                ((few, size, size), BF16, "v"),
                ((size, 128), F32, "v"),
            ],
            [pltpu.VMEM((size, size), F32)],
            deps=deps,
        )

    qkv_peer, given_att, *given_halves, powers_peer, sums_peer = attend(
        normed_peer, length_peer, "attend_peer"
    )
    low_peer = peer(after(low, given_att))
    if fast:
        b_pieces = distant(b_pieces, given_att)
        b_copies = [
            (number, 0, piece.shape[0], 0, 0, row, 0, part_ff, 2 * shard, far, 0)
            for number, (piece, row, far) in enumerate(rows_of(b_pieces))
        ]
        c_pieces = near(w_ffout)
    served = tuple(b_pieces[n] for n in (1, 2)) if fast else ()
    length_own = jnp.broadcast_to(row_lengths.astype(F32)[None], (1, 128))
    qkv_own, attended, *own_halves, powers_own, sums_own = attend(
        normed, length_own, "attend_own", given_att, out_other, *served
    )
    served = tuple(b_pieces[n] for n in (3, 4)) if fast else ()
    got_att = [peer(after(v, attended, *served)) for v in given_halves]
    residual, normed_two, *thirds, sums = call(
        residual_kernel,
        "residual",
        meta,
        vm(hidden_in, attended, *got_att, gain_two, out_half, out_other),
        [((size, width), F32, "v"), ((size, width), BF16, "v")]
        + [((size, width // 3), BF16, "v")] * 3
        + [((8, width), F32, "v")],
        [pltpu.VMEM((width, width), BF16)],
        deps=(low_peer,),
    )
    thirds = [peer(v) for v in thirds]
    shape_in = pltpu.VMEM((width, part_ff), BF16)
    shape_ff = pltpu.VMEM((part_ff, width), BF16)
    if fast:
        ff_plan, in_plan = message_plan(block), message_plan(2 * shard)
        ff_outs = [((block, width), BF16, "v")] * 4
        in_outs = [((2 * shard, part_ff), BF16, "v")] * 4
    else:
        ff_plan = [(0, 0, part_ff, 0, 0, 0)]
        in_plan = [(0, 0, width, 0, 0, 0)]
        ff_outs = [((part_ff, width), BF16, "v")]
        in_outs = [((width, part_ff), BF16, "v")]
    act_own, slope_own, in_w = call(
        functools.partial(expand_kernel, b_copies, len(b_pieces)),
        "expand_own",
        meta,
        vm(normed_two, *b_pieces),
        [((size, part_ff), BF16, "v")] * 2 + [((width, part_ff), BF16, "v")],
        deps=tuple(thirds),
    )
    if fast:
        c_pieces = distant(c_pieces, act_own)
        c_copies = [
            (number, 0, piece.shape[0], 0, 0, row, 0, width, block, far, 0)
            for number, (piece, row, far) in enumerate(rows_of(c_pieces))
        ]
    act_peer, slope_peer, normed_two_peer = call(
        functools.partial(expand_kernel, (), 3),
        "expand_peer",
        meta,
        vm(thirds[0], in_w, *thirds[1:]),
        [((size, part_ff), BF16, "v")] * 2 + [((size, width), BF16, "v")],
        deps=tuple(c_pieces[n] for n in (1, 2)) if fast else (),
    )
    ff_parts = call(
        functools.partial(product_kernel, ff_plan, len(ff_outs)),
        "product",
        meta,
        vm(act_own, act_peer, low, low_peer),
        ff_outs,
        [shape_ff],
    )
    ff_parts = list(ff_parts)
    if fast:
        ff_x = on_x.send(after(ff_parts[0], c_pieces[3], c_pieces[4]))
        ff_y = on_y.send(after(ff_parts[1], c_pieces[3], c_pieces[4]))
    pre_own, pre_peer, part_gn, *send_gn, ff_w = call(
        functools.partial(contract_kernel, c_copies, len(c_pieces)),
        "contract",
        meta,
        vm(slope_own, slope_peer, low, low_peer, in_w, *c_pieces),
        [((size, part_ff), BF16, "v")] * 2
        + [((size, width), F32, "v")]
        + [((size, width // 3), BF16, "v")] * 3
        + [((part_ff, width), BF16, "v")],
        deps=(ff_parts[0],),
    )
    in_parts = call(
        functools.partial(product_kernel, in_plan, len(in_outs)),
        "outer",
        meta,
        vm(normed_two, normed_two_peer, pre_own, pre_peer),
        in_outs,
        [shape_in],
    )
    in_parts = list(in_parts)
    last = in_parts[0]

    def turn(parts, by_x, by_y, *deps):
        h = parts[3].shape[0] // 2
        columns = parts[3].shape[1]
        to_y, to_x = call(
            turn_kernel,
            "turn",
            meta,
            vm(parts[2], by_x, parts[3], by_y),
            [((parts[2].shape[0] - h, columns), BF16, "v"), ((h, columns), BF16, "v")],
            deps=deps,
        )
        return on_y.send(to_y), on_x.send(to_x), to_y

    def add(a, b, *deps):
        (out,) = call(add_kernel, "add", meta, vm(a, b), [(a.shape, BF16, "v")], deps=deps)
        return out

    other_gn = [peer(v) for v in send_gn]
    grad_residual, low_mine, *low_given, grad_keep, grad_send, grad_gain_two = call(
        through_kernel,
        "through",
        meta,
        vm(residual, part_gn, *other_gn, out_cotangent, pool_cotangent, gain_two, out_half, out_other),
        [
            ((size, width), F32, "v"),
            ((size, half), BF16, "v"),
            ((size // 2, half), BF16, "v"),
            ((size // 2, half), BF16, "v"),
            ((size, half), BF16, "v"),
            ((size, half), BF16, "v"),
            ((1, width), F32, "v"),
        ],
        deps=(last,),
    )
    grad_got = peer(grad_send)
    last = grad_gain_two
    if fast:
        last_y, last_x, last = turn(ff_parts, ff_x, ff_y, last)
        ff_last = (last_y, last_x)
    head_rows = 8

    def halve_first(parts, by_x, by_y, last_y, last_x, *deps, extra=0):
        rows, columns = parts[3].shape
        keep, send = call(
            land_half_kernel,
            "land",
            meta,
            vm(parts[2], by_x, last_y, parts[3], by_y, last_x),
            [((rows // 2, columns + extra), BF16, "v")] * 2,
            deps=deps,
        )
        return keep, swap(send, "dp", nz, 1)

    def halve_next(keep, got, *deps, extra=0):
        rows, columns = keep.shape
        keep, send = call(
            functools.partial(halve_kernel, columns - extra),
            "halve",
            meta,
            vm(keep, got),
            [((rows // 2, columns), BF16, "v")] * 2,
            deps=deps,
        )
        return keep, swap(send, "dp", nz, 2)

    def quarter(keep, got, *deps):
        own = add(keep, got, *deps)
        return own, swap(own, "dp", nz, 1), swap(own, "dp", nz, 2)

    def quarters(own, by_low, by_high, *deps):
        return own, by_low, by_high, swap(after(by_high, *deps), "dp", nz, 1)

    def shards(four, *deps):
        columns = four[0].shape[1]
        return call(join_kernel, "join", meta, vm(*four), [((shard, columns), BF16, "v")] * 2, deps=deps)

    def attend_back(qkv, powers, g, att, sums, diag, name, *deps):
        return call(
            attend_back_kernel,
            name,
            meta,
            vm(qkv, powers, g, att, sums, diag),
            [((size, wide), BF16, "v"), ((head_rows, 2 * size), F32, "v")],
            [pltpu.VMEM((size, size), BF16), pltpu.VMEM((128, 2 * size), F32)],
            deps=deps,
        )

    diag = jnp.zeros((head_rows, 2 * size), F32)
    dqkv_own, diag = attend_back(
        qkv_own, powers_own, grad_keep, attended, sums_own, diag, "attend_back_own", last, grad_got
    )
    last = dqkv_own
    if fast:
        ff_keep, ff_one = halve_first(ff_parts, ff_x, ff_y, *ff_last, last)
        in_x = on_x.send(after(in_parts[0], dqkv_own))
        in_y = on_y.send(after(in_parts[1], dqkv_own))
        last = ff_keep
    dqkv_peer, diag = attend_back(
        qkv_peer, powers_peer, grad_got, given_att, sums_peer, diag, "attend_back_peer", last
    )
    last = diag
    if fast:
        ff_keep, ff_two = halve_next(ff_keep, ff_one, last)
        last = ff_keep
    got_att_peer = [peer(after(v, last)) for v in own_halves]
    if fast:
        at_plan = message_plan(2 * shard)
        at_plan = at_plan + [(n, 2 * shard, 16, 0, 0, width) for n in (0, 2)]
        at_outs = [((2 * shard + (16 if n in (0, 2) else 0), 4 * half), BF16, "v") for n in range(4)]
    else:
        at_plan = [(0, 0, width + 16, 0, 0, 0)]
        at_outs = [((width + 16, 4 * half), BF16, "v")]
    part_gh, *send_gh, small_grads = call(
        inputs_kernel,
        "inputs",
        meta,
        vm(dqkv_own, dqkv_peer, qkv_w, hidden_in, hidden_peer, grad_gain_two, diag, buckets),
        [((size, width), F32, "v")] + [((size, half), BF16, "v")] * 2 + [((16, 128), F32, "v")],
        [pltpu.VMEM((1, width), F32)],
        deps=(last,),
    )
    low_other = [peer(after(v, part_gh, *got_att_peer)) for v in low_given]
    last = part_gh
    if fast:
        last_y, last_x, last = turn(in_parts, in_x, in_y, last)
        in_last = (last_y, last_x)
    at_parts = call(
        functools.partial(weights_kernel, at_plan, len(at_outs)),
        "weights",
        meta,
        vm(
            normed,
            normed_peer,
            dqkv_own,
            dqkv_peer,
            attended,
            *got_att,
            given_att,
            *got_att_peer,
            low_mine,
            *low_other,
            small_grads,
        ),
        at_outs,
        [pltpu.VMEM((width + 16, 4 * half), BF16)],
        deps=(last,),
    )
    at_parts = list(at_parts)
    last = at_parts[0]
    if fast:
        at_x = on_x.send(at_parts[0])
        at_y = on_y.send(at_parts[1])
        in_keep, in_one = halve_first(in_parts, in_x, in_y, *in_last, last)
        last = in_keep
    other_gh = [peer(after(v, last)) for v in send_gh]
    part_branch, *send_branch = call(
        output_kernel,
        "output",
        meta,
        vm(act_own, act_peer, ff_w),
        [((size, width), F32, "v")] + [((size, half), BF16, "v")] * 2,
        deps=(last,),
    )
    last = part_branch
    (grad_hidden,) = call(
        hidden_kernel,
        "hidden",
        meta,
        vm(hidden_in, grad_residual, part_gh, *other_gh, gain_one),
        [((size, width), F32, "v")],
        deps=(last,),
    )
    last = grad_hidden

    if fast:
        ff_four = quarter(ff_keep, ff_two, last)
        last_y, last_x, last = turn(at_parts, at_x, at_y, ff_four[0])
        at_last = (last_y, last_x)
        in_keep, in_two = halve_next(in_keep, in_one, last)
        ff_four = quarters(*ff_four, in_keep)
        at_keep, at_one = halve_first(at_parts, at_x, at_y, *at_last, in_keep, extra=128)
        in_four = quarter(in_keep, in_two, at_keep)
        (grad_ffout,) = call(
            join_rows_kernel,
            "join_rows",
            meta,
            vm(*ff_four),
            [((block, width), F32, "v")],
            deps=(in_four[0],),
        )
        last = grad_ffout
        other_branch = [peer(after(v, last)) for v in send_branch]
    else:
        other_branch = [peer(v) for v in send_branch]
    hidden_out, pooled, stats = call(
        finish_kernel,
        "finish",
        meta,
        vm(residual, part_branch, *other_branch, sums),
        [((size, width), BF16, "v"), ((1, width), F32, "v"), ((1, width), F32, "v")],
        deps=(last,),
    )
    last = stats
    if fast:
        at_keep, at_two = halve_next(at_keep, at_one, last, extra=128)
        in_four = quarters(*in_four, at_keep)
        mine_in, other_in = shards(in_four, at_keep)
        got_in = peer(other_in)
        own_at, small_grads = call(
            last_kernel,
            "last",
            meta,
            vm(at_keep, at_two),
            [((shard // 2, 4 * half), BF16, "v"), ((16, 128), F32, "v")],
            deps=(mine_in,),
        )
        at_four = own_at, swap(own_at, "dp", nz, 1), swap(own_at, "dp", nz, 2)
        small_grads = small_grads + peer(small_grads)
        (grad_in,) = call(
            functools.partial(weave_in_kernel, block),
            "weave_in",
            meta,
            vm(mine_in, got_in),
            [((shard, full_ff), F32, "v")],
            deps=(own_at,),
        )
        at_four = quarters(*at_four, grad_in)
        mine_at, other_at = shards(at_four, small_grads)
        got_at = peer(other_at)
        grad_at = call(
            weave_at_kernel, "weave_at", meta, vm(mine_at, got_at), [((shard, width), F32, "v")] * 4
        )
    else:

        def reduced(v):
            v = lax.psum_scatter(v, "fsdp", scatter_dimension=0, tiled=True)
            return lax.psum(v, "dp").astype(F32)

        def spread(v, axis):
            none = jnp.zeros_like(v)
            return by_core(jnp.stack([v, none], axis), jnp.stack([none, v], axis))

        grad_ffout = reduced(
            spread(ff_parts[0].reshape(nf // 2, block, width), 1).reshape(full_ff, width)
        )
        grad_in = reduced(
            spread(in_parts[0].reshape(width, nf // 2, block), 2).reshape(width, full_ff)
        )
        grads = spread(at_parts[0][:width].reshape(width, 4, half), 2).reshape(width, 4 * width)
        grads = reduced(grads)
        grad_at = [grads[:, n * width : (n + 1) * width] for n in range(4)]
        small_grads = lax.psum(small_grads, ("fsdp", "dp"))

    count = width // 128
    rows = levels // nf
    table = small_grads[2 * count :].reshape(-1)[: heads * levels].reshape(heads, levels)
    grad_table = lax.dynamic_slice_in_dim(table, me * rows, rows, 1).T
    gains = small_grads[: 2 * count].reshape(2, width)
    gains = lax.dynamic_slice_in_dim(gains, me * shard, shard, 1)
    return (
        hidden_out,
        pooled,
        grad_hidden,
        gains[0],
        grad_at[0],
        grad_at[1],
        grad_at[2],
        grad_at[3],
        grad_table,
        gains[1],
        grad_in,
        grad_ffout,
        stats[:, :3],
    )


def solution(mesh):
    token = P(("fsdp", "dp"), None)
    weight = P("fsdp", None)
    return jax.shard_map(
        functools.partial(body, mesh.shape["fsdp"], mesh.shape["dp"]),
        mesh=mesh,
        in_specs=(
            token,
            P("fsdp"),
            weight,
            weight,
            weight,
            weight,
            weight,
            P("fsdp"),
            weight,
            weight,
            P(),
            P(("fsdp", "dp")),
            P(("fsdp", "dp")),
            token,
            token,
        ),
        out_specs=(
            token,
            token,
            token,
            P("fsdp"),
            weight,
            weight,
            weight,
            weight,
            weight,
            P("fsdp"),
            weight,
            weight,
            token,
        ),
        check_vma=False,
    )
```

```python
import functools
import math

import jax
import jax.numpy as jnp
from jax import lax
from jax.experimental import pallas as pl
from jax.experimental.pallas import tpu as pltpu
from jax.sharding import PartitionSpec as P

EPS = 1e-06
F32 = jnp.float32
BF16 = jnp.bfloat16
VMEM_SPARE = 3 * 2**20
WEIGHTS = {"turn": 30.0, "expand_own": 30.0}
GELU_A = 0.7978845608028654
GELU_B = 0.044715


def dot(a, b):
    return lax.dot_general(a, b, (((1,), (0,)), ((), ())), preferred_element_type=F32)


def dot_right(a, b):
    return lax.dot_general(a, b, (((1,), (1,)), ((), ())), preferred_element_type=F32)


def dot_left(a, b):
    return lax.dot_general(a, b, (((0,), (0,)), ((), ())), preferred_element_type=F32)


def iota(shape, dim):
    return lax.broadcasted_iota(jnp.int32, shape, dim)


def call(kernel, name, meta, ins, outs, scratch=(), deps=(), limit=0):
    spaces = {"v": pltpu.VMEM, "s": pltpu.SMEM, "h": pl.ANY}
    held = [(a.shape, a.dtype) for a, m in ins if m == "v"]
    held += [(s, d) for s, d, m in outs if m == "v"]
    held += [(x.shape, x.dtype) for x in scratch if x.memory_space == pltpu.VMEM]
    need = sum(math.prod(s) * jnp.dtype(d).itemsize for s, d in held)
    ins = [(after(meta, *deps), "s")] + list(ins)
    return pl.pallas_call(
        kernel,
        name=name,
        out_shape=[jax.ShapeDtypeStruct(s, d) for s, d, _ in outs],
        in_specs=[pl.BlockSpec(memory_space=spaces[m]) for _, m in ins],
        out_specs=[pl.BlockSpec(memory_space=spaces[m]) for _, _, m in outs],
        scratch_shapes=list(scratch),
        compiler_params=pltpu.CompilerParams(vmem_limit_bytes=max(limit, need + VMEM_SPARE)),
        cost_estimate=pl.CostEstimate(
            flops=1000, bytes_accessed=int(3.7e6 * WEIGHTS.get(name, 0.0)) + 1000, transcendentals=0
        ),
    )(*[a for a, _ in ins])


def after(v, *deps):
    return lax.optimization_barrier((v,) + deps)[0] if deps else v


def place(meta, pieces, targets, copies):
    for src, row, rows, from_column, dst, base, column, width, unit, far, side in copies:
        start = base
        if unit:
            start = base + unit * jnp.bitwise_xor(meta[1], far)
            if side == 1:
                start = start + (unit // 2) * meta[2]
            if side == 2:
                start = start + (unit // 2) * (1 - meta[2])
            start = pl.multiple_of(start, 16)
        targets[dst][pl.ds(start, rows), column : column + width] = pieces[src][
            row : row + rows, from_column : from_column + width
        ]


def rows_loop(count, step, fn):
    def one(i, carry):
        fn(pl.ds(pl.multiple_of(i * step, step), step))
        return carry

    lax.fori_loop(0, count // step, one, 0)


def scatter_out(meta, scratch, outs, plan):
    for dst, row, rows, unit, far, offset in plan:
        start = offset
        if unit:
            start = pl.multiple_of(offset + unit * jnp.bitwise_xor(meta[1], far), 16)
        outs[dst][row : row + rows, :] = scratch[pl.ds(start, rows), :]


def small_block(meta, gain_one, gain_two, rel):
    row, lane = iota((16, 128), 0), iota((16, 128), 1)
    block = jnp.where((row == 2) & (lane == 0), (meta[4] // 256).astype(F32), 0.0)
    block = jnp.where((row == 2) & (lane == 1), (meta[4] % 256).astype(F32), block)
    parts = [(0, gain_one), (1, gain_two)] + [(4 + n, rel[n : n + 1, :]) for n in range(rel.shape[0])]
    for at, value in parts:
        value = value[...].astype(F32)
        wide = jnp.concatenate([value, jnp.zeros((1, 128 - value.shape[1]), F32)], axis=1)
        block = jnp.where(row == at, wide, block)
    return block.astype(BF16)


def pack_kernel(n_chips, meta, *refs):
    sources = refs[:5]
    gain_one, gain_two, rel = refs[5:8]
    kept_a, given_a, kept_b, given_b = refs[8:12]
    held, sems = refs[12:17], refs[17]
    handles = [pltpu.make_async_copy(a, b, sems.at[n]) for n, (a, b) in enumerate(zip(sources, held))]
    for handle in handles:
        handle.start()
    width = 4 * (held[0].shape[1] // 2)
    block = small_block(meta, gain_one, gain_two, rel)
    for out in (kept_a, given_a):
        out[:, width:] = jnp.zeros((out.shape[0], 128), BF16)
        out[0:16, width:] = block
    for handle in handles:
        handle.wait()
    wq, wk, wv, wo, w_in = held
    core = meta[2]
    half = wq.shape[1] // 2
    block = w_in.shape[1] // (2 * n_chips)
    for which, a_ref, b_ref in ((core, kept_a, kept_b), (1 - core, given_a, given_b)):
        for n, w in enumerate((wq, wk, wv, wo)):
            cols = pl.ds(pl.multiple_of(which * half, 128), half)
            a_ref[:, n * half : (n + 1) * half] = w[:, cols]
        for n in range(b_ref.shape[1] // block):
            cols = pl.ds(pl.multiple_of((2 * n + which) * block, 128), block)
            b_ref[:, n * block : (n + 1) * block] = w_in[:, cols]


def stack_kernel(meta, kept, taken, both):
    shard = kept.shape[0]
    both[pl.ds(pl.multiple_of(shard * meta[2], 16), shard), :] = kept[...]
    both[pl.ds(pl.multiple_of(shard * (1 - meta[2]), 16), shard), :] = taken[...]


def cut_kernel(meta, by_x, by_y, upper, lower):
    h = upper.shape[0]
    upper[...] = by_x[:h, :]
    lower[...] = by_y[h:, :]


def low_kernel(meta, out_cot, pool_cot, low):
    size = low.shape[0]
    length, prefix = meta[4], meta[5]
    count = (length - prefix).astype(F32)

    def lows(ds):
        t = iota((256, 1), 0) + ds.start
        pool = jnp.where((t >= prefix) & (t < length), 1.0, 0.0) / count
        low[ds, :] = (out_cot[ds, :].astype(F32) + pool * pool_cot[...]).astype(BF16)

    rows_loop(size, 256, lows)


def prepare_kernel(copies, n_pieces, levels, meta, hidden, hidden_peer, buckets, *refs):
    pieces = refs[:n_pieces]
    normed, normed_peer, bias, gain_one, gain_two, length_peer = refs[n_pieces : n_pieces + 6]
    rest = refs[n_pieces + 6 :]
    if copies:
        qkv, w_half, table, table_rows = rest
        place(meta, pieces, (qkv, w_half), copies)
        count = n_pieces
        column = pieces[0].shape[1] - 128
        blocks = [ref[0:16, column:].astype(F32) for ref in pieces]
        places = [jnp.bitwise_xor(meta[0], 2 * (p % 4) + p // 4) for p in range(count)]
    else:
        table, table_rows = rest
        count = pieces[0].shape[0] // 16
        blocks = [pieces[0][16 * p : 16 * p + 16, :].astype(F32) for p in range(count)]
        places = [jnp.int32(p) for p in range(count)]
    size, width = hidden.shape
    shard = width // count
    some = levels // count
    table[...] = jnp.zeros_like(table)
    first = jnp.zeros((1, width), F32)
    second = jnp.zeros((1, width), F32)
    rest = jnp.zeros((1, width - 128), F32)
    peers = jnp.zeros((1, 1), F32)
    for where, piece in zip(places, blocks):
        first += pltpu.roll(jnp.concatenate([piece[0:1], rest], axis=1), shard * where, 1)
        second += pltpu.roll(jnp.concatenate([piece[1:2], rest], axis=1), shard * where, 1)
        length = 256.0 * piece[2:3, 0:1] + piece[2:3, 1:2]
        peers += jnp.where(where == jnp.bitwise_xor(meta[0], 1), length, 0.0)
        for b in range(some):
            table[pl.ds(some * where + b, 1), :] = piece[4 + b : 5 + b]
    length_peer[...] = jnp.broadcast_to(peers, (1, 128))
    gain_one[...] = first
    gain_two[...] = second

    for x_ref, n_ref in ((hidden, normed), (hidden_peer, normed_peer)):

        def rows(ds, x_ref=x_ref, n_ref=n_ref):
            x = x_ref[ds, :].astype(F32)
            inv = lax.rsqrt(jnp.mean(x * x, axis=-1, keepdims=True) + EPS)
            n_ref[ds, :] = (x * inv * gain_one[...]).astype(BF16)

        rows_loop(size, 256, rows)

    span = 2 * size
    hot = (buckets[...] == iota((levels, span), 0)).astype(BF16)
    table_rows[...] = dot_left(table[...].astype(BF16), hot)
    heads, _, wide = bias.shape
    base = heads * meta[2]

    def head(h, carry):
        row = table_rows[pl.ds(base + h, 1), :]
        first = jnp.broadcast_to(pltpu.roll(row, span - 127, 1), (8, span))
        sub = iota((8, span), 0)
        full = first
        for k in range(1, 8):
            full = jnp.where(sub == k, pltpu.roll(first, k, 1), full)
        bias[h, 0:8, :] = full[:, :wide]
        have = 8
        while have < 128:
            more = pltpu.roll(full, have, 1)
            bias[h, have : 2 * have, :] = more[:, :wide]
            full = jnp.concatenate([full, more], axis=0)
            have *= 2
        return carry

    lax.fori_loop(0, heads, head, 0, unroll=True)


def attend_kernel(meta, x_ref, bias, w, length, qkv, out, upper, lower, powers, inv_sums, scores):
    size = x_ref.shape[0]
    part = w.shape[1] // 3
    pairs = part // 128
    lane = iota((1, 128), 1)
    half = lane < 64
    strips = size // 128
    inv_sums[...] = jnp.zeros_like(inv_sums)

    def project(ds):
        for n in range(3):
            cols = slice(n * part, (n + 1) * part)
            qkv[ds, cols] = dot(x_ref[ds, :], w[:, cols]).astype(BF16)

    rows_loop(size, size, project)
    masked = jnp.where(iota((size, 1), 0).astype(F32) < length[0:1, 0:1], 0.0, -1e30).astype(F32)

    def pair(p, carry):
        base = pl.multiple_of(p * 128, 128)
        qp = qkv[:, pl.ds(base, 128)].astype(F32)
        kp = qkv[:, pl.ds(base + part, 128)].astype(F32)
        vp = qkv[:, pl.ds(base + 2 * part, 128)].astype(F32)
        joined = None
        for side in range(2):
            head = 2 * p + side
            own = half if side == 0 else jnp.logical_not(half)
            spare = lane == (64 if side == 0 else 0)
            qa = jnp.where(own, qp, jnp.where(spare, 1.0, 0.0)).astype(BF16)
            ka = jnp.where(own, kp, jnp.where(spare, masked, 0.0)).astype(BF16)
            va = jnp.where(own, vp, jnp.where(spare, 1.0, 0.0)).astype(BF16)
            top = None
            for a in range(strips):
                rows = slice(128 * a, 128 * a + 128)
                off = 128 * (strips - 1 - a)
                s = dot_right(ka[rows], qa) + bias[head, :, off : off + size]
                scores[rows, :] = s
                peak = jnp.max(s, axis=0, keepdims=True)
                top = peak if top is None else jnp.maximum(top, peak)
            for a in range(strips):
                rows = slice(128 * a, 128 * a + 128)
                powers[head, rows, :] = jnp.exp(scores[rows, :] - top).astype(BF16)
            mixed = dot_left(va, powers[head]).T
            sums = jnp.sum(jnp.where(spare, mixed, 0.0), axis=1, keepdims=True)
            inv = 1.0 / sums
            inv_sums[...] = jnp.where(lane == head, inv, inv_sums[...])
            mixed = mixed * inv
            joined = mixed if side == 0 else jnp.where(half, joined, mixed)
        joined = joined.astype(BF16)
        cols = pl.ds(base, 128)
        out[:, cols] = joined
        upper[:, cols] = joined[: size // 2]
        lower[:, cols] = joined[size // 2 :]
        return carry

    lax.fori_loop(0, pairs, pair, 0, unroll=True)


def residual_kernel(meta, hidden, attended, upper, lower, gain, w_half, w_other, residual, normed, left, middle, right, sums, w_out):
    size, width = hidden.shape
    half = width // 2
    length = meta[4]
    core = meta[2]
    w_out[:, pl.ds(pl.multiple_of(core * half, 128), half)] = w_half[...]
    w_out[:, pl.ds(pl.multiple_of((1 - core) * half, 128), half)] = w_other[...]
    mine = pl.ds(pl.multiple_of(core * half, 128), half)
    other = pl.ds(pl.multiple_of((1 - core) * half, 128), half)
    sums[...] = jnp.zeros_like(sums)

    for first, got in ((0, upper), (size // 2, lower)):
        ds = slice(first, first + size // 2)
        x = hidden[ds, :].astype(F32)
        branch = dot(attended[ds, :], w_out[mine, :]) + dot(got[...], w_out[other, :])
        live = (iota((size // 2, 1), 0) + first) < length
        sums[0:1, :] += jnp.sum(jnp.where(live, x * x, 0.0), axis=0, keepdims=True)
        sums[1:2, :] += jnp.sum(jnp.where(live, branch * branch, 0.0), axis=0, keepdims=True)
        r = x + branch
        residual[ds, :] = r
        inv = lax.rsqrt(jnp.mean(r * r, axis=-1, keepdims=True) + EPS)
        value = (r * inv * gain[...]).astype(BF16)
        normed[ds, :] = value
        third = left.shape[1]
        for n, ref in enumerate((left, middle, right)):
            ref[ds, :] = value[:, n * third : (n + 1) * third]


def expand_kernel(copies, n_pieces, *refs):
    meta, x_ref = refs[:2]
    pieces = refs[2 : 2 + n_pieces]
    if copies:
        activated, slope, w_in = refs[2 + n_pieces :]
        place(meta, pieces, (w_in,), copies)
    else:
        w_in = pieces[0]
        activated, slope, whole = refs[2 + n_pieces :]
        third = x_ref.shape[1]
        for n, ref in enumerate((x_ref, *pieces[1:])):
            whole[:, n * third : (n + 1) * third] = ref[...]
        x_ref = whole
    chunk = 512 if w_in.shape[1] % 512 == 0 else 256

    def rows(ds):
        x = x_ref[ds, :]
        for c in range(0, w_in.shape[1], chunk):
            t = dot(x, w_in[:, c : c + chunk])
            square = t * t
            th = jnp.tanh(t * (GELU_A + (GELU_A * GELU_B) * square))
            phi = 0.5 + 0.5 * th
            activated[ds, c : c + chunk] = (t * phi).astype(BF16)
            inner = GELU_A + (3.0 * GELU_A * GELU_B) * square
            slope[ds, c : c + chunk] = (phi + 0.5 * t * (1.0 - th * th) * inner).astype(BF16)

    rows_loop(x_ref.shape[0], x_ref.shape[0], rows)


def product_kernel(plan, n_out, *refs):
    meta, left_own, left_peer, right_own, right_peer = refs[:5]
    outs = refs[5 : 5 + n_out]
    grads = refs[5 + n_out]
    step = 512 if grads.shape[0] % 512 == 0 else 384
    for c in range(0, grads.shape[0], step):
        part = dot_left(left_own[:, c : c + step], right_own[...])
        part += dot_left(left_peer[:, c : c + step], right_peer[...])
        grads[c : c + step, :] = part.astype(BF16)
    scatter_out(meta, grads, outs, plan)


def contract_kernel(copies, n_pieces, *refs):
    meta, slope_own, slope_peer, low_own, low_peer, w_in = refs[:6]
    pieces = refs[6 : 6 + n_pieces]
    pre_own, pre_peer, part_own, *sends, w_ffout = refs[6 + n_pieces :]
    third = sends[0].shape[1]
    place(meta, pieces, (w_ffout,), copies)
    size = low_own.shape[0]
    chunk = 512 if w_in.shape[1] % 512 == 0 else 256
    for slope, low, grad_pre, part in (
        (slope_peer, low_peer, pre_peer, sends),
        (slope_own, low_own, pre_own, (part_own,)),
    ):

        def rows(ds, slope=slope, low=low, grad_pre=grad_pre, part=part):
            y = low[ds, :]
            total = None
            for c in range(0, w_in.shape[1], chunk):
                g = dot_right(y, w_ffout[c : c + chunk, :])
                g = (slope[ds, c : c + chunk].astype(F32) * g).astype(BF16)
                grad_pre[ds, c : c + chunk] = g
                t = dot_right(g, w_in[:, c : c + chunk])
                total = t if total is None else total + t
            if len(part) > 1:
                for n, ref in enumerate(part):
                    ref[ds, :] = total[:, n * third : (n + 1) * third].astype(BF16)
            else:
                part[0][ds, :] = total

        rows_loop(size, size, rows)


def through_kernel(meta, residual, part, left, center, right, out_cot, pool_cot, gain, w_half, w_other,
                   grad_residual, low_mine, upper, lower, grad_keep, grad_send, grad_gain):
    size, width = residual.shape
    half = width // 2
    core = meta[2]
    mine = pl.ds(pl.multiple_of(core * half, 128), half)
    theirs = pl.ds(pl.multiple_of((1 - core) * half, 128), half)
    length, prefix = meta[4], meta[5]
    count = (length - prefix).astype(F32)
    grad_gain[...] = jnp.zeros_like(grad_gain)

    def rows(ds, low_given, start):
        x = residual[ds, :]
        gn = part[ds, :] + jnp.concatenate([left[ds, :], center[ds, :], right[ds, :]], axis=1).astype(F32)
        inv = lax.rsqrt(jnp.mean(x * x, axis=-1, keepdims=True) + EPS)
        u = gain[...] * gn
        xr = x * inv
        t = iota((256, 1), 0) + ds.start
        pool = jnp.where((t >= prefix) & (t < length), 1.0, 0.0) / count
        go = out_cot[ds, :].astype(F32) + pool * pool_cot[...]
        g = go + inv * (u - xr * jnp.mean(xr * u, axis=-1, keepdims=True))
        grad_gain[...] += jnp.sum(xr * gn, axis=0, keepdims=True)
        grad_residual[ds, :] = g
        first, second = g[:, :half].astype(BF16), g[:, half:].astype(BF16)
        on_first = jnp.broadcast_to(core == 0, first.shape)
        a = jnp.where(on_first, g[:, :half], g[:, half:]).astype(BF16)
        b = jnp.where(on_first, g[:, half:], g[:, :half]).astype(BF16)
        low_mine[ds, :] = a
        low_given[pl.ds(ds.start - start, 256), :] = b
        grad_keep[ds, :] = (dot_right(a, w_half[mine, :]) + dot_right(b, w_other[mine, :])).astype(BF16)
        grad_send[ds, :] = (dot_right(a, w_half[theirs, :]) + dot_right(b, w_other[theirs, :])).astype(BF16)

    middle = size // 2
    for first, low_given in ((0, upper), (middle, lower)):

        def some(i, carry, first=first, low_given=low_given):
            rows(pl.ds(pl.multiple_of(first + 256 * i, 256), 256), low_given, first)
            return carry

        lax.fori_loop(0, middle // 256, some, 0)


def attend_back_kernel(meta, qkv, powers, g_ref, a_ref, inv_sums, diag_in, out, diag, grads, slant):
    size = g_ref.shape[0]
    part = qkv.shape[1] // 3
    pairs = part // 128
    strips = size // 128
    span = 2 * size
    lane = iota((1, 128), 1)
    half = lane < 64
    diag[...] = diag_in[...]

    def pair(p, carry):
        base = pl.multiple_of(p * 128, 128)
        cols = pl.ds(base, 128)
        kcols = pl.ds(base + part, 128)
        vcols = pl.ds(base + 2 * part, 128)
        qp, kp = qkv[:, cols], qkv[:, kcols]
        vp = qkv[:, vcols].astype(F32)
        do = g_ref[:, cols].astype(F32)
        prod = do * a_ref[:, cols].astype(F32)
        dq_all = dk_all = dv_all = None
        for side in range(2):
            head = 2 * p + side
            own = half if side == 0 else jnp.logical_not(half)
            one = 64 if side == 0 else 0
            inv = jnp.sum(jnp.where(lane == head, inv_sums[...], 0.0), axis=1, keepdims=True)
            inner = jnp.sum(jnp.where(own, prod, 0.0), axis=1, keepdims=True) * inv
            upper = inner.astype(BF16).astype(F32)
            dos = jnp.where(
                own,
                do * inv,
                jnp.where(lane == one, -upper, jnp.where(lane == one + 1, upper - inner, 0.0)),
            ).astype(BF16)
            ones = (lane == one) | (lane == one + 1)
            va = jnp.where(own, vp, jnp.where(ones, 1.0, 0.0)).astype(BF16)
            slant[...] = jnp.zeros_like(slant)
            for a in range(strips):
                rows = slice(128 * a, 128 * a + 128)
                off = 128 * (strips - 1 - a)
                ds = (powers[head, rows, :].astype(F32) * dot_right(va[rows], dos)).astype(BF16)
                grads[rows, :] = ds
                slant[:, off : off + size] += ds.astype(F32)
            dk = dot(grads[...], qp)
            dv = dot(powers[head], dos)
            dk_all = dk if side == 0 else jnp.where(half, dk_all, dk)
            dv_all = dv if side == 0 else jnp.where(half, dv_all, dv)
            dq = dot_left(kp, grads[...]).T
            dq_all = dq if side == 0 else jnp.where(half, dq_all, dq)
            y = slant[...]
            rest = 64
            while rest >= 1:
                y = y[:rest] + pltpu.roll(y[rest:], span - rest, 1)
                rest //= 2
            diag[pl.ds(head, 1), :] += pltpu.roll(y, 127, 1)
        out[:, cols] = dq_all.astype(BF16)
        out[:, kcols] = dk_all.astype(BF16)
        out[:, vcols] = dv_all.astype(BF16)
        return carry

    lax.fori_loop(0, pairs, pair, 0, unroll=True)


def weights_kernel(plan, n_out, *refs):
    meta, x_own, x_peer, dqkv_own, dqkv_peer, att_own, upper, lower, att_peer, got_upper, got_lower, low_own, low_upper, low_lower, small = refs[:15]
    outs = refs[15 : 15 + n_out]
    (grads,) = refs[15 + n_out :]
    middle = upper.shape[0]
    part = dqkv_own.shape[1]
    depth = x_own.shape[1]
    half = depth // 2
    for c in range(0, depth, 384):
        cols = slice(c, c + 384)
        g = dot_left(x_own[:, cols], dqkv_own[...]) + dot_left(x_peer[:, cols], dqkv_peer[...])
        grads[cols, 0:part] = g.astype(BF16)
    core = meta[2]
    mine = pl.multiple_of(core * half, 16)
    theirs = pl.multiple_of((1 - core) * half, 16)
    for c in range(0, half, 384):
        cols = slice(c, c + 384)
        g = dot_left(att_own[:, cols], low_own[...]) + dot_left(att_peer[:middle, cols], low_upper[...])
        g += dot_left(att_peer[middle:, cols], low_lower[...])
        grads[pl.ds(mine + c, 384), part:] = g.astype(BF16)
        g = dot_left(upper[:, cols], low_own[:middle]) + dot_left(lower[:, cols], low_own[middle:])
        g += dot_left(got_upper[:, cols], low_upper[...])
        g += dot_left(got_lower[:, cols], low_lower[...])
        grads[pl.ds(theirs + c, 384), part:] = g.astype(BF16)
    grads[depth:, :] = jnp.zeros((16, grads.shape[1]), BF16)
    grads[depth:, 0:128] = small[...].astype(BF16)
    scatter_out(meta, grads, outs, plan)


def inputs_kernel(meta, dqkv_own, dqkv_peer, w, hidden, hidden_peer, gain_two, diag, buckets,
                  part_own, left, right, small, gain_one):
    size, width = part_own.shape
    half = width // 2
    small[...] = jnp.zeros_like(small)
    gain_one[...] = jnp.zeros_like(gain_one)

    def share(x_ref, ds, value):
        x = x_ref[ds, :].astype(F32)
        inv = lax.rsqrt(jnp.mean(x * x, axis=-1, keepdims=True) + EPS)
        gain_one[...] += jnp.sum(x * inv * value, axis=0, keepdims=True)

    def peers(ds):
        value = dot_right(dqkv_peer[ds, :], w[...])
        share(hidden_peer, ds, value)
        value = value.astype(BF16)
        left[ds, :] = value[:, :half]
        right[ds, :] = value[:, half:]

    def own(ds):
        value = dot_right(dqkv_own[ds, :], w[...])
        share(hidden, ds, value)
        part_own[ds, :] = value

    rows_loop(size, size, peers)
    rows_loop(size, size, own)
    count = width // 128
    for n in range(count):
        small[n : n + 1, :] = gain_one[:, 128 * n : 128 * n + 128]
        small[count + n : count + n + 1, :] = gain_two[:, 128 * n : 128 * n + 128]
    hot = (buckets[...] == iota((128, diag.shape[1]), 0)).astype(F32)
    table = lax.dot_general(
        diag[...],
        hot,
        (((1,), (1,)), ((), ())),
        preferred_element_type=F32,
        precision=lax.Precision.HIGHEST,
    )
    lane = iota((1, 128), 1)
    few = (16 - 2 * count) * 2 - 2
    for n in range(few):
        head = few * meta[2] + n
        row = jnp.where(lane < 32, table[n : n + 1, :], 0.0)
        small[pl.ds(2 * count + head // 4, 1), :] += pltpu.roll(row, 32 * (head % 4), 1)


def hidden_kernel(meta, hidden, grad_residual, part, left, right, gain, grad_hidden):
    def rows(ds):
        total = part[ds, :] + jnp.concatenate([left[ds, :], right[ds, :]], axis=1).astype(F32)
        x = hidden[ds, :].astype(F32)
        inv = lax.rsqrt(jnp.mean(x * x, axis=-1, keepdims=True) + EPS)
        u = gain[...] * total
        xr = x * inv
        grad_hidden[ds, :] = grad_residual[ds, :] + inv * (
            u - xr * jnp.mean(xr * u, axis=-1, keepdims=True)
        )

    rows_loop(hidden.shape[0], 256, rows)


def output_kernel(meta, act_own, act_peer, w_ffout, part_own, left, right):
    size, width = part_own.shape
    half = width // 2

    def peers(ds):
        value = dot(act_peer[ds, :], w_ffout[...]).astype(BF16)
        left[ds, :] = value[:, :half]
        right[ds, :] = value[:, half:]

    def own(ds):
        part_own[ds, :] = dot(act_own[ds, :], w_ffout[...])

    rows_loop(size, size, peers)
    rows_loop(size, size, own)


def finish_kernel(meta, residual, part, left, right, sums, hidden_out, pooled, stats):
    size, width = residual.shape
    length, prefix = meta[4], meta[5]
    count = (length - prefix).astype(F32)
    pooled[...] = jnp.zeros_like(pooled)
    stats[...] = jnp.zeros_like(stats)

    def rows(ds):
        branch = part[ds, :] + jnp.concatenate([left[ds, :], right[ds, :]], axis=1).astype(F32)
        out = residual[ds, :] + branch
        hidden_out[ds, :] = out.astype(BF16)
        t = iota((128, 1), 0) + ds.start
        live = t < length
        stats[0:1, :] += jnp.sum(jnp.where(live, branch * branch, 0.0), axis=0, keepdims=True)
        pooled[...] += jnp.sum(jnp.where((t >= prefix) & live, out, 0.0), axis=0, keepdims=True)

    rows_loop(size, 128, rows)
    pooled[...] = pooled[...] / count
    total = jnp.sum(stats[0:1, :])
    first = jnp.sum(sums[0:1, :])
    second = jnp.sum(sums[1:2, :])
    denominator = length.astype(F32) * width
    column = iota(stats.shape, 1)
    values = jnp.where(column == 0, first, jnp.where(column == 1, second, total))
    stats[...] = jnp.sqrt(values / denominator)


def total(*parts):
    value = parts[0].astype(F32)
    for part in parts[1:]:
        value = value + part.astype(F32)
    return value.astype(BF16)


def turn_kernel(meta, keep_a, got_x, keep_b, got_y, on_y, on_x):
    h = on_x.shape[0]
    on_y[...] = total(keep_a[h:], got_x[h:])
    on_x[...] = total(keep_b[h:], got_y[h:])


def add_kernel(meta, a, b, out):
    out[...] = total(a[...], b[...])


def land_half_kernel(meta, keep_a, got_x, last_y, keep_b, got_y, last_x, keep, send):
    h, width = last_x.shape
    upper = total(keep_a[:h], got_x[:h], last_y[:h])
    lower = total(keep_b[:h], got_y[:h], last_x[...])
    first = jnp.broadcast_to(meta[3] % 2 == 0, upper.shape)
    keep[:, :width] = jnp.where(first, upper.astype(F32), lower.astype(F32)).astype(BF16)
    send[:, :width] = jnp.where(first, lower.astype(F32), upper.astype(F32)).astype(BF16)
    if keep.shape[1] > width:
        rows = slice(2 * h, 2 * h + 16)
        small = total(keep_a[rows, 0:128], got_x[rows, 0:128], last_y[h:, 0:128])
        for out in (keep, send):
            out[:, width:] = jnp.zeros((h, 128), BF16)
            out[:16, width:] = small


def halve_kernel(width, meta, a, b, keep, send):
    h = keep.shape[0]
    place_at = pl.multiple_of(h * (meta[3] // 2), 16)
    other_at = pl.multiple_of(h * (1 - meta[3] // 2), 16)
    keep[:, :width] = total(a[pl.ds(place_at, h), :width], b[pl.ds(place_at, h), :width])
    send[:, :width] = total(a[pl.ds(other_at, h), :width], b[pl.ds(other_at, h), :width])
    if width < keep.shape[1]:
        extra = total(a[:h, width:], b[:h, width:])
        keep[:, width:] = extra
        send[:, width:] = extra


def last_kernel(meta, a, b, out, small):
    width = out.shape[1]
    out[...] = total(a[:, :width], b[:, :width])
    small[...] = a[:16, width:].astype(F32) + b[:16, width:].astype(F32)


def join_rows_kernel(meta, own, by_low, by_high, by_both, out):
    h = own.shape[0]
    low, high = meta[3] % 2, meta[3] // 2
    for value, at_low, at_high in (
        (own, low, high),
        (by_low, 1 - low, high),
        (by_high, low, 1 - high),
        (by_both, 1 - low, 1 - high),
    ):
        out[pl.ds(pl.multiple_of(h * (2 * at_low + at_high), 16), h), :] = value[...].astype(F32)


def join_kernel(meta, own, by_low, by_high, by_both, mine, other):
    h = own.shape[0]
    low, high = meta[3] % 2, meta[3] // 2
    for value, at_low, at_high in (
        (own, low, high),
        (by_low, 1 - low, high),
        (by_high, low, 1 - high),
        (by_both, 1 - low, 1 - high),
    ):
        rows = pl.ds(pl.multiple_of(h * at_high, 16), h)

        @pl.when(at_low == meta[2])
        def _(value=value, rows=rows):
            mine[rows, :] = value[...]

        @pl.when(at_low != meta[2])
        def _(value=value, rows=rows):
            other[rows, :] = value[...]


def weave_in_kernel(block, meta, mine, other, out):
    for which, ref in ((meta[2], mine), (1 - meta[2], other)):
        for n in range(ref.shape[1] // block):
            cols = pl.ds(pl.multiple_of((2 * n + which) * block, 128), block)
            out[:, cols] = ref[:, n * block : (n + 1) * block].astype(F32)


def weave_at_kernel(meta, mine, other, *outs):
    half = outs[0].shape[1] // 2
    for which, ref in ((meta[2], mine), (1 - meta[2], other)):
        cols = pl.ds(pl.multiple_of(which * half, 128), half)
        for n, out in enumerate(outs):
            out[:, cols] = ref[:, n * half : (n + 1) * half].astype(F32)


def swap(v, axis, count, far):
    return lax.ppermute(v, axis, [(i, i ^ far) for i in range(count)])


def message_plan(unit):
    h = unit // 2
    plan = []
    for dst, (near, far) in enumerate(((1, 3), (2, 3), (0, 2), (0, 1))):
        offset = 0 if dst in (0, 2) else h
        plan.append((dst, 0, h, unit, near, offset))
        plan.append((dst, h, h, unit, far, offset))
    return plan


class Link:
    def __init__(self, far):
        self.far = far
        self.sent = []

    def send(self, v):
        if len(self.sent) >= 2:
            v = after(v, self.sent[-2])
        got = swap(v, "fsdp", 8, self.far)
        self.sent.append(got)
        return got


def body(
    nf,
    nz,
    hidden_in,
    norm_gain_attn,
    w_query,
    w_key,
    w_value,
    w_out,
    rel_bias,
    norm_gain_ffn,
    w_in,
    w_ffout,
    bucket_index,
    row_lengths,
    prefix_lengths,
    out_cotangent,
    pool_cotangent,
):
    fast = nf == 8 and nz == 4
    size, width = hidden_in.shape
    shard = w_query.shape[0]
    heads = rel_bias.shape[1]
    levels = rel_bias.shape[0] * nf
    full_ff = w_in.shape[1]
    part_ff = full_ff // 2
    block = w_ffout.shape[0]
    half = width // 2
    few = heads // 2
    me = lax.axis_index("fsdp").astype(jnp.int32)
    where = lax.axis_index("dp").astype(jnp.int32)
    core = me & 1
    zero = jnp.zeros((), jnp.int32)

    def by_core(first, second):
        return jnp.where(core == 0, first, second)

    def peer(v):
        return swap(v, "fsdp", nf, 1)

    def dma(n):
        return pltpu.SemaphoreType.DMA((n,))

    def vm(*arrays):
        return [(a, "v") for a in arrays]

    meta = jnp.stack([me, me >> 1, core, where, row_lengths[0], prefix_lengths[0], zero, zero])
    hidden_peer = peer(hidden_in)
    wide = 3 * half
    buckets = jnp.concatenate([bucket_index[::-1], jnp.full((1,), -1, jnp.int32)])[None, :]

    if fast:
        kept_a, given_a, kept_b, given_b = call(
            functools.partial(pack_kernel, nf // 2),
            "pack",
            meta,
            [(a, "h") for a in (w_query, w_key, w_value, w_out, w_in)]
            + vm(norm_gain_attn[None], norm_gain_ffn[None], rel_bias),
            [((shard, 4 * half + 128), BF16, "v")] * 2 + [((shard, part_ff), BF16, "v")] * 2,
            [pltpu.VMEM(w.shape, BF16) for w in (w_query, w_key, w_value, w_out, w_in)] + [dma(5)],
            limit=56 * 2**20,
        )
        on_x, on_y = Link(2), Link(4)
        taken_a = peer(given_a)
        x_kept, y_taken = on_x.send(kept_a), on_y.send(taken_a)
        x_taken, y_kept = on_x.send(taken_a), on_y.send(kept_a)
        far_kept, far_taken = on_y.send(x_kept), on_x.send(y_taken)
        a_pieces = [kept_a, x_kept, y_kept, far_kept, taken_a, x_taken, y_taken, far_taken]
        a_copies = []
        for number in range(8):
            far, side = number % 4, 1 + number // 4
            a_copies.append((number, 0, shard, 0, 0, 0, 0, wide, 2 * shard, far, side))
            a_copies.append((number, 0, shard, wide, 1, 0, 0, half, 2 * shard, far, side))
        taken_b = peer(after(given_b, hidden_peer, taken_a))
        (both_b,) = call(
            stack_kernel,
            "stack",
            meta,
            vm(kept_b, taken_b),
            [((2 * shard, part_ff), BF16, "v")],
        )

        def near(v):
            return [v, on_x.send(v), on_y.send(v)]

        def distant(three, *deps):
            v, by_x, by_y = three
            h = v.shape[0] // 2
            upper, lower = call(
                cut_kernel, "cut", meta, vm(by_x, by_y), [((h, v.shape[1]), BF16, "v")] * 2, deps=deps
            )
            far_y, far_x = on_y.send(upper), on_x.send(lower)
            return three + [far_y, far_x]

        def rows_of(five):
            h = five[3].shape[0]
            return zip(five, (0, 0, 0, 0, h), (0, 1, 2, 3, 3))

    else:

        def whole(v):
            return lax.all_gather(v, "fsdp", axis=0, tiled=True)

        a_full = [whole(w) for w in (w_query, w_key, w_value, w_out)]
        a_full = [by_core(w[:, :half], w[:, half:]) for w in a_full]
        qkv_w, out_half = jnp.concatenate(a_full[:3], axis=1), a_full[3]
        b_full = whole(w_in).reshape(width, nf // 2, 2, block)
        b_pieces = [by_core(b_full[:, :, 0], b_full[:, :, 1]).reshape(width, part_ff)]
        b_copies = [(0, 0, width, 0, 0, 0, 0, part_ff, 0, 0, 0)]
        c_full = whole(w_ffout).reshape(nf // 2, 2, block, width)
        c_pieces = [by_core(c_full[:, 0], c_full[:, 1]).reshape(part_ff, width)]
        c_copies = [(0, 0, part_ff, 0, 0, 0, 0, width, 0, 0, 0)]
        length = row_lengths[0]
        split = jnp.stack([length // 256, length % 256]).astype(BF16)[None]
        rows = [norm_gain_attn[None], norm_gain_ffn[None], split, split, rel_bias]
        rows = [jnp.pad(r, ((0, 0), (0, 128 - r.shape[1]))) for r in rows]
        small = jnp.concatenate(rows, axis=0)
        a_pieces, a_copies = [whole(jnp.pad(small, ((0, 16 - small.shape[0]), (0, 0))))], ()

    (low,) = call(
        low_kernel, "low", meta, vm(out_cotangent, pool_cotangent), [((size, width), BF16, "v")]
    )
    normed, normed_peer, bias, gain_one, gain_two, length_peer, *weights = call(
        functools.partial(prepare_kernel, a_copies, len(a_pieces), levels),
        "prepare",
        meta,
        vm(hidden_in, hidden_peer, buckets, *a_pieces),
        [
            ((size, width), BF16, "v"),
            ((size, width), BF16, "v"),
            ((few, 128, 2 * size - 128), F32, "v"),
            ((1, width), F32, "v"),
            ((1, width), F32, "v"),
            ((1, 128), F32, "v"),
        ]
        + ([((width, wide), BF16, "v"), ((width, half), BF16, "v")] if fast else []),
        [pltpu.VMEM((levels, 128), F32), pltpu.VMEM((128, 2 * size), F32)],
        deps=(low,),
    )
    if fast:
        b_pieces = near(both_b)
        qkv_w, out_half = weights
    out_other = peer(out_half)

    def attend(x, length, name, *deps):
        return call(
            attend_kernel,
            name,
            meta,
            vm(x, bias, qkv_w, length),
            [
                ((size, wide), BF16, "v"),
                ((size, half), BF16, "v"),
                ((size // 2, half), BF16, "v"),
                ((size // 2, half), BF16, "v"),
                ((few, size, size), BF16, "v"),
                ((size, 128), F32, "v"),
            ],
            [pltpu.VMEM((size, size), F32)],
            deps=deps,
        )

    qkv_peer, given_att, *given_halves, powers_peer, sums_peer = attend(
        normed_peer, length_peer, "attend_peer"
    )
    low_peer = peer(after(low, given_att))
    if fast:
        b_pieces = distant(b_pieces, given_att)
        b_copies = [
            (number, 0, piece.shape[0], 0, 0, row, 0, part_ff, 2 * shard, far, 0)
            for number, (piece, row, far) in enumerate(rows_of(b_pieces))
        ]
        c_pieces = near(w_ffout)
    served = tuple(b_pieces[n] for n in (1, 2)) if fast else ()
    length_own = jnp.broadcast_to(row_lengths.astype(F32)[None], (1, 128))
    qkv_own, attended, *own_halves, powers_own, sums_own = attend(
        normed, length_own, "attend_own", given_att, out_other, *served
    )
    served = tuple(b_pieces[n] for n in (3, 4)) if fast else ()
    got_att = [peer(after(v, attended, *served)) for v in given_halves]
    residual, normed_two, *thirds, sums = call(
        residual_kernel,
        "residual",
        meta,
        vm(hidden_in, attended, *got_att, gain_two, out_half, out_other),
        [((size, width), F32, "v"), ((size, width), BF16, "v")]
        + [((size, width // 3), BF16, "v")] * 3
        + [((8, width), F32, "v")],
        [pltpu.VMEM((width, width), BF16)],
        deps=(low_peer,),
    )
    thirds = [peer(v) for v in thirds]
    shape_in = pltpu.VMEM((width, part_ff), BF16)
    shape_ff = pltpu.VMEM((part_ff, width), BF16)
    if fast:
        ff_plan, in_plan = message_plan(block), message_plan(2 * shard)
        ff_outs = [((block, width), BF16, "v")] * 4
        in_outs = [((2 * shard, part_ff), BF16, "v")] * 4
    else:
        ff_plan = [(0, 0, part_ff, 0, 0, 0)]
        in_plan = [(0, 0, width, 0, 0, 0)]
        ff_outs = [((part_ff, width), BF16, "v")]
        in_outs = [((width, part_ff), BF16, "v")]
    act_own, slope_own, in_w = call(
        functools.partial(expand_kernel, b_copies, len(b_pieces)),
        "expand_own",
        meta,
        vm(normed_two, *b_pieces),
        [((size, part_ff), BF16, "v")] * 2 + [((width, part_ff), BF16, "v")],
        deps=tuple(thirds),
    )
    if fast:
        c_pieces = distant(c_pieces, act_own)
        c_copies = [
            (number, 0, piece.shape[0], 0, 0, row, 0, width, block, far, 0)
            for number, (piece, row, far) in enumerate(rows_of(c_pieces))
        ]
    act_peer, slope_peer, normed_two_peer = call(
        functools.partial(expand_kernel, (), 3),
        "expand_peer",
        meta,
        vm(thirds[0], in_w, *thirds[1:]),
        [((size, part_ff), BF16, "v")] * 2 + [((size, width), BF16, "v")],
        deps=tuple(c_pieces[n] for n in (1, 2)) if fast else (),
    )
    ff_parts = call(
        functools.partial(product_kernel, ff_plan, len(ff_outs)),
        "product",
        meta,
        vm(act_own, act_peer, low, low_peer),
        ff_outs,
        [shape_ff],
    )
    ff_parts = list(ff_parts)
    if fast:
        ff_x = on_x.send(after(ff_parts[0], c_pieces[3], c_pieces[4]))
        ff_y = on_y.send(after(ff_parts[1], c_pieces[3], c_pieces[4]))
    pre_own, pre_peer, part_gn, *send_gn, ff_w = call(
        functools.partial(contract_kernel, c_copies, len(c_pieces)),
        "contract",
        meta,
        vm(slope_own, slope_peer, low, low_peer, in_w, *c_pieces),
        [((size, part_ff), BF16, "v")] * 2
        + [((size, width), F32, "v")]
        + [((size, width // 3), BF16, "v")] * 3
        + [((part_ff, width), BF16, "v")],
        deps=(ff_parts[0],),
    )
    in_parts = call(
        functools.partial(product_kernel, in_plan, len(in_outs)),
        "outer",
        meta,
        vm(normed_two, normed_two_peer, pre_own, pre_peer),
        in_outs,
        [shape_in],
    )
    in_parts = list(in_parts)
    last = in_parts[0]

    def turn(parts, by_x, by_y, *deps):
        h = parts[3].shape[0] // 2
        columns = parts[3].shape[1]
        to_y, to_x = call(
            turn_kernel,
            "turn",
            meta,
            vm(parts[2], by_x, parts[3], by_y),
            [((parts[2].shape[0] - h, columns), BF16, "v"), ((h, columns), BF16, "v")],
            deps=deps,
        )
        return on_y.send(to_y), on_x.send(to_x), to_y

    def add(a, b, *deps):
        (out,) = call(add_kernel, "add", meta, vm(a, b), [(a.shape, BF16, "v")], deps=deps)
        return out

    other_gn = [peer(v) for v in send_gn]
    grad_residual, low_mine, *low_given, grad_keep, grad_send, grad_gain_two = call(
        through_kernel,
        "through",
        meta,
        vm(residual, part_gn, *other_gn, out_cotangent, pool_cotangent, gain_two, out_half, out_other),
        [
            ((size, width), F32, "v"),
            ((size, half), BF16, "v"),
            ((size // 2, half), BF16, "v"),
            ((size // 2, half), BF16, "v"),
            ((size, half), BF16, "v"),
            ((size, half), BF16, "v"),
            ((1, width), F32, "v"),
        ],
        deps=(last,),
    )
    grad_got = peer(grad_send)
    last = grad_gain_two
    if fast:
        last_y, last_x, last = turn(ff_parts, ff_x, ff_y, last)
        ff_last = (last_y, last_x)
    head_rows = 8

    def halve_first(parts, by_x, by_y, last_y, last_x, *deps, extra=0):
        rows, columns = parts[3].shape
        keep, send = call(
            land_half_kernel,
            "land",
            meta,
            vm(parts[2], by_x, last_y, parts[3], by_y, last_x),
            [((rows // 2, columns + extra), BF16, "v")] * 2,
            deps=deps,
        )
        return keep, swap(send, "dp", nz, 1)

    def halve_next(keep, got, *deps, extra=0):
        rows, columns = keep.shape
        keep, send = call(
            functools.partial(halve_kernel, columns - extra),
            "halve",
            meta,
            vm(keep, got),
            [((rows // 2, columns), BF16, "v")] * 2,
            deps=deps,
        )
        return keep, swap(send, "dp", nz, 2)

    def quarter(keep, got, *deps):
        own = add(keep, got, *deps)
        return own, swap(own, "dp", nz, 1), swap(own, "dp", nz, 2)

    def quarters(own, by_low, by_high, *deps):
        return own, by_low, by_high, swap(after(by_high, *deps), "dp", nz, 1)

    def shards(four, *deps):
        columns = four[0].shape[1]
        return call(join_kernel, "join", meta, vm(*four), [((shard, columns), BF16, "v")] * 2, deps=deps)

    def attend_back(qkv, powers, g, att, sums, diag, name, *deps):
        return call(
            attend_back_kernel,
            name,
            meta,
            vm(qkv, powers, g, att, sums, diag),
            [((size, wide), BF16, "v"), ((head_rows, 2 * size), F32, "v")],
            [pltpu.VMEM((size, size), BF16), pltpu.VMEM((128, 2 * size), F32)],
            deps=deps,
        )

    diag = jnp.zeros((head_rows, 2 * size), F32)
    dqkv_own, diag = attend_back(
        qkv_own, powers_own, grad_keep, attended, sums_own, diag, "attend_back_own", last, grad_got
    )
    last = dqkv_own
    if fast:
        ff_keep, ff_one = halve_first(ff_parts, ff_x, ff_y, *ff_last, last)
        in_x = on_x.send(after(in_parts[0], dqkv_own))
        in_y = on_y.send(after(in_parts[1], dqkv_own))
        last = ff_keep
    dqkv_peer, diag = attend_back(
        qkv_peer, powers_peer, grad_got, given_att, sums_peer, diag, "attend_back_peer", last
    )
    last = diag
    if fast:
        ff_keep, ff_two = halve_next(ff_keep, ff_one, last)
        last = ff_keep
    got_att_peer = [peer(after(v, last)) for v in own_halves]
    if fast:
        at_plan = message_plan(2 * shard)
        at_plan = at_plan + [(n, 2 * shard, 16, 0, 0, width) for n in (0, 2)]
        at_outs = [((2 * shard + (16 if n in (0, 2) else 0), 4 * half), BF16, "v") for n in range(4)]
    else:
        at_plan = [(0, 0, width + 16, 0, 0, 0)]
        at_outs = [((width + 16, 4 * half), BF16, "v")]
    part_gh, *send_gh, small_grads = call(
        inputs_kernel,
        "inputs",
        meta,
        vm(dqkv_own, dqkv_peer, qkv_w, hidden_in, hidden_peer, grad_gain_two, diag, buckets),
        [((size, width), F32, "v")] + [((size, half), BF16, "v")] * 2 + [((16, 128), F32, "v")],
        [pltpu.VMEM((1, width), F32)],
        deps=(last,),
    )
    low_other = [peer(after(v, part_gh, *got_att_peer)) for v in low_given]
    last = part_gh
    if fast:
        last_y, last_x, last = turn(in_parts, in_x, in_y, last)
        in_last = (last_y, last_x)
    at_parts = call(
        functools.partial(weights_kernel, at_plan, len(at_outs)),
        "weights",
        meta,
        vm(
            normed,
            normed_peer,
            dqkv_own,
            dqkv_peer,
            attended,
            *got_att,
            given_att,
            *got_att_peer,
            low_mine,
            *low_other,
            small_grads,
        ),
        at_outs,
        [pltpu.VMEM((width + 16, 4 * half), BF16)],
        deps=(last,),
    )
    at_parts = list(at_parts)
    last = at_parts[0]
    if fast:
        at_x = on_x.send(at_parts[0])
        at_y = on_y.send(at_parts[1])
        in_keep, in_one = halve_first(in_parts, in_x, in_y, *in_last, last)
        last = in_keep
    other_gh = [peer(after(v, last)) for v in send_gh]
    part_branch, *send_branch = call(
        output_kernel,
        "output",
        meta,
        vm(act_own, act_peer, ff_w),
        [((size, width), F32, "v")] + [((size, half), BF16, "v")] * 2,
        deps=(last,),
    )
    last = part_branch
    (grad_hidden,) = call(
        hidden_kernel,
        "hidden",
        meta,
        vm(hidden_in, grad_residual, part_gh, *other_gh, gain_one),
        [((size, width), F32, "v")],
        deps=(last,),
    )
    last = grad_hidden

    if fast:
        ff_four = quarter(ff_keep, ff_two, last)
        last_y, last_x, last = turn(at_parts, at_x, at_y, ff_four[0])
        at_last = (last_y, last_x)
        in_keep, in_two = halve_next(in_keep, in_one, last)
        ff_four = quarters(*ff_four, in_keep)
        at_keep, at_one = halve_first(at_parts, at_x, at_y, *at_last, in_keep, extra=128)
        in_four = quarter(in_keep, in_two, at_keep)
        (grad_ffout,) = call(
            join_rows_kernel,
            "join_rows",
            meta,
            vm(*ff_four),
            [((block, width), F32, "v")],
            deps=(in_four[0],),
        )
        last = grad_ffout
        other_branch = [peer(after(v, last)) for v in send_branch]
    else:
        other_branch = [peer(v) for v in send_branch]
    hidden_out, pooled, stats = call(
        finish_kernel,
        "finish",
        meta,
        vm(residual, part_branch, *other_branch, sums),
        [((size, width), BF16, "v"), ((1, width), F32, "v"), ((1, width), F32, "v")],
        deps=(last,),
    )
    last = stats
    if fast:
        at_keep, at_two = halve_next(at_keep, at_one, last, extra=128)
        in_four = quarters(*in_four, at_keep)
        mine_in, other_in = shards(in_four, at_keep)
        got_in = peer(other_in)
        own_at, small_grads = call(
            last_kernel,
            "last",
            meta,
            vm(at_keep, at_two),
            [((shard // 2, 4 * half), BF16, "v"), ((16, 128), F32, "v")],
            deps=(mine_in,),
        )
        at_four = own_at, swap(own_at, "dp", nz, 1), swap(own_at, "dp", nz, 2)
        small_grads = small_grads + peer(small_grads)
        (grad_in,) = call(
            functools.partial(weave_in_kernel, block),
            "weave_in",
            meta,
            vm(mine_in, got_in),
            [((shard, full_ff), F32, "v")],
            deps=(own_at,),
        )
        at_four = quarters(*at_four, grad_in)
        mine_at, other_at = shards(at_four, small_grads)
        got_at = peer(other_at)
        grad_at = call(
            weave_at_kernel, "weave_at", meta, vm(mine_at, got_at), [((shard, width), F32, "v")] * 4
        )
    else:

        def reduced(v):
            v = lax.psum_scatter(v, "fsdp", scatter_dimension=0, tiled=True)
            return lax.psum(v, "dp").astype(F32)

        def spread(v, axis):
            none = jnp.zeros_like(v)
            return by_core(jnp.stack([v, none], axis), jnp.stack([none, v], axis))

        grad_ffout = reduced(
            spread(ff_parts[0].reshape(nf // 2, block, width), 1).reshape(full_ff, width)
        )
        grad_in = reduced(
            spread(in_parts[0].reshape(width, nf // 2, block), 2).reshape(width, full_ff)
        )
        grads = spread(at_parts[0][:width].reshape(width, 4, half), 2).reshape(width, 4 * width)
        grads = reduced(grads)
        grad_at = [grads[:, n * width : (n + 1) * width] for n in range(4)]
        small_grads = lax.psum(small_grads, ("fsdp", "dp"))

    count = width // 128
    rows = levels // nf
    table = small_grads[2 * count :].reshape(-1)[: heads * levels].reshape(heads, levels)
    grad_table = lax.dynamic_slice_in_dim(table, me * rows, rows, 1).T
    gains = small_grads[: 2 * count].reshape(2, width)
    gains = lax.dynamic_slice_in_dim(gains, me * shard, shard, 1)
    return (
        hidden_out,
        pooled,
        grad_hidden,
        gains[0],
        grad_at[0],
        grad_at[1],
        grad_at[2],
        grad_at[3],
        grad_table,
        gains[1],
        grad_in,
        grad_ffout,
        stats[:, :3],
    )


def solution(mesh):
    token = P(("fsdp", "dp"), None)
    weight = P("fsdp", None)
    return jax.shard_map(
        functools.partial(body, mesh.shape["fsdp"], mesh.shape["dp"]),
        mesh=mesh,
        in_specs=(
            token,
            P("fsdp"),
            weight,
            weight,
            weight,
            weight,
            weight,
            P("fsdp"),
            weight,
            weight,
            P(),
            P(("fsdp", "dp")),
            P(("fsdp", "dp")),
            token,
            token,
        ),
        out_specs=(
            token,
            token,
            token,
            P("fsdp"),
            weight,
            weight,
            weight,
            weight,
            weight,
            P("fsdp"),
            weight,
            weight,
            token,
        ),
        check_vma=False,
    )
```
